32 devices in a mesh: groups: 2 (over y), tm: 4 (over z), zoom: 2 (over x), pol: 2 (over core).
Axes of the slice: x: 2, y: 2, z: 4, core: 2. Of those that a mesh axis runs over, the one named last changes fastest.
Arguments:
- voltages: bfloat16 [2, 4, 7464960], P('pol', 'groups', ('tm', 'zoom')), parts along dimension 1, may hold values from -6 to 6
- section1_taps: float32 [12, 512], replicated, may hold values from -0.078125 to 0.078125
- section2_taps: float32 [5, 3456], replicated, may hold values from -0.046875 to 0.046875
- band_starts: int32 [4], P('groups'), parts along dimension 0, may hold values from 0 to 511
- band_widths: int32 [4], P('groups'), parts along dimension 0, may hold values from 1 to 20, 24 in all
Outputs:
- fine: float32 [2, 2, 4, 1, 58320], P('pol', 'zoom', 'groups', None, 'tm'), parts along dimension 2
The draws below stay inside these ranges and needn't reach their ends.
There are 2 independent parts, one for each index of `groups`. The reference program is written for one: setup_inputs(seed, part) draws one part's arguments, and reference() takes and returns one part's arrays. A program takes and returns all parts, laid end to end along the dimension named above; an argument that names none is the same for every part. Nothing has to cross between parts.
Inputs may be any that keep to these rules, and one draw needn't show every extreme that they name: `band_widths`: the 2 widths sum to 24, and one band has exactly 20 coarse channels.
All inputs are finite; a program needn't handle non-finite values.
Results may differ from the reference program's by a relative error of at most 0.0069.
Values may be sent and summed in bfloat16 or wider, within the bound.
No kernel may reach another device: no remote copies, remote signals or barrier semaphores. Data moves between devices by JAX's collectives and lax.ppermute only.
A program may use at most 192 MiB of HBM per device.

```python
import math
import jax
import jax.numpy as jnp
import numpy as np
from jax import lax

CHAN = 512
HOP = 432
TAPS1 = 12
TAPS2 = 5
FA = 27
FB = 128
FINE = 3456
KEEP = 2916
EDGE = 128
FSPEC = 1
NB = 2
WMAX = 20
LIVE_TOTAL = 24
SPEC_ALL = 17280
SAMPLES = 7464960
POLS = 2


def levels(own_key, extent, shards, smallest, largest):
    factor_of, own = 1.0, jax.random.fold_in(own_key, 6)
    for dim, shards_of in shards:
        heights = jnp.exp(jax.random.uniform(jax.random.fold_in(own, dim), (shards_of,), jnp.float32, smallest / len(shards), largest / len(shards)))
        factor_of = factor_of * jnp.repeat(heights, extent[dim] // shards_of).reshape([-1 if axis == dim else 1 for axis in range(len(extent))])
    return factor_of


def split_up(count, total, bound, skew):
    loads = [(1 << 20) // math.isqrt(standing ** skew) + 1 for standing in range(2, count + 1)]
    surplus, counts = total - bound - (count - 1), [1] * (count - 1)
    while surplus > 0:
        free = [i for i in range(count - 1) if counts[i] < bound]
        whole, remaining = sum([loads[i] for i in free]), surplus
        for i in free:
            more = min(bound - counts[i], max(1, remaining * loads[i] // whole), surplus)
            counts[i] = counts[i] + more
            surplus = surplus - more
    return np.array([bound] + counts)


def uneven(key, amount, total, bound, lean):
    if amount == 2:
        one = jax.random.randint(key, (), max(1, total - bound), min(bound, total - 1) + 1)
        return jnp.stack([one, total - one])
    lengths = jnp.asarray(split_up(amount, total, bound, lean), jnp.int32)
    couples = (amount - 1) // 2
    donor, taker = lengths[1:1 + 2 * couples:2], lengths[2:2 + 2 * couples:2]
    slack = jnp.minimum(donor - 1, bound - taker)
    moved = jax.random.randint(jax.random.fold_in(key, 1), (couples,), 0, 1 << 20) % (slack + 1)
    lengths = lengths.at[1:1 + 2 * couples:2].set(donor - moved).at[2:2 + 2 * couples:2].set(taker + moved)
    return lengths[jax.random.permutation(jax.random.fold_in(key, 2), amount)]


def scatter_about(stream_key, extent, width, bound, cuts=(), held_as=jnp.bfloat16):
    array = width * jax.random.normal(stream_key, extent, jnp.float32)
    if cuts:
        array = array * levels(stream_key, extent, cuts, -0.22, 0.18)
    return jnp.clip(array, -bound, bound).astype(held_as)


def setup_inputs(seed: int = 0, part: int = 0) -> dict:
    key_list = jax.random.split(jax.random.key(seed), 6)
    part_splits = jax.random.split(jax.random.fold_in(key_list[5], part), 6)
    return {
        "voltages": scatter_about(part_splits[0], (POLS, 2, SAMPLES), 1.0, 6.0, ((0, 2), (2, 8))),
        "section1_taps": scatter_about(key_list[1], (TAPS1, CHAN), (TAPS1 * CHAN) ** -0.5, 0.078125, (), jnp.float32),
        "section2_taps": scatter_about(key_list[2], (TAPS2, FINE), (TAPS2 * FINE) ** -0.5, 0.046875, (), jnp.float32),
        "band_starts": jax.random.randint(part_splits[3], (NB,), 0, CHAN).astype(jnp.int32),
        "band_widths": uneven(part_splits[4], NB, LIVE_TOTAL, WMAX, 2).astype(jnp.int32),
    }


def angle_table(rows, cols, length):
    product = (jnp.arange(rows, dtype=jnp.int32)[:, None] * jnp.arange(cols, dtype=jnp.int32)[None, :]) % length
    return product.astype(jnp.float32) * (2.0 * math.pi / length)


def rotation_block(length):
    angles = angle_table(length, length, length)
    cosine_tab = jnp.cos(angles).astype(jnp.bfloat16)
    sine_tab = jnp.sin(angles).astype(jnp.bfloat16)
    return jnp.stack([jnp.stack([cosine_tab, sine_tab]), jnp.stack([-sine_tab, cosine_tab])])


def joined_table(length):
    angles = angle_table(length, length, length)
    cosine_tab = jnp.cos(angles).astype(jnp.bfloat16)
    sine_tab = jnp.sin(angles).astype(jnp.bfloat16)
    top_rows = jnp.concatenate([cosine_tab, -sine_tab], axis=1)
    bottom_rows = jnp.concatenate([sine_tab, cosine_tab], axis=1)
    return jnp.concatenate([top_rows, bottom_rows], axis=0)


def bin_index(radix_a, radix_b, keep_len, edge_len):
    fine_len = radix_a * radix_b
    offsets = (np.arange(keep_len + 2 * edge_len) - keep_len // 2 - edge_len) % fine_len
    base = (offsets % radix_a) * (2 * radix_b) + offsets // radix_a
    return base, base + radix_b


def frame_view(segment, spectra, chan_len, hop_len):
    pieces = -(-chan_len // hop_len)
    framed = segment[:, :(spectra + pieces - 1) * hop_len].reshape(segment.shape[0], spectra + pieces - 1, hop_len)
    joined = jnp.concatenate([framed[:, offset:offset + spectra] for offset in range(pieces)], axis=2)
    return joined[:, :, :chan_len]


def weighted_frames(signal, taps, spectra, hop_len):
    chan_len = taps.shape[1]
    running = jnp.zeros((2, spectra, chan_len), jnp.float32)
    for tap_index in range(taps.shape[0]):
        frames = frame_view(signal[:, tap_index * chan_len:], spectra, chan_len, hop_len)
        running = running + taps[tap_index][None, None, :] * frames.astype(jnp.float32)
    return running.astype(jnp.bfloat16)


def fine_spectra(series, section2_taps, radix_a, radix_b, keep_len, edge_len):
    tap_count, fine_len = section2_taps.shape
    items = series.shape[1]
    row_count = series.shape[2] // fine_len
    spectra = row_count - tap_count + 1
    row_blocks = series.reshape(2, items, row_count, fine_len)
    running = jnp.zeros((2, items, spectra, fine_len), jnp.float32)
    for tap_index in range(tap_count):
        running = running + section2_taps[tap_index] * row_blocks[:, :, tap_index:tap_index + spectra].astype(jnp.float32)
    weighted = running.astype(jnp.bfloat16).reshape(2, items, spectra, radix_a, radix_b)
    partial_value = jnp.einsum("pqkm,qcfmb->pcfkb", rotation_block(radix_a).astype(jnp.float32), weighted.astype(jnp.float32), precision=lax.Precision.HIGHEST)
    angles = angle_table(radix_a, radix_b, fine_len)
    cosine_tab = jnp.cos(angles)
    sine_tab = jnp.sin(angles)
    real_part = partial_value[0] * cosine_tab + partial_value[1] * sine_tab
    imag_part = partial_value[1] * cosine_tab - partial_value[0] * sine_tab
    twiddled = jnp.concatenate([real_part, imag_part], axis=-1).astype(jnp.bfloat16)
    spectrum = jnp.einsum("cfkm,mj->cfkj", twiddled.astype(jnp.float32), joined_table(radix_b).astype(jnp.float32), precision=lax.Precision.HIGHEST)
    flattened = spectrum.reshape(items, spectra, radix_a * 2 * radix_b)
    real_index, imag_index = bin_index(radix_a, radix_b, keep_len, edge_len)
    return jnp.stack([jnp.take(flattened, real_index, axis=2), jnp.take(flattened, imag_index, axis=2)])


def stitch_bands(extended, upper_rim, lower_rim, slot_ids, band_width, keep_len, edge_len):
    centre = extended[..., edge_len:edge_len + keep_len]
    live = (slot_ids < band_width).astype(jnp.float32)[None, :, None, None]
    upper_ok = (slot_ids + 1 < band_width).astype(jnp.float32)[None, :, None, None]
    lower_ok = ((slot_ids >= 1) & (slot_ids < band_width)).astype(jnp.float32)[None, :, None, None]
    ramp = (jnp.arange(edge_len, dtype=jnp.float32) + 0.5) / (2.0 * edge_len)
    upper_weight = ramp * upper_ok
    lower_weight = ramp[::-1] * lower_ok
    low_part = centre[..., :edge_len] * (1.0 - lower_weight) + lower_rim * lower_weight
    high_part = centre[..., keep_len - edge_len:] * (1.0 - upper_weight) + upper_rim * upper_weight
    joined = jnp.concatenate([low_part, centre[..., edge_len:keep_len - edge_len], high_part], axis=-1)
    return joined * live


def reference(voltages, section1_taps, section2_taps, band_starts, band_widths):
    chan_len = section1_taps.shape[1]
    pieces = -(-chan_len // HOP)
    rotation = rotation_block(chan_len).astype(jnp.float32)
    slot_ids = jnp.arange(WMAX, dtype=jnp.int32)
    results = []
    for pol_index in range(POLS):
        signal = jnp.pad(voltages[pol_index], ((0, 0), (0, TAPS1 * chan_len + pieces * HOP)))
        weighted = weighted_frames(signal, section1_taps, SPEC_ALL, HOP)
        coarse = jnp.einsum("pqkn,qsn->pks", rotation, weighted.astype(jnp.float32), precision=lax.Precision.HIGHEST).astype(jnp.bfloat16)

        def one_band(pair):
            start, band_width = pair
            channels = ((start + slot_ids) % chan_len).astype(jnp.int32)
            series = jnp.take(coarse, channels, axis=1)
            extended = fine_spectra(series, section2_taps, FA, FB, KEEP, EDGE)
            zero_rim = jnp.zeros_like(extended[:, :1, :, :EDGE])
            upper_rim = jnp.concatenate([extended[:, 1:, :, :EDGE], zero_rim], axis=1)
            lower_rim = jnp.concatenate([zero_rim, extended[:, :-1, :, KEEP + EDGE:]], axis=1)
            stitched = stitch_bands(extended, upper_rim, lower_rim, slot_ids, band_width, KEEP, EDGE)
            return jnp.transpose(stitched, (0, 2, 1, 3)).reshape(2, FSPEC, WMAX * KEEP)

        results.append(lax.map(one_band, (band_starts, band_widths)))
    return jnp.stack(results)
```

```python
import functools
import math

import jax
import jax.numpy as jnp
import numpy as np
from jax import lax
from jax.experimental import pallas as pl
from jax.experimental.pallas import tpu as pltpu
from jax.sharding import PartitionSpec as P

HOP = 432
FA = 27
FB = 128
KEEP = 2916
EDGE = 128
CH_DEV = 5
LIVE_DEV = 3


def shifted(value, axis, steps):
    count = lax.axis_size(axis)
    initial, last = (max(0, -steps), min(count, count - steps))
    return lax.ppermute(value, axis, [(source, source + steps) for source in range(initial, last)])


def with_halo(value, sides, width):
    for axis, dim in sides:
        count, length = (lax.axis_size(axis), value.shape[dim])
        up = [(i, (i + 1) % count) for i in range(count - 1)]
        down = [(j, i) for i, j in up]
        last = lax.slice_in_dim(value, length - width, length, axis=dim)
        initial = lax.slice_in_dim(value, 0, width, axis=dim)
        before = lax.ppermute(last, axis, up)
        after = lax.ppermute(initial, axis, down)
        value = jnp.concatenate([before, value, after], axis=dim)
    return value


def angle_table(rows, cols, length):
    product = (
        jnp.arange(rows, dtype=jnp.int32)[:, None]
        * jnp.arange(cols, dtype=jnp.int32)[None, :]
        % length
    )
    return product.astype(jnp.float32) * (2.0 * math.pi / length)


def rotation_block(length):
    angles = angle_table(length, length, length)
    cosine_tab = jnp.cos(angles).astype(jnp.bfloat16)
    sine_tab = jnp.sin(angles).astype(jnp.bfloat16)
    return jnp.stack([jnp.stack([cosine_tab, sine_tab]), jnp.stack([-sine_tab, cosine_tab])])


def joined_table(length):
    angles = angle_table(length, length, length)
    cosine_tab = jnp.cos(angles).astype(jnp.bfloat16)
    sine_tab = jnp.sin(angles).astype(jnp.bfloat16)
    top_rows = jnp.concatenate([cosine_tab, -sine_tab], axis=1)
    bottom_rows = jnp.concatenate([sine_tab, cosine_tab], axis=1)
    return jnp.concatenate([top_rows, bottom_rows], axis=0)


def bin_index(radix_a, radix_b, keep_len, edge_len):
    fine_len = radix_a * radix_b
    offsets = (np.arange(keep_len + 2 * edge_len) - keep_len // 2 - edge_len) % fine_len
    base = offsets % radix_a * (2 * radix_b) + offsets // radix_a
    return (base, base + radix_b)


def frame_view(segment, spectra, chan_len, hop_len):
    pieces = -(-chan_len // hop_len)
    framed = segment[:, : (spectra + pieces - 1) * hop_len].reshape(
        segment.shape[0], spectra + pieces - 1, hop_len
    )
    joined = jnp.concatenate(
        [framed[:, offset : offset + spectra] for offset in range(pieces)], axis=2
    )
    return joined[:, :, :chan_len]


def weighted_frames(signal, taps, spectra, hop_len):
    chan_len = taps.shape[1]
    running = jnp.zeros((2, spectra, chan_len), jnp.float32)
    for tap_index in range(taps.shape[0]):
        frames = frame_view(signal[:, tap_index * chan_len :], spectra, chan_len, hop_len)
        running = running + taps[tap_index][None, None, :] * frames.astype(jnp.float32)
    return running.astype(jnp.bfloat16)


def fine_spectra(series, section2_taps, radix_a, radix_b, keep_len, edge_len):
    tap_count, fine_len = section2_taps.shape
    items = series.shape[1]
    row_count = series.shape[2] // fine_len
    spectra = row_count - tap_count + 1
    row_blocks = series.reshape(2, items, row_count, fine_len)
    running = jnp.zeros((2, items, spectra, fine_len), jnp.float32)
    for tap_index in range(tap_count):
        running = running + section2_taps[tap_index] * row_blocks[
            :, :, tap_index : tap_index + spectra
        ].astype(jnp.float32)
    weighted = running.astype(jnp.bfloat16).reshape(2, items, spectra, radix_a, radix_b)
    partial_value = jnp.einsum(
        "pqkm,qcfmb->pcfkb", rotation_block(radix_a), weighted, preferred_element_type=jnp.float32
    )
    angles = angle_table(radix_a, radix_b, fine_len)
    cosine_tab = jnp.cos(angles)
    sine_tab = jnp.sin(angles)
    real_part = partial_value[0] * cosine_tab + partial_value[1] * sine_tab
    imag_part = partial_value[1] * cosine_tab - partial_value[0] * sine_tab
    twiddled = jnp.concatenate([real_part, imag_part], axis=-1).astype(jnp.bfloat16)
    spectrum = jnp.einsum(
        "cfkm,mj->cfkj", twiddled, joined_table(radix_b), preferred_element_type=jnp.float32
    )
    flattened = spectrum.reshape(items, spectra, radix_a * 2 * radix_b)
    real_index, imag_index = bin_index(radix_a, radix_b, keep_len, edge_len)
    return jnp.stack(
        [jnp.take(flattened, real_index, axis=2), jnp.take(flattened, imag_index, axis=2)]
    )


def stitch_bands(extended, upper_rim, lower_rim, slot_ids, band_width, keep_len, edge_len):
    centre = extended[..., edge_len : edge_len + keep_len]
    live = (slot_ids < band_width).astype(jnp.float32)[None, :, None, None]
    upper_ok = (slot_ids + 1 < band_width).astype(jnp.float32)[None, :, None, None]
    lower_ok = ((slot_ids >= 1) & (slot_ids < band_width)).astype(jnp.float32)[None, :, None, None]
    ramp = (jnp.arange(edge_len, dtype=jnp.float32) + 0.5) / (2.0 * edge_len)
    upper_weight = ramp * upper_ok
    lower_weight = ramp[::-1] * lower_ok
    low_part = centre[..., :edge_len] * (1.0 - lower_weight) + lower_rim * lower_weight
    high_part = centre[..., keep_len - edge_len :] * (1.0 - upper_weight) + upper_rim * upper_weight
    joined = jnp.concatenate(
        [low_part, centre[..., edge_len : keep_len - edge_len], high_part], axis=-1
    )
    return joined * live


def general_plan(voltages, section1_taps, section2_taps, band_starts, band_widths):
    signal = voltages[0]
    tap_count, chan_len = section1_taps.shape
    spectra = signal.shape[1] // HOP
    rim_len = tap_count * chan_len - HOP
    pieces = -(-chan_len // HOP)
    following = shifted(signal[:, :rim_len], ("tm", "zoom"), -1)
    padded = jnp.concatenate(
        [signal, following, jnp.zeros((2, pieces * HOP), jnp.bfloat16)], axis=1
    )
    weighted = weighted_frames(padded, section1_taps, spectra, HOP)
    coarse = jnp.einsum(
        "pqkn,qsn->pks", rotation_block(chan_len), weighted, preferred_element_type=jnp.float32
    ).astype(jnp.bfloat16)
    tm_count = lax.axis_size("tm")
    zoom_count = lax.axis_size("zoom")
    slot_local = jnp.arange(CH_DEV, dtype=jnp.int32)
    slot_ids = lax.axis_index("tm") * CH_DEV + slot_local
    band_count = band_widths.shape[0]
    band_ids = jnp.arange(band_count, dtype=jnp.int32)
    my_band = band_ids == lax.axis_index("zoom")
    band_width = jnp.sum(jnp.where(my_band, band_widths, 0))
    device_count = tm_count * zoom_count
    live_count = LIVE_DEV * device_count
    band_ends = jnp.cumsum(band_widths)
    band_firsts = band_ends - band_widths
    live_ids = jnp.arange(live_count, dtype=jnp.int32)
    band_of = jnp.sum((band_ends[None, :] <= live_ids[:, None]).astype(jnp.int32), axis=1)
    member = band_of[:, None] == band_ids[None, :]
    first_of = jnp.sum(jnp.where(member, band_firsts[None, :], 0), axis=1)
    start_of = jnp.sum(jnp.where(member, band_starts[None, :], 0), axis=1)
    live_channels = (start_of + live_ids - first_of) % chan_len
    packed_order = live_channels.reshape(device_count, LIVE_DEV).T.reshape(-1)
    packed = jnp.take(coarse, packed_order, axis=1).reshape(2, LIVE_DEV, device_count, spectra)
    received = lax.all_to_all(packed, ("tm", "zoom"), split_axis=2, concat_axis=2, tiled=True)
    series = received.reshape(2, received.shape[1], -1)
    computed = fine_spectra(series, section2_taps, FA, FB, KEEP, EDGE)
    wanted = jnp.sum(jnp.where(my_band, band_firsts, 0)) + slot_ids
    valid = slot_ids < band_width
    piece = lax.all_gather(computed, ("tm", "zoom"), axis=1, tiled=True)
    piece_ids = jnp.arange(piece.shape[1], dtype=jnp.int32)
    chosen = ((wanted[:, None] == piece_ids[None, :]) & valid[:, None]).astype(jnp.float32)
    extended = jnp.einsum("kn,pnfx->pkfx", chosen, piece, precision=lax.Precision.HIGHEST)
    seam_rows = jnp.concatenate([extended[..., :EDGE], extended[..., KEEP + EDGE :]], axis=-1)
    widened = with_halo(seam_rows, (("tm", 1),), 1)
    upper_rim = widened[:, 2:, :, :EDGE]
    lower_rim = widened[:, :CH_DEV, :, EDGE:]
    stitched = stitch_bands(extended, upper_rim, lower_rim, slot_ids, band_width, KEEP, EDGE)
    fine_count = stitched.shape[2]
    result = jnp.transpose(stitched, (0, 2, 1, 3)).reshape(2, fine_count, CH_DEV * KEEP)
    return result[None, None]


ROWS = 8
LANES = 128
SLOT_LANES = 2 * ROWS
NT = (((1,), (1,)), ((), ()))


def sine_quarter(value):
    square = value * value
    total = -3.5988432e-06
    for factor in (1.604411848e-04, -4.6817541353e-03, 7.96926262462e-02, -6.459640975062e-01):
        total = total * square + factor
    return (total * square + 1.5707963267949) * value


def section_one_kernel(plan, starts_ref, widths_ref, taps_ref, signal_ref, *rest):
    (outs, (table, taps_rows, frames, total, sems)) = (rest[: plan.devices], rest[plan.devices :])
    blocks, chan_len, live = (plan.blocks, plan.chan_len, plan.live)
    half = ROWS * live
    columns = 2 * half
    lead = plan.lead
    copies = [
        pltpu.make_async_copy(
            signal_ref.at[:, block], frames.at[block, pl.ds(lead, plan.local_rows)], sems.at[block]
        )
        for block in range(blocks)
    ]
    for copy in copies:
        copy.start()
    edge = jnp.zeros((blocks, lead, 2, LANES), jnp.bfloat16)
    frames[:, :lead] = edge
    frames[:, lead + plan.local_rows :] = edge

    row = lax.broadcasted_iota(jnp.int32, (columns, 1), 0)
    imag = (row >= half).astype(jnp.int32)
    shift = (row - imag * half) // live
    ident = row - imag * half - shift * live
    channel = jnp.zeros((columns, 1), jnp.int32)
    first = jnp.int32(0)
    firsts = []
    for band in range(plan.bands):
        inside = (ident >= first) & (ident < first + widths_ref[band])
        channel = jnp.where(inside, starts_ref[band] + ident - first, channel)
        firsts.append(first)
        first = first + widths_ref[band]
    phase = lax.broadcasted_iota(jnp.int32, (columns, chan_len), 1) - HOP * shift
    turn = (channel * phase + imag * (chan_len // 4)) & (chan_len - 1)
    quarter = chan_len // 4
    folded = jnp.abs(turn - 2 * quarter)
    angle = (folded - quarter).astype(jnp.float32) * (1.0 / quarter)
    rotation = sine_quarter(angle).astype(jnp.bfloat16).astype(jnp.float32)

    flat = jnp.concatenate(
        [jnp.broadcast_to(taps_ref[tap : tap + 1, :], (8, chan_len)) for tap in range(plan.taps)]
        + [jnp.zeros((8, plan.depth - plan.taps * chan_len), jnp.float32)],
        axis=1,
    )
    for shift_index in range(ROWS):
        taps_rows[shift_index] = (
            pltpu.roll(flat, HOP * shift_index, axis=1) if shift_index else flat
        )
    for piece in range(plan.depth // chan_len):
        span = pl.ds(piece * chan_len, chan_len)
        scale = jnp.concatenate(
            [
                jnp.broadcast_to(
                    taps_rows[shift_index, :, span][None], (live // 8, 8, chan_len)
                ).reshape(live, chan_len)
                for shift_index in range(ROWS)
            ],
            axis=0,
        )
        for part in range(2):
            table[pl.ds(part * half, half), span] = (
                scale * rotation[part * half : (part + 1) * half]
            ).astype(jnp.bfloat16)

    for copy in copies:
        copy.wait()
    count = 2 * plan.out_rows
    pairs = frames.reshape(blocks, 2 * (plan.local_rows + 2 * lead), LANES)
    acc = jnp.zeros((count, columns), jnp.float32)
    for index in range(0, plan.depth // LANES, 2):
        left = jnp.concatenate(
            [
                pairs[(index + step) % blocks, pl.ds(2 * ((index + step) // blocks), count), :]
                for step in range(2)
            ],
            axis=1,
        )
        right = table[:, index * LANES : (index + 2) * LANES]
        acc = acc + lax.dot_general(left, right, NT, preferred_element_type=jnp.float32)
    for tile in range(columns // LANES):
        total[tile] = acc[:, tile * LANES : (tile + 1) * LANES]
    (real_rows, imag_rows) = (
        jnp.concatenate(
            [total[tile, pl.ds(part, plan.out_rows, 2), :] for tile in range(columns // LANES)],
            axis=1,
        )
        for part in range(2)
    )
    lane = lax.broadcasted_iota(jnp.int32, (1, columns), 1)
    sign = jnp.where(lane < half, -1.0, 1.0)
    coarse = (real_rows + sign * pltpu.roll(imag_rows, half, axis=1)).astype(jnp.bfloat16)

    here = lax.axis_index("tm") * plan.zooms + lax.axis_index("zoom")
    code = ident * SLOT_LANES + imag * ROWS + shift
    out_lane = lax.broadcasted_iota(jnp.int32, (1, LANES), 1)
    slot = out_lane // SLOT_LANES
    for step in range(plan.devices):
        target = jnp.bitwise_xor(here, step)
        (target_tm, target_zoom) = (target // plan.zooms, target % plan.zooms)
        (band_first, width) = (jnp.int32(0), jnp.int32(0))
        for band in range(plan.bands):
            band_first = jnp.where(target_zoom == band, firsts[band], band_first)
            width = jnp.where(target_zoom == band, widths_ref[band], width)
        base = target_tm * CH_DEV - 1
        position = base + slot
        valid = (position >= 0) & (position < width) & (slot < CH_DEV + 2)
        wanted = jnp.where(valid, (band_first + base) * SLOT_LANES + out_lane, -1)
        pick = (code == wanted).astype(jnp.float32).astype(jnp.bfloat16)
        outs[step][...] = lax.dot_general(
            coarse, pick, (((1,), (0,)), ((), ())), preferred_element_type=jnp.float32
        ).astype(jnp.bfloat16)


def section_two_kernel(plan, widths_ref, taps_ref, dft_ref, cos_ref, sin_ref, join_ref, *rest):
    (blocks, out_ref, series) = (rest[: plan.devices], rest[plan.devices], rest[plan.devices + 1])
    here = lax.axis_index("tm") * plan.zooms + lax.axis_index("zoom")
    fine_rows = plan.fine_rows
    pad = 8
    series[...] = jnp.zeros_like(series)
    for step in range(plan.devices):
        source = jnp.bitwise_xor(here, step)
        span = pl.ds(source * plan.local_rows + (pad - plan.lead), plan.out_rows)
        series[span, :] += blocks[step][...].astype(jnp.float32)
    fine_in = jnp.zeros((fine_rows, LANES), jnp.float32)
    for tap in range(plan.fine_taps):
        fine_in = fine_in + taps_ref[tap] * series[pl.ds(pad + tap * fine_rows, fine_rows), :]
    spun = lax.dot_general(
        dft_ref[...],
        fine_in.astype(jnp.bfloat16),
        (((1,), (0,)), ((), ())),
        preferred_element_type=jnp.float32,
    )
    (even, odd) = (spun[:fine_rows], spun[fine_rows:])
    (cosine_tab, sine_tab) = (cos_ref[...], sin_ref[...])
    mixed = jnp.concatenate(
        [
            (part * factor).astype(jnp.bfloat16)
            for part in (even, odd)
            for factor in (cosine_tab, sine_tab)
        ],
        axis=1,
    )
    out_ref[...] = lax.dot_general(
        join_ref[...], mixed, NT, preferred_element_type=jnp.float32
    )


def fine_tables(fine_rows):
    fine_len = fine_rows * ROWS
    offset = KEEP // 2 + EDGE
    bins = np.arange(fine_rows) - offset
    spin = 2.0 * np.pi * (np.outer(bins, np.arange(fine_rows)) % fine_rows) / fine_rows
    dft = np.concatenate([np.cos(spin), np.sin(spin)], axis=0)
    twist = 2.0 * np.pi * (np.outer(bins, np.arange(LANES) % ROWS) % fine_len) / fine_len
    join = np.zeros((ROWS, 2, LANES // SLOT_LANES, 4, LANES // SLOT_LANES, 2, ROWS))
    turn = 2.0 * np.pi * (np.outer(np.arange(ROWS), np.arange(ROWS)) % ROWS) / ROWS
    (cosine, sine) = (np.cos(turn), np.sin(turn))
    for slot in range(LANES // SLOT_LANES):
        real, imag = (join[:, 0, slot, :, slot], join[:, 1, slot, :, slot])
        real[:, 0, 0], real[:, 0, 1] = (cosine, sine)
        real[:, 1, 0], real[:, 1, 1] = (-sine, cosine)
        real[:, 2, 0], real[:, 2, 1] = (-sine, cosine)
        real[:, 3, 0], real[:, 3, 1] = (-cosine, -sine)
        imag[:, 0, 0], imag[:, 0, 1] = (-sine, cosine)
        imag[:, 1, 0], imag[:, 1, 1] = (-cosine, -sine)
        imag[:, 2, 0], imag[:, 2, 1] = (-cosine, -sine)
        imag[:, 3, 0], imag[:, 3, 1] = (sine, -cosine)
    return (
        jnp.asarray(dft, jnp.bfloat16),
        jnp.asarray(np.cos(twist), jnp.float32),
        jnp.asarray(np.sin(twist), jnp.float32),
        jnp.asarray(join.reshape(LANES, 4 * LANES), jnp.bfloat16),
    )


class Plan:
    def __init__(self, mesh, samples, bands, section1_shape, section2_shape):
        (self.tms, self.zooms) = (mesh.shape["tm"], mesh.shape["zoom"])
        self.devices = self.tms * self.zooms
        self.bands = bands
        (self.taps, self.chan_len) = section1_shape
        self.fine_taps = section2_shape[0]
        self.live = LIVE_DEV * self.devices
        self.samples = samples
        self.row_len = ROWS * HOP
        self.blocks = self.row_len // LANES
        self.local_rows = samples // self.row_len
        reach = (ROWS - 1) * HOP + self.taps * self.chan_len
        unit = max(self.chan_len, 2 * LANES)
        self.depth = -(-reach // unit) * unit
        self.lead = -(-self.depth // self.row_len) - 1
        self.out_rows = self.local_rows + self.lead
        self.fine_rows = section2_shape[1] // ROWS

    def fits(self, section2_shape):
        return (
            self.row_len % LANES == 0
            and self.samples % self.row_len == 0
            and self.chan_len & (self.chan_len - 1) == 0
            and self.chan_len % LANES == 0
            and self.devices & (self.devices - 1) == 0
            and self.live % 8 == 0
            and (2 * ROWS * self.live) % LANES == 0
            and 2 * ROWS * self.live <= 4 * LANES
            and (CH_DEV + 2) * SLOT_LANES <= LANES
            and self.out_rows % 16 == 0
            and self.fine_rows % 16 == 0
            and section2_shape[1] % ROWS == 0
            and self.devices * self.samples == HOP * self.fine_taps * section2_shape[1]
        )


def direct_plan(plan, voltages, section1_taps, section2_taps, band_starts, band_widths):
    signal = voltages[0].reshape(2, plan.local_rows, plan.blocks, LANES).transpose(1, 2, 0, 3)
    smem = pl.BlockSpec(memory_space=pltpu.SMEM)
    vmem = pl.BlockSpec(memory_space=pltpu.VMEM)
    columns = 2 * ROWS * plan.live
    block = jax.ShapeDtypeStruct((plan.out_rows, LANES), jnp.bfloat16)
    sent = pl.pallas_call(
        functools.partial(section_one_kernel, plan),
        out_shape=[block] * plan.devices,
        in_specs=[smem, smem, vmem, pl.BlockSpec(memory_space=pl.ANY)],
        out_specs=[vmem] * plan.devices,
        scratch_shapes=[
            pltpu.VMEM((columns, plan.depth), jnp.bfloat16),
            pltpu.VMEM((ROWS, 8, plan.depth), jnp.float32),
            pltpu.VMEM((plan.blocks, plan.local_rows + 2 * plan.lead, 2, LANES), jnp.bfloat16),
            pltpu.VMEM((columns // LANES, 2 * plan.out_rows, LANES), jnp.float32),
            pltpu.SemaphoreType.DMA((plan.blocks,)),
        ],
        compiler_params=pltpu.CompilerParams(vmem_limit_bytes=40 * 2**20),
        name="section_one",
    )(band_starts, band_widths, section1_taps, signal)
    received = [sent[0]]
    for step in range(1, plan.devices):
        pairs = [(index, index ^ step) for index in range(plan.devices)]
        received.append(lax.ppermute(sent[step], ("tm", "zoom"), pairs))
    fine_rows = plan.fine_rows
    spread = jnp.tile(
        section2_taps.reshape(plan.fine_taps, fine_rows, ROWS), (1, 1, LANES // ROWS)
    )
    (dft, cosine_tab, sine_tab, join) = fine_tables(fine_rows)
    bins = pl.pallas_call(
        functools.partial(section_two_kernel, plan),
        out_shape=jax.ShapeDtypeStruct((LANES, fine_rows), jnp.float32),
        in_specs=[smem] + [vmem] * (5 + plan.devices),
        out_specs=vmem,
        scratch_shapes=[
            pltpu.VMEM((plan.fine_taps * fine_rows + 16 + plan.lead, LANES), jnp.float32)
        ],
        compiler_params=pltpu.CompilerParams(vmem_limit_bytes=24 * 2**20),
        name="section_two",
    )(band_widths, spread, dft, cosine_tab, sine_tab, join, *received)
    slots = LANES // SLOT_LANES
    whole = bins.reshape(ROWS, 2, slots, fine_rows).transpose(1, 2, 0, 3)
    whole = whole.reshape(2, slots, 1, ROWS * fine_rows)
    zoom = lax.axis_index("zoom")
    band_width = jnp.sum(jnp.where(jnp.arange(plan.bands) == zoom, band_widths, 0))
    slot_ids = lax.axis_index("tm") * CH_DEV + jnp.arange(CH_DEV, dtype=jnp.int32)
    stitched = stitch_bands(
        whole[:, 1 : CH_DEV + 1],
        whole[:, 2 : CH_DEV + 2, :, :EDGE],
        whole[:, :CH_DEV, :, KEEP + EDGE : KEEP + 2 * EDGE],
        slot_ids,
        band_width,
        KEEP,
        EDGE,
    )
    return stitched.reshape(1, 1, 2, 1, CH_DEV * KEEP)


def solution(mesh):
    placed = (P("pol", "groups", ("tm", "zoom")), P(), P(), P("groups"), P("groups"))

    def on_device(voltages, section1_taps, section2_taps, band_starts, band_widths):
        plan = Plan(
            mesh,
            voltages.shape[2],
            band_widths.shape[0],
            section1_taps.shape,
            section2_taps.shape,
        )
        arrays = (voltages, section1_taps, section2_taps, band_starts, band_widths)
        if plan.fits(section2_taps.shape):
            return direct_plan(plan, *arrays)
        return general_plan(*arrays)

    return jax.shard_map(
        on_device,
        mesh=mesh,
        in_specs=placed,
        out_specs=P("pol", "zoom", "groups", None, "tm"),
        check_vma=False,
    )
```

```python
import functools
import math

import jax
import jax.numpy as jnp
import numpy as np
from jax import lax
from jax.experimental import pallas as pl
from jax.experimental.pallas import tpu as pltpu
from jax.sharding import PartitionSpec as P

HOP = 432
FA = 27
FB = 128
KEEP = 2916
EDGE = 128
CH_DEV = 5
LIVE_DEV = 3


def shifted(value, axis, steps):
    count = lax.axis_size(axis)
    initial, last = (max(0, -steps), min(count, count - steps))
    return lax.ppermute(value, axis, [(source, source + steps) for source in range(initial, last)])


def with_halo(value, sides, width):
    for axis, dim in sides:
        count, length = (lax.axis_size(axis), value.shape[dim])
        up = [(i, (i + 1) % count) for i in range(count - 1)]
        down = [(j, i) for i, j in up]
        last = lax.slice_in_dim(value, length - width, length, axis=dim)
        initial = lax.slice_in_dim(value, 0, width, axis=dim)
        before = lax.ppermute(last, axis, up)
        after = lax.ppermute(initial, axis, down)
        value = jnp.concatenate([before, value, after], axis=dim)
    return value


def angle_table(rows, cols, length):
    product = (
        jnp.arange(rows, dtype=jnp.int32)[:, None]
        * jnp.arange(cols, dtype=jnp.int32)[None, :]
        % length
    )
    return product.astype(jnp.float32) * (2.0 * math.pi / length)


def rotation_block(length):
    angles = angle_table(length, length, length)
    cosine_tab = jnp.cos(angles).astype(jnp.bfloat16)
    sine_tab = jnp.sin(angles).astype(jnp.bfloat16)
    return jnp.stack([jnp.stack([cosine_tab, sine_tab]), jnp.stack([-sine_tab, cosine_tab])])


def joined_table(length):
    angles = angle_table(length, length, length)
    cosine_tab = jnp.cos(angles).astype(jnp.bfloat16)
    sine_tab = jnp.sin(angles).astype(jnp.bfloat16)
    top_rows = jnp.concatenate([cosine_tab, -sine_tab], axis=1)
    bottom_rows = jnp.concatenate([sine_tab, cosine_tab], axis=1)
    return jnp.concatenate([top_rows, bottom_rows], axis=0)


def bin_index(radix_a, radix_b, keep_len, edge_len):
    fine_len = radix_a * radix_b
    offsets = (np.arange(keep_len + 2 * edge_len) - keep_len // 2 - edge_len) % fine_len
    base = offsets % radix_a * (2 * radix_b) + offsets // radix_a
    return (base, base + radix_b)


def frame_view(segment, spectra, chan_len, hop_len):
    pieces = -(-chan_len // hop_len)
    framed = segment[:, : (spectra + pieces - 1) * hop_len].reshape(
        segment.shape[0], spectra + pieces - 1, hop_len
    )
    joined = jnp.concatenate(
        [framed[:, offset : offset + spectra] for offset in range(pieces)], axis=2
    )
    return joined[:, :, :chan_len]


def weighted_frames(signal, taps, spectra, hop_len):
    chan_len = taps.shape[1]
    running = jnp.zeros((2, spectra, chan_len), jnp.float32)
    for tap_index in range(taps.shape[0]):
        frames = frame_view(signal[:, tap_index * chan_len :], spectra, chan_len, hop_len)
        running = running + taps[tap_index][None, None, :] * frames.astype(jnp.float32)
    return running.astype(jnp.bfloat16)


def fine_spectra(series, section2_taps, radix_a, radix_b, keep_len, edge_len):
    tap_count, fine_len = section2_taps.shape
    items = series.shape[1]
    row_count = series.shape[2] // fine_len
    spectra = row_count - tap_count + 1
    row_blocks = series.reshape(2, items, row_count, fine_len)
    running = jnp.zeros((2, items, spectra, fine_len), jnp.float32)
    for tap_index in range(tap_count):
        running = running + section2_taps[tap_index] * row_blocks[
            :, :, tap_index : tap_index + spectra
        ].astype(jnp.float32)
    weighted = running.astype(jnp.bfloat16).reshape(2, items, spectra, radix_a, radix_b)
    partial_value = jnp.einsum(
        "pqkm,qcfmb->pcfkb", rotation_block(radix_a), weighted, preferred_element_type=jnp.float32
    )
    angles = angle_table(radix_a, radix_b, fine_len)
    cosine_tab = jnp.cos(angles)
    sine_tab = jnp.sin(angles)
    real_part = partial_value[0] * cosine_tab + partial_value[1] * sine_tab
    imag_part = partial_value[1] * cosine_tab - partial_value[0] * sine_tab
    twiddled = jnp.concatenate([real_part, imag_part], axis=-1).astype(jnp.bfloat16)
    spectrum = jnp.einsum(
        "cfkm,mj->cfkj", twiddled, joined_table(radix_b), preferred_element_type=jnp.float32
    )
    flattened = spectrum.reshape(items, spectra, radix_a * 2 * radix_b)
    real_index, imag_index = bin_index(radix_a, radix_b, keep_len, edge_len)
    return jnp.stack(
        [jnp.take(flattened, real_index, axis=2), jnp.take(flattened, imag_index, axis=2)]
    )


def stitch_bands(extended, upper_rim, lower_rim, slot_ids, band_width, keep_len, edge_len):
    centre = extended[..., edge_len : edge_len + keep_len]
    live = (slot_ids < band_width).astype(jnp.float32)[None, :, None, None]
    upper_ok = (slot_ids + 1 < band_width).astype(jnp.float32)[None, :, None, None]
    lower_ok = ((slot_ids >= 1) & (slot_ids < band_width)).astype(jnp.float32)[None, :, None, None]
    ramp = (jnp.arange(edge_len, dtype=jnp.float32) + 0.5) / (2.0 * edge_len)
    upper_weight = ramp * upper_ok
    lower_weight = ramp[::-1] * lower_ok
    low_part = centre[..., :edge_len] * (1.0 - lower_weight) + lower_rim * lower_weight
    high_part = centre[..., keep_len - edge_len :] * (1.0 - upper_weight) + upper_rim * upper_weight
    joined = jnp.concatenate(
        [low_part, centre[..., edge_len : keep_len - edge_len], high_part], axis=-1
    )
    return joined * live


def general_plan(voltages, section1_taps, section2_taps, band_starts, band_widths):
    signal = voltages[0]
    tap_count, chan_len = section1_taps.shape
    spectra = signal.shape[1] // HOP
    rim_len = tap_count * chan_len - HOP
    pieces = -(-chan_len // HOP)
    following = shifted(signal[:, :rim_len], ("tm", "zoom"), -1)
    padded = jnp.concatenate(
        [signal, following, jnp.zeros((2, pieces * HOP), jnp.bfloat16)], axis=1
    )
    weighted = weighted_frames(padded, section1_taps, spectra, HOP)
    coarse = jnp.einsum(
        "pqkn,qsn->pks", rotation_block(chan_len), weighted, preferred_element_type=jnp.float32
    ).astype(jnp.bfloat16)
    tm_count = lax.axis_size("tm")
    zoom_count = lax.axis_size("zoom")
    slot_local = jnp.arange(CH_DEV, dtype=jnp.int32)
    slot_ids = lax.axis_index("tm") * CH_DEV + slot_local
    band_count = band_widths.shape[0]
    band_ids = jnp.arange(band_count, dtype=jnp.int32)
    my_band = band_ids == lax.axis_index("zoom")
    band_width = jnp.sum(jnp.where(my_band, band_widths, 0))
    device_count = tm_count * zoom_count
    live_count = LIVE_DEV * device_count
    band_ends = jnp.cumsum(band_widths)
    band_firsts = band_ends - band_widths
    live_ids = jnp.arange(live_count, dtype=jnp.int32)
    band_of = jnp.sum((band_ends[None, :] <= live_ids[:, None]).astype(jnp.int32), axis=1)
    member = band_of[:, None] == band_ids[None, :]
    first_of = jnp.sum(jnp.where(member, band_firsts[None, :], 0), axis=1)
    start_of = jnp.sum(jnp.where(member, band_starts[None, :], 0), axis=1)
    live_channels = (start_of + live_ids - first_of) % chan_len
    packed_order = live_channels.reshape(device_count, LIVE_DEV).T.reshape(-1)
    packed = jnp.take(coarse, packed_order, axis=1).reshape(2, LIVE_DEV, device_count, spectra)
    received = lax.all_to_all(packed, ("tm", "zoom"), split_axis=2, concat_axis=2, tiled=True)
    series = received.reshape(2, received.shape[1], -1)
    computed = fine_spectra(series, section2_taps, FA, FB, KEEP, EDGE)
    wanted = jnp.sum(jnp.where(my_band, band_firsts, 0)) + slot_ids
    valid = slot_ids < band_width
    piece = lax.all_gather(computed, ("tm", "zoom"), axis=1, tiled=True)
    piece_ids = jnp.arange(piece.shape[1], dtype=jnp.int32)
    chosen = ((wanted[:, None] == piece_ids[None, :]) & valid[:, None]).astype(jnp.float32)
    extended = jnp.einsum("kn,pnfx->pkfx", chosen, piece, precision=lax.Precision.HIGHEST)
    seam_rows = jnp.concatenate([extended[..., :EDGE], extended[..., KEEP + EDGE :]], axis=-1)
    widened = with_halo(seam_rows, (("tm", 1),), 1)
    upper_rim = widened[:, 2:, :, :EDGE]
    lower_rim = widened[:, :CH_DEV, :, EDGE:]
    stitched = stitch_bands(extended, upper_rim, lower_rim, slot_ids, band_width, KEEP, EDGE)
    fine_count = stitched.shape[2]
    result = jnp.transpose(stitched, (0, 2, 1, 3)).reshape(2, fine_count, CH_DEV * KEEP)
    return result[None, None]


ROWS = 8
LANES = 128
SLOT_LANES = 2 * ROWS
NT = (((1,), (1,)), ((), ()))


def sine_quarter(value):
    square = value * value
    total = -3.5988432e-06
    for factor in (1.604411848e-04, -4.6817541353e-03, 7.96926262462e-02, -6.459640975062e-01):
        total = total * square + factor
    return (total * square + 1.5707963267949) * value


def section_one_kernel(plan, starts_ref, widths_ref, taps_ref, signal_ref, *rest):
    (outs, (taps_rows, frames, total, sems)) = (rest[: plan.devices], rest[plan.devices :])
    blocks, chan_len, live = (plan.blocks, plan.chan_len, plan.live)
    half = ROWS * live
    columns = 2 * half
    lead = plan.lead
    copies = [
        pltpu.make_async_copy(
            signal_ref.at[:, block], frames.at[block, pl.ds(lead, plan.local_rows)], sems.at[block]
        )
        for block in range(blocks)
    ]
    for copy in copies:
        copy.start()
    edge = jnp.zeros((blocks, lead, 2, LANES), jnp.bfloat16)
    frames[:, :lead] = edge
    frames[:, lead + plan.local_rows :] = edge

    row = lax.broadcasted_iota(jnp.int32, (columns, 1), 0)
    imag = (row >= half).astype(jnp.int32)
    shift = (row - imag * half) // live
    ident = row - imag * half - shift * live
    channel = jnp.zeros((columns, 1), jnp.int32)
    first = jnp.int32(0)
    firsts = []
    for band in range(plan.bands):
        inside = (ident >= first) & (ident < first + widths_ref[band])
        channel = jnp.where(inside, starts_ref[band] + ident - first, channel)
        firsts.append(first)
        first = first + widths_ref[band]
    phase = lax.broadcasted_iota(jnp.int32, (columns, chan_len), 1) - HOP * shift
    turn = (channel * phase + imag * (chan_len // 4)) & (chan_len - 1)
    quarter = chan_len // 4
    folded = jnp.abs(turn - 2 * quarter)
    angle = (folded - quarter).astype(jnp.float32) * (1.0 / quarter)
    rotation = sine_quarter(angle).astype(jnp.bfloat16).astype(jnp.float32)

    flat = jnp.concatenate(
        [jnp.broadcast_to(taps_ref[tap : tap + 1, :], (8, chan_len)) for tap in range(plan.taps)]
        + [jnp.zeros((8, plan.depth - plan.taps * chan_len), jnp.float32)],
        axis=1,
    )
    for shift_index in range(ROWS):
        taps_rows[shift_index] = (
            pltpu.roll(flat, HOP * shift_index, axis=1) if shift_index else flat
        )
    count = 2 * plan.out_rows
    pairs = frames.reshape(blocks, 2 * (plan.local_rows + 2 * lead), LANES)
    acc = jnp.zeros((count, columns), jnp.float32)
    order = sorted(range(plan.depth // LANES), key=lambda index: (index % blocks, index // blocks))
    turns = chan_len // LANES
    batch = -(-blocks // 3)
    arrived = 0
    for piece in range(0, len(order), turns):
        group = order[piece : piece + turns]
        needed = max(index % blocks for index in group) // batch * batch + batch
        while arrived < min(blocks, needed):
            copies[arrived].wait()
            arrived += 1
        right = jnp.concatenate(
            [
                (
                    jnp.concatenate(
                        [
                            jnp.broadcast_to(
                                taps_rows[shift_index, :, pl.ds(index * LANES, LANES)][None],
                                (live // 8, 8, LANES),
                            ).reshape(live, LANES)
                            for shift_index in range(ROWS)
                        ]
                        * 2,
                        axis=0,
                    )
                    * rotation[:, index % turns * LANES : (index % turns + 1) * LANES]
                ).astype(jnp.bfloat16)
                for index in group
            ],
            axis=1,
        )
        left = jnp.concatenate(
            [pairs[index % blocks, pl.ds(2 * (index // blocks), count), :] for index in group],
            axis=1,
        )
        acc = acc + lax.dot_general(left, right, NT, preferred_element_type=jnp.float32)
    for tile in range(columns // LANES):
        total[tile] = acc[:, tile * LANES : (tile + 1) * LANES]
    (real_rows, imag_rows) = (
        jnp.concatenate(
            [total[tile, pl.ds(part, plan.out_rows, 2), :] for tile in range(columns // LANES)],
            axis=1,
        )
        for part in range(2)
    )
    lane = lax.broadcasted_iota(jnp.int32, (1, columns), 1)
    sign = jnp.where(lane < half, -1.0, 1.0)
    coarse = (real_rows + sign * pltpu.roll(imag_rows, half, axis=1)).astype(jnp.bfloat16)

    here = lax.axis_index("tm") * plan.zooms + lax.axis_index("zoom")
    code = ident * SLOT_LANES + imag * ROWS + shift
    out_lane = lax.broadcasted_iota(jnp.int32, (1, LANES), 1)
    slot = out_lane // SLOT_LANES
    for step in range(plan.devices):
        target = jnp.bitwise_xor(here, step)
        (target_tm, target_zoom) = (target // plan.zooms, target % plan.zooms)
        (band_first, width) = (jnp.int32(0), jnp.int32(0))
        for band in range(plan.bands):
            band_first = jnp.where(target_zoom == band, firsts[band], band_first)
            width = jnp.where(target_zoom == band, widths_ref[band], width)
        base = target_tm * CH_DEV - 1
        position = base + slot
        valid = (position >= 0) & (position < width) & (slot < CH_DEV + 2)
        wanted = jnp.where(valid, (band_first + base) * SLOT_LANES + out_lane, -1)
        pick = (code == wanted).astype(jnp.float32).astype(jnp.bfloat16)
        outs[step][...] = lax.dot_general(
            coarse, pick, (((1,), (0,)), ((), ())), preferred_element_type=jnp.float32
        ).astype(jnp.bfloat16)


def fine_taps_kernel(plan, taps_ref, after_ref, out_ref):
    lane = lax.broadcasted_iota(jnp.int32, (SLOT_LANES, LANES), 1)
    row = lax.broadcasted_iota(jnp.int32, (SLOT_LANES, LANES), 0)
    keep = lane // ROWS == row
    source = lax.broadcasted_iota(jnp.int32, (2 * LANES, LANES), 0)
    target = lax.broadcasted_iota(jnp.int32, (2 * LANES, LANES), 1)
    spread = (source % ROWS == target % ROWS).astype(jnp.float32).astype(jnp.bfloat16)
    for tap in range(plan.fine_taps):
        (high, low) = ([], [])
        for tile in range(plan.fine_rows // SLOT_LANES):
            line = taps_ref[tap : tap + 1, tile * LANES : (tile + 1) * LANES]
            part = jnp.where(keep, jnp.broadcast_to(line, (SLOT_LANES, LANES)), 0.0)
            rounded = part.astype(jnp.bfloat16)
            high.append(rounded)
            low.append((part - rounded.astype(jnp.float32)).astype(jnp.bfloat16))
        both = jnp.concatenate([jnp.concatenate(high, axis=0), jnp.concatenate(low, axis=0)], axis=1)
        out_ref[tap] = lax.dot_general(
            both, spread, (((1,), (0,)), ((), ())), preferred_element_type=jnp.float32
        )


def section_two_kernel(plan, widths_ref, taps_ref, dft_ref, cos_ref, sin_ref, join_ref, *rest):
    (blocks, out_ref, series) = (rest[: plan.devices], rest[plan.devices], rest[plan.devices + 1])
    (tm, zoom) = (lax.axis_index("tm"), lax.axis_index("zoom"))
    here = tm * plan.zooms + zoom
    (fine_rows, bins) = (plan.fine_rows, plan.bins)
    pad = 8
    series[...] = jnp.zeros_like(series)
    for step in range(plan.devices):
        source = jnp.bitwise_xor(here, step)
        span = pl.ds(source * plan.local_rows + (pad - plan.lead), plan.out_rows)
        series[span, :] += blocks[step][...].astype(jnp.float32)
    fine_in = jnp.zeros((fine_rows, LANES), jnp.float32)
    for tap in range(plan.fine_taps):
        fine_in = fine_in + taps_ref[tap] * series[pl.ds(pad + tap * fine_rows, fine_rows), :]
    spun = lax.dot_general(
        dft_ref[...],
        fine_in.astype(jnp.bfloat16),
        (((1,), (0,)), ((), ())),
        preferred_element_type=jnp.float32,
    )
    (cosine_tab, sine_tab) = (cos_ref[...], sin_ref[...])
    mixed = jnp.concatenate(
        [
            (part * factor).astype(jnp.bfloat16)
            for part in (spun[:bins], spun[bins:])
            for factor in (cosine_tab, sine_tab)
        ],
        axis=1,
    )
    joined = lax.dot_general(join_ref[...], mixed, NT, preferred_element_type=jnp.float32)

    slots = LANES // SLOT_LANES
    high = 2 * slots
    flat = [jnp.zeros((high, LANES), jnp.float32)] * (-(-(ROWS * fine_rows) // LANES) + 2)
    for turn in range(ROWS):
        (first, offset) = divmod(turn * fine_rows, LANES)
        piece = jnp.concatenate(
            [joined[turn * high : (turn + 1) * high], jnp.zeros((high, LANES), jnp.float32)], axis=1
        )
        if offset:
            piece = pltpu.roll(piece, offset, axis=1)
        for tile in range(min(bins // LANES + 1, len(flat) - first)):
            flat[first + tile] = flat[first + tile] + piece[:, tile * LANES : (tile + 1) * LANES]

    row = lax.broadcasted_iota(jnp.int32, (high, LANES), 0)
    lane = lax.broadcasted_iota(jnp.int32, (high, LANES), 1)
    width = jnp.int32(0)
    for band in range(plan.bands):
        width = jnp.where(zoom == band, widths_ref[band], width)
    slot = tm * CH_DEV + row % slots - 1
    live = (slot < width).astype(jnp.float32)
    upper_ok = (slot + 1 < width).astype(jnp.float32)
    lower_ok = ((slot >= 1) & (slot < width)).astype(jnp.float32)
    (lead, skew) = divmod(KEEP + EDGE, LANES)
    below = jnp.where(
        lane < LANES - skew,
        pltpu.roll(flat[lead], LANES - skew, axis=1),
        pltpu.roll(flat[lead + 1], LANES - skew, axis=1),
    )
    below = pltpu.roll(below, 1, axis=0)
    (lead, skew) = divmod(KEEP - EDGE, LANES)
    above = pltpu.roll(pltpu.roll(flat[0], skew, axis=1), high - 1, axis=0)
    position = lane.astype(jnp.float32)
    own = flat[1:]
    span = -(-KEEP // LANES)
    parts = []
    for tile in range(span):
        value = own[tile]
        if tile == 0:
            weight = (EDGE - 0.5 - position) * (0.5 / EDGE) * lower_ok
            value = value * (1.0 - weight) + below * weight
        if tile in (lead, lead + 1):
            ramp = (position + (tile * LANES - (KEEP - EDGE) + 0.5)) * (0.5 / EDGE)
            inside = lane >= skew if tile == lead else lane < skew
            weight = jnp.where(inside, ramp * upper_ok, 0.0)
            value = value * (1.0 - weight) + above * weight
        value = value * live
        if tile == span - 1:
            value = jnp.where(lane < KEEP - tile * LANES, value, 0.0)
        parts.append(value)
    parts = [jnp.zeros_like(parts[0])] + parts + [jnp.zeros_like(parts[0])]

    carry = [None, None]
    for place in range(CH_DEV):
        (first, offset) = divmod(place * KEEP, LANES)
        (after, _) = divmod((place + 1) * KEEP, LANES)
        last = place == CH_DEV - 1
        count = after - first + 1
        for part in range(2):
            picked = part * slots + place + 1
            tiles = []
            for tile in range(count):
                value = parts[tile + 1][part * slots : (part + 1) * slots]
                if offset:
                    before = parts[tile][part * slots : (part + 1) * slots]
                    value = jnp.where(
                        lane[:slots] < offset,
                        pltpu.roll(before, offset, axis=1),
                        pltpu.roll(value, offset, axis=1),
                    )
                tiles.append(value[picked % slots : picked % slots + 1])
            if place:
                tiles[0] = tiles[0] + carry[part]
            carry[part] = tiles[-1]
            if not last:
                tiles = tiles[:-1]
            line = jnp.concatenate(tiles, axis=1)
            end = min(first * LANES + len(tiles) * LANES, CH_DEV * KEEP)
            out_ref[part, :, first * LANES : end] = line[:, : end - first * LANES]


def fine_tables(fine_rows):
    fine_len = fine_rows * ROWS
    offset = KEEP // 2 + EDGE
    bins = np.arange(fine_rows) - offset
    spin = 2.0 * np.pi * (np.outer(bins, np.arange(fine_rows)) % fine_rows) / fine_rows
    margin = ((0, -fine_rows % LANES), (0, 0))
    dft = np.concatenate([np.pad(np.cos(spin), margin), np.pad(np.sin(spin), margin)], axis=0)
    twist = 2.0 * np.pi * (np.outer(bins, np.arange(LANES) % ROWS) % fine_len) / fine_len
    join = np.zeros((ROWS, 2, LANES // SLOT_LANES, 4, LANES // SLOT_LANES, 2, ROWS))
    turn = 2.0 * np.pi * (np.outer(np.arange(ROWS), np.arange(ROWS)) % ROWS) / ROWS
    (cosine, sine) = (np.cos(turn), np.sin(turn))
    for slot in range(LANES // SLOT_LANES):
        real, imag = (join[:, 0, slot, :, slot], join[:, 1, slot, :, slot])
        real[:, 0, 0], real[:, 0, 1] = (cosine, sine)
        real[:, 1, 0], real[:, 1, 1] = (-sine, cosine)
        real[:, 2, 0], real[:, 2, 1] = (-sine, cosine)
        real[:, 3, 0], real[:, 3, 1] = (-cosine, -sine)
        imag[:, 0, 0], imag[:, 0, 1] = (-sine, cosine)
        imag[:, 1, 0], imag[:, 1, 1] = (-cosine, -sine)
        imag[:, 2, 0], imag[:, 2, 1] = (-cosine, -sine)
        imag[:, 3, 0], imag[:, 3, 1] = (sine, -cosine)
    return (
        jnp.asarray(dft, jnp.bfloat16),
        jnp.asarray(np.pad(np.cos(twist), margin), jnp.float32),
        jnp.asarray(np.pad(np.sin(twist), margin), jnp.float32),
        jnp.asarray(join.reshape(LANES, 4 * LANES), jnp.bfloat16),
    )


class Plan:
    def __init__(self, mesh, samples, bands, section1_shape, section2_shape):
        (self.tms, self.zooms) = (mesh.shape["tm"], mesh.shape["zoom"])
        self.devices = self.tms * self.zooms
        self.bands = bands
        (self.taps, self.chan_len) = section1_shape
        self.fine_taps = section2_shape[0]
        self.live = LIVE_DEV * self.devices
        self.samples = samples
        self.row_len = ROWS * HOP
        self.blocks = self.row_len // LANES
        self.local_rows = samples // self.row_len
        reach = (ROWS - 1) * HOP + self.taps * self.chan_len
        unit = max(self.chan_len, 2 * LANES)
        self.depth = -(-reach // unit) * unit
        self.lead = -(-self.depth // self.row_len) - 1
        self.out_rows = self.local_rows + self.lead
        self.fine_rows = section2_shape[1] // ROWS
        self.bins = -(-self.fine_rows // LANES) * LANES

    def fits(self, section2_shape):
        return (
            self.row_len % LANES == 0
            and self.samples % self.row_len == 0
            and self.chan_len & (self.chan_len - 1) == 0
            and self.chan_len % LANES == 0
            and self.devices & (self.devices - 1) == 0
            and self.live % 8 == 0
            and (2 * ROWS * self.live) % LANES == 0
            and 2 * ROWS * self.live <= 4 * LANES
            and (CH_DEV + 2) * SLOT_LANES <= LANES
            and self.out_rows % 16 == 0
            and self.fine_rows % 16 == 0
            and EDGE == LANES
            and KEEP + 2 * EDGE <= section2_shape[1]
            and section2_shape[1] % ROWS == 0
            and self.devices * self.samples == HOP * self.fine_taps * section2_shape[1]
        )


def direct_plan(plan, voltages, section1_taps, section2_taps, band_starts, band_widths):
    signal = voltages[0].reshape(2, plan.local_rows, plan.blocks, LANES).transpose(1, 2, 0, 3)
    smem = pl.BlockSpec(memory_space=pltpu.SMEM)
    vmem = pl.BlockSpec(memory_space=pltpu.VMEM)
    columns = 2 * ROWS * plan.live
    block = jax.ShapeDtypeStruct((plan.out_rows, LANES), jnp.bfloat16)
    sent = pl.pallas_call(
        functools.partial(section_one_kernel, plan),
        out_shape=[block] * plan.devices,
        in_specs=[smem, smem, vmem, pl.BlockSpec(memory_space=pl.ANY)],
        out_specs=[vmem] * plan.devices,
        scratch_shapes=[
            pltpu.VMEM((ROWS, 8, plan.depth), jnp.float32),
            pltpu.VMEM((plan.blocks, plan.local_rows + 2 * plan.lead, 2, LANES), jnp.bfloat16),
            pltpu.VMEM((columns // LANES, 2 * plan.out_rows, LANES), jnp.float32),
            pltpu.SemaphoreType.DMA((plan.blocks,)),
        ],
        compiler_params=pltpu.CompilerParams(vmem_limit_bytes=62 * 2**20),
        name="section_one",
    )(band_starts, band_widths, section1_taps, signal)
    received = [sent[0]]
    for step in range(1, plan.devices):
        pairs = [(index, index ^ step) for index in range(plan.devices)]
        received.append(lax.ppermute(sent[step], ("tm", "zoom"), pairs))
    fine_rows = plan.fine_rows
    spread = pl.pallas_call(
        functools.partial(fine_taps_kernel, plan),
        out_shape=jax.ShapeDtypeStruct((plan.fine_taps, fine_rows, LANES), jnp.float32),
        in_specs=[vmem, pl.BlockSpec(memory_space=pl.ANY)],
        out_specs=vmem,
        compiler_params=pltpu.CompilerParams(vmem_limit_bytes=16 * 2**20),
        name="fine_taps",
    )(section2_taps, received[3])
    (dft, cosine_tab, sine_tab, join) = fine_tables(fine_rows)
    lines = pl.pallas_call(
        functools.partial(section_two_kernel, plan),
        out_shape=jax.ShapeDtypeStruct((2, 1, CH_DEV * KEEP), jnp.float32),
        in_specs=[smem] + [vmem] * (5 + plan.devices),
        out_specs=vmem,
        scratch_shapes=[
            pltpu.VMEM((plan.fine_taps * fine_rows + 16 + plan.lead, LANES), jnp.float32)
        ],
        compiler_params=pltpu.CompilerParams(vmem_limit_bytes=24 * 2**20),
        name="section_two",
    )(band_widths, spread, dft, cosine_tab, sine_tab, join, *received)
    return lines.reshape(1, 1, 2, 1, CH_DEV * KEEP)


def solution(mesh):
    placed = (P("pol", "groups", ("tm", "zoom")), P(), P(), P("groups"), P("groups"))

    def on_device(voltages, section1_taps, section2_taps, band_starts, band_widths):
        plan = Plan(
            mesh,
            voltages.shape[2],
            band_widths.shape[0],
            section1_taps.shape,
            section2_taps.shape,
        )
        arrays = (voltages, section1_taps, section2_taps, band_starts, band_widths)
        if plan.fits(section2_taps.shape):
            return direct_plan(plan, *arrays)
        return general_plan(*arrays)

    return jax.shard_map(
        on_device,
        mesh=mesh,
        in_specs=placed,
        out_specs=P("pol", "zoom", "groups", None, "tm"),
        check_vma=False,
    )
```

```python
import functools
import math

import jax
import jax.numpy as jnp
import numpy as np
from jax import lax
from jax.experimental import pallas as pl
from jax.experimental.pallas import tpu as pltpu
from jax.sharding import PartitionSpec as P

HOP = 432
FA = 27
FB = 128
KEEP = 2916
EDGE = 128
CH_DEV = 5
LIVE_DEV = 3


def shifted(value, axis, steps):
    count = lax.axis_size(axis)
    initial, last = (max(0, -steps), min(count, count - steps))
    return lax.ppermute(value, axis, [(source, source + steps) for source in range(initial, last)])


def with_halo(value, sides, width):
    for axis, dim in sides:
        count, length = (lax.axis_size(axis), value.shape[dim])
        up = [(i, (i + 1) % count) for i in range(count - 1)]
        down = [(j, i) for i, j in up]
        last = lax.slice_in_dim(value, length - width, length, axis=dim)
        initial = lax.slice_in_dim(value, 0, width, axis=dim)
        before = lax.ppermute(last, axis, up)
        after = lax.ppermute(initial, axis, down)
        value = jnp.concatenate([before, value, after], axis=dim)
    return value


def angle_table(rows, cols, length):
    product = (
        jnp.arange(rows, dtype=jnp.int32)[:, None]
        * jnp.arange(cols, dtype=jnp.int32)[None, :]
        % length
    )
    return product.astype(jnp.float32) * (2.0 * math.pi / length)


def rotation_block(length):
    angles = angle_table(length, length, length)
    cosine_tab = jnp.cos(angles).astype(jnp.bfloat16)
    sine_tab = jnp.sin(angles).astype(jnp.bfloat16)
    return jnp.stack([jnp.stack([cosine_tab, sine_tab]), jnp.stack([-sine_tab, cosine_tab])])


def joined_table(length):
    angles = angle_table(length, length, length)
    cosine_tab = jnp.cos(angles).astype(jnp.bfloat16)
    sine_tab = jnp.sin(angles).astype(jnp.bfloat16)
    top_rows = jnp.concatenate([cosine_tab, -sine_tab], axis=1)
    bottom_rows = jnp.concatenate([sine_tab, cosine_tab], axis=1)
    return jnp.concatenate([top_rows, bottom_rows], axis=0)


def bin_index(radix_a, radix_b, keep_len, edge_len):
    fine_len = radix_a * radix_b
    offsets = (np.arange(keep_len + 2 * edge_len) - keep_len // 2 - edge_len) % fine_len
    base = offsets % radix_a * (2 * radix_b) + offsets // radix_a
    return (base, base + radix_b)


def frame_view(segment, spectra, chan_len, hop_len):
    pieces = -(-chan_len // hop_len)
    framed = segment[:, : (spectra + pieces - 1) * hop_len].reshape(
        segment.shape[0], spectra + pieces - 1, hop_len
    )
    joined = jnp.concatenate(
        [framed[:, offset : offset + spectra] for offset in range(pieces)], axis=2
    )
    return joined[:, :, :chan_len]


def weighted_frames(signal, taps, spectra, hop_len):
    chan_len = taps.shape[1]
    running = jnp.zeros((2, spectra, chan_len), jnp.float32)
    for tap_index in range(taps.shape[0]):
        frames = frame_view(signal[:, tap_index * chan_len :], spectra, chan_len, hop_len)
        running = running + taps[tap_index][None, None, :] * frames.astype(jnp.float32)
    return running.astype(jnp.bfloat16)


def fine_spectra(series, section2_taps, radix_a, radix_b, keep_len, edge_len):
    tap_count, fine_len = section2_taps.shape
    items = series.shape[1]
    row_count = series.shape[2] // fine_len
    spectra = row_count - tap_count + 1
    row_blocks = series.reshape(2, items, row_count, fine_len)
    running = jnp.zeros((2, items, spectra, fine_len), jnp.float32)
    for tap_index in range(tap_count):
        running = running + section2_taps[tap_index] * row_blocks[
            :, :, tap_index : tap_index + spectra
        ].astype(jnp.float32)
    weighted = running.astype(jnp.bfloat16).reshape(2, items, spectra, radix_a, radix_b)
    partial_value = jnp.einsum(
        "pqkm,qcfmb->pcfkb", rotation_block(radix_a), weighted, preferred_element_type=jnp.float32
    )
    angles = angle_table(radix_a, radix_b, fine_len)
    cosine_tab = jnp.cos(angles)
    sine_tab = jnp.sin(angles)
    real_part = partial_value[0] * cosine_tab + partial_value[1] * sine_tab
    imag_part = partial_value[1] * cosine_tab - partial_value[0] * sine_tab
    twiddled = jnp.concatenate([real_part, imag_part], axis=-1).astype(jnp.bfloat16)
    spectrum = jnp.einsum(
        "cfkm,mj->cfkj", twiddled, joined_table(radix_b), preferred_element_type=jnp.float32
    )
    flattened = spectrum.reshape(items, spectra, radix_a * 2 * radix_b)
    real_index, imag_index = bin_index(radix_a, radix_b, keep_len, edge_len)
    return jnp.stack(
        [jnp.take(flattened, real_index, axis=2), jnp.take(flattened, imag_index, axis=2)]
    )


def stitch_bands(extended, upper_rim, lower_rim, slot_ids, band_width, keep_len, edge_len):
    centre = extended[..., edge_len : edge_len + keep_len]
    live = (slot_ids < band_width).astype(jnp.float32)[None, :, None, None]
    upper_ok = (slot_ids + 1 < band_width).astype(jnp.float32)[None, :, None, None]
    lower_ok = ((slot_ids >= 1) & (slot_ids < band_width)).astype(jnp.float32)[None, :, None, None]
    ramp = (jnp.arange(edge_len, dtype=jnp.float32) + 0.5) / (2.0 * edge_len)
    upper_weight = ramp * upper_ok
    lower_weight = ramp[::-1] * lower_ok
    low_part = centre[..., :edge_len] * (1.0 - lower_weight) + lower_rim * lower_weight
    high_part = centre[..., keep_len - edge_len :] * (1.0 - upper_weight) + upper_rim * upper_weight
    joined = jnp.concatenate(
        [low_part, centre[..., edge_len : keep_len - edge_len], high_part], axis=-1
    )
    return joined * live


def general_plan(voltages, section1_taps, section2_taps, band_starts, band_widths):
    signal = voltages[0]
    tap_count, chan_len = section1_taps.shape
    spectra = signal.shape[1] // HOP
    rim_len = tap_count * chan_len - HOP
    pieces = -(-chan_len // HOP)
    following = shifted(signal[:, :rim_len], ("tm", "zoom"), -1)
    padded = jnp.concatenate(
        [signal, following, jnp.zeros((2, pieces * HOP), jnp.bfloat16)], axis=1
    )
    weighted = weighted_frames(padded, section1_taps, spectra, HOP)
    coarse = jnp.einsum(
        "pqkn,qsn->pks", rotation_block(chan_len), weighted, preferred_element_type=jnp.float32
    ).astype(jnp.bfloat16)
    tm_count = lax.axis_size("tm")
    zoom_count = lax.axis_size("zoom")
    slot_local = jnp.arange(CH_DEV, dtype=jnp.int32)
    slot_ids = lax.axis_index("tm") * CH_DEV + slot_local
    band_count = band_widths.shape[0]
    band_ids = jnp.arange(band_count, dtype=jnp.int32)
    my_band = band_ids == lax.axis_index("zoom")
    band_width = jnp.sum(jnp.where(my_band, band_widths, 0))
    device_count = tm_count * zoom_count
    live_count = LIVE_DEV * device_count
    band_ends = jnp.cumsum(band_widths)
    band_firsts = band_ends - band_widths
    live_ids = jnp.arange(live_count, dtype=jnp.int32)
    band_of = jnp.sum((band_ends[None, :] <= live_ids[:, None]).astype(jnp.int32), axis=1)
    member = band_of[:, None] == band_ids[None, :]
    first_of = jnp.sum(jnp.where(member, band_firsts[None, :], 0), axis=1)
    start_of = jnp.sum(jnp.where(member, band_starts[None, :], 0), axis=1)
    live_channels = (start_of + live_ids - first_of) % chan_len
    packed_order = live_channels.reshape(device_count, LIVE_DEV).T.reshape(-1)
    packed = jnp.take(coarse, packed_order, axis=1).reshape(2, LIVE_DEV, device_count, spectra)
    received = lax.all_to_all(packed, ("tm", "zoom"), split_axis=2, concat_axis=2, tiled=True)
    series = received.reshape(2, received.shape[1], -1)
    computed = fine_spectra(series, section2_taps, FA, FB, KEEP, EDGE)
    wanted = jnp.sum(jnp.where(my_band, band_firsts, 0)) + slot_ids
    valid = slot_ids < band_width
    piece = lax.all_gather(computed, ("tm", "zoom"), axis=1, tiled=True)
    piece_ids = jnp.arange(piece.shape[1], dtype=jnp.int32)
    chosen = ((wanted[:, None] == piece_ids[None, :]) & valid[:, None]).astype(jnp.float32)
    extended = jnp.einsum("kn,pnfx->pkfx", chosen, piece, precision=lax.Precision.HIGHEST)
    seam_rows = jnp.concatenate([extended[..., :EDGE], extended[..., KEEP + EDGE :]], axis=-1)
    widened = with_halo(seam_rows, (("tm", 1),), 1)
    upper_rim = widened[:, 2:, :, :EDGE]
    lower_rim = widened[:, :CH_DEV, :, EDGE:]
    stitched = stitch_bands(extended, upper_rim, lower_rim, slot_ids, band_width, KEEP, EDGE)
    fine_count = stitched.shape[2]
    result = jnp.transpose(stitched, (0, 2, 1, 3)).reshape(2, fine_count, CH_DEV * KEEP)
    return result[None, None]


ROWS = 8
LANES = 128
SLOT_LANES = 2 * ROWS
PAD = 8
NT = (((1,), (1,)), ((), ()))


def sine_quarter(value):
    square = value * value
    total = -3.5988432e-06
    for factor in (1.604411848e-04, -4.6817541353e-03, 7.96926262462e-02, -6.459640975062e-01):
        total = total * square + factor
    return (total * square + 1.5707963267949) * value


def section_one_kernel(plan, starts_hbm, widths_hbm, taps_hbm, signal_ref, *rest):
    (outs, (width_ref, taps_rows, frames, total, *rest)) = (
        rest[: plan.devices],
        rest[plan.devices :],
    )
    (starts_ref, widths_ref, taps_ref, small_sems, sems) = rest
    small = [
        pltpu.make_async_copy(source, target, small_sems.at[index])
        for index, (source, target) in enumerate(
            [(starts_hbm, starts_ref), (widths_hbm, widths_ref), (taps_hbm, taps_ref)]
        )
    ]
    for copy in small:
        copy.start()
    blocks, chan_len, live = (plan.blocks, plan.chan_len, plan.live)
    half = ROWS * live
    columns = 2 * half
    lead = plan.lead
    copies = [
        pltpu.make_async_copy(
            signal_ref.at[:, block], frames.at[block, pl.ds(lead, plan.local_rows)], sems.at[block]
        )
        for block in range(blocks)
    ]
    for copy in copies:
        copy.start(priority=1)
    edge = jnp.zeros((blocks, lead, 2, LANES), jnp.bfloat16)
    frames[:, :lead] = edge
    frames[:, lead + plan.local_rows :] = edge

    for copy in small:
        copy.wait()
    row = lax.broadcasted_iota(jnp.int32, (columns, 1), 0)
    imag = (row >= half).astype(jnp.int32)
    shift = (row - imag * half) // live
    ident = row - imag * half - shift * live
    channel = jnp.zeros((columns, 1), jnp.int32)
    first = jnp.int32(0)
    firsts = []
    for band in range(plan.bands):
        inside = (ident >= first) & (ident < first + widths_ref[band])
        channel = jnp.where(inside, starts_ref[band] + ident - first, channel)
        firsts.append(first)
        first = first + widths_ref[band]
    phase = lax.broadcasted_iota(jnp.int32, (columns, chan_len), 1) - HOP * shift
    turn = (channel * phase + imag * (chan_len // 4)) & (chan_len - 1)
    quarter = chan_len // 4
    folded = jnp.abs(turn - 2 * quarter)
    angle = (folded - quarter).astype(jnp.float32) * (1.0 / quarter)
    rotation = sine_quarter(angle).astype(jnp.bfloat16).astype(jnp.float32)

    flat = jnp.concatenate(
        [jnp.broadcast_to(taps_ref[tap : tap + 1, :], (8, chan_len)) for tap in range(plan.taps)]
        + [jnp.zeros((8, plan.depth - plan.taps * chan_len), jnp.float32)],
        axis=1,
    )
    for shift_index in range(ROWS):
        taps_rows[shift_index] = (
            pltpu.roll(flat, HOP * shift_index, axis=1) if shift_index else flat
        )
    count = 2 * plan.out_rows
    pairs = frames.reshape(blocks, 2 * (plan.local_rows + 2 * lead), LANES)
    acc = jnp.zeros((count, columns), jnp.float32)
    order = sorted(range(plan.depth // LANES), key=lambda index: (index % blocks, index // blocks))
    turns = chan_len // LANES
    batch = -(-blocks // 3)
    arrived = 0
    for piece in range(0, len(order), turns):
        group = order[piece : piece + turns]
        needed = max(index % blocks for index in group) // batch * batch + batch
        while arrived < min(blocks, needed):
            copies[arrived].wait()
            arrived += 1
        right = jnp.concatenate(
            [
                (
                    jnp.concatenate(
                        [
                            jnp.broadcast_to(
                                taps_rows[shift_index, :, pl.ds(index * LANES, LANES)][None],
                                (live // 8, 8, LANES),
                            ).reshape(live, LANES)
                            for shift_index in range(ROWS)
                        ]
                        * 2,
                        axis=0,
                    )
                    * rotation[:, index % turns * LANES : (index % turns + 1) * LANES]
                ).astype(jnp.bfloat16)
                for index in group
            ],
            axis=1,
        )
        left = jnp.concatenate(
            [pairs[index % blocks, pl.ds(2 * (index // blocks), count), :] for index in group],
            axis=1,
        )
        acc = acc + lax.dot_general(left, right, NT, preferred_element_type=jnp.float32)
    for tile in range(columns // LANES):
        total[tile] = acc[:, tile * LANES : (tile + 1) * LANES]
    (real_rows, imag_rows) = (
        jnp.concatenate(
            [total[tile, pl.ds(part, plan.out_rows, 2), :] for tile in range(columns // LANES)],
            axis=1,
        )
        for part in range(2)
    )
    lane = lax.broadcasted_iota(jnp.int32, (1, columns), 1)
    sign = jnp.where(lane < half, -1.0, 1.0)
    coarse = (real_rows + sign * pltpu.roll(imag_rows, half, axis=1)).astype(jnp.bfloat16)

    (tm, zoom) = (lax.axis_index("tm"), lax.axis_index("zoom"))
    mine = jnp.int32(0)
    for band in range(plan.bands):
        mine = jnp.where(zoom == band, widths_ref[band], mine)
    width_ref[...] = jnp.broadcast_to(mine, width_ref.shape)
    code = ident * SLOT_LANES + imag * ROWS + shift
    out_lane = lax.broadcasted_iota(jnp.int32, (1, LANES), 1)
    slot = out_lane // SLOT_LANES
    for step in range(plan.devices):
        target = jnp.bitwise_xor(tm * plan.zooms + zoom, step)
        (target_tm, target_zoom) = (target // plan.zooms, target % plan.zooms)
        (band_first, width) = (jnp.int32(0), jnp.int32(0))
        for band in range(plan.bands):
            band_first = jnp.where(target_zoom == band, firsts[band], band_first)
            width = jnp.where(target_zoom == band, widths_ref[band], width)
        base = target_tm * CH_DEV - 1
        position = base + slot
        valid = (position >= 0) & (position < width) & (slot < CH_DEV + 2)
        wanted = jnp.where(valid, (band_first + base) * SLOT_LANES + out_lane, -1)
        pick = (code == wanted).astype(jnp.float32).astype(jnp.bfloat16)
        outs[step][...] = lax.dot_general(
            coarse, pick, (((1,), (0,)), ((), ())), preferred_element_type=jnp.float32
        ).astype(jnp.bfloat16)


def fine_taps_kernel(plan, taps_ref, after_ref, out_ref):
    lane = lax.broadcasted_iota(jnp.int32, (SLOT_LANES, LANES), 1)
    row = lax.broadcasted_iota(jnp.int32, (SLOT_LANES, LANES), 0)
    keep = lane // ROWS == row
    source = lax.broadcasted_iota(jnp.int32, (2 * LANES, LANES), 0)
    target = lax.broadcasted_iota(jnp.int32, (2 * LANES, LANES), 1)
    spread = (source % ROWS == target % ROWS).astype(jnp.float32).astype(jnp.bfloat16)
    for tap in range(plan.fine_taps):
        (high, low) = ([], [])
        for tile in range(plan.fine_rows // SLOT_LANES):
            line = taps_ref[tap : tap + 1, tile * LANES : (tile + 1) * LANES]
            part = jnp.where(keep, jnp.broadcast_to(line, (SLOT_LANES, LANES)), 0.0)
            rounded = part.astype(jnp.bfloat16)
            high.append(rounded)
            low.append((part - rounded.astype(jnp.float32)).astype(jnp.bfloat16))
        both = jnp.concatenate([jnp.concatenate(high, axis=0), jnp.concatenate(low, axis=0)], axis=1)
        out_ref[pl.ds(PAD + tap * plan.fine_rows, plan.fine_rows), :] = lax.dot_general(
            both, spread, (((1,), (0,)), ((), ())), preferred_element_type=jnp.float32
        )
    out_ref[:PAD] = jnp.zeros((PAD, LANES), jnp.float32)


def add_blocks(plan, steps, taps_ref, blocks, sums):
    here = lax.axis_index("tm") * plan.zooms + lax.axis_index("zoom")
    (fine_rows, out_rows) = (plan.fine_rows, plan.out_rows)
    sums[...] = jnp.zeros_like(sums)
    for step, block in zip(steps, blocks):
        start = jnp.bitwise_xor(here, step) * plan.local_rows + (PAD - plan.lead)
        goal = pl.ds(lax.rem(start + (fine_rows - PAD), fine_rows), out_rows)
        scale = taps_ref[pl.ds(start, out_rows), :]
        sums[goal, :] += scale * block[...].astype(jnp.float32)
    return jnp.concatenate(
        [
            sums[:out_rows] + sums[fine_rows : fine_rows + out_rows],
            sums[out_rows:fine_rows],
        ],
        axis=0,
    )


def merge_kernel(plan, steps, taps_ref, *rest):
    (blocks, (kept_ref, sums)) = (rest[: len(steps)], rest[len(steps) :])
    kept_ref[...] = add_blocks(plan, steps, taps_ref, blocks, sums)


def section_two_kernel(
    plan, steps, width_ref, kept_ref, taps_ref, dft_ref, cos_ref, sin_ref, join_ref, *rest
):
    (blocks, (out_ref, sums)) = (rest[: len(steps)], rest[len(steps) :])
    tm = lax.axis_index("tm")
    (fine_rows, bins) = (plan.fine_rows, plan.bins)
    fine_in = kept_ref[...] + add_blocks(plan, steps, taps_ref, blocks, sums)
    spun = lax.dot_general(
        dft_ref[...],
        fine_in.astype(jnp.bfloat16),
        (((1,), (0,)), ((), ())),
        preferred_element_type=jnp.float32,
    )
    (cosine_tab, sine_tab) = (cos_ref[...], sin_ref[...])
    mixed = jnp.concatenate(
        [
            (part * factor).astype(jnp.bfloat16)
            for part in (spun[:bins], spun[bins:])
            for factor in (cosine_tab, sine_tab)
        ],
        axis=1,
    )
    joined = lax.dot_general(join_ref[...], mixed, NT, preferred_element_type=jnp.float32)

    slots = LANES // SLOT_LANES
    high = 2 * slots
    flat = [jnp.zeros((high, LANES), jnp.float32)] * (-(-(ROWS * fine_rows) // LANES) + 2)
    for turn in range(ROWS):
        (first, offset) = divmod(turn * fine_rows, LANES)
        piece = jnp.concatenate(
            [joined[turn * high : (turn + 1) * high], jnp.zeros((high, LANES), jnp.float32)], axis=1
        )
        if offset:
            piece = pltpu.roll(piece, offset, axis=1)
        for tile in range(min(bins // LANES + 1, len(flat) - first)):
            flat[first + tile] = flat[first + tile] + piece[:, tile * LANES : (tile + 1) * LANES]

    row = lax.broadcasted_iota(jnp.int32, (high, LANES), 0)
    lane = lax.broadcasted_iota(jnp.int32, (high, LANES), 1)
    width = width_ref[0:1, :]
    slot = tm * CH_DEV + row % slots - 1
    live = (slot < width).astype(jnp.float32)
    upper_ok = (slot + 1 < width).astype(jnp.float32)
    lower_ok = ((slot >= 1) & (slot < width)).astype(jnp.float32)
    (lead, skew) = divmod(KEEP + EDGE, LANES)
    below = jnp.where(
        lane < LANES - skew,
        pltpu.roll(flat[lead], LANES - skew, axis=1),
        pltpu.roll(flat[lead + 1], LANES - skew, axis=1),
    )
    below = pltpu.roll(below, 1, axis=0)
    (lead, skew) = divmod(KEEP - EDGE, LANES)
    above = pltpu.roll(pltpu.roll(flat[0], skew, axis=1), high - 1, axis=0)
    position = lane.astype(jnp.float32)
    own = flat[1:]
    span = -(-KEEP // LANES)
    parts = []
    for tile in range(span):
        value = own[tile]
        if tile == 0:
            weight = (EDGE - 0.5 - position) * (0.5 / EDGE) * lower_ok
            value = value * (1.0 - weight) + below * weight
        if tile in (lead, lead + 1):
            ramp = (position + (tile * LANES - (KEEP - EDGE) + 0.5)) * (0.5 / EDGE)
            inside = lane >= skew if tile == lead else lane < skew
            weight = jnp.where(inside, ramp * upper_ok, 0.0)
            value = value * (1.0 - weight) + above * weight
        value = value * live
        if tile == span - 1:
            value = jnp.where(lane < KEEP - tile * LANES, value, 0.0)
        parts.append(value)
    parts = [jnp.zeros_like(parts[0])] + parts + [jnp.zeros_like(parts[0])]

    carry = [None, None]
    for place in range(CH_DEV):
        (first, offset) = divmod(place * KEEP, LANES)
        (after, _) = divmod((place + 1) * KEEP, LANES)
        last = place == CH_DEV - 1
        count = after - first + 1
        for part in range(2):
            picked = part * slots + place + 1
            tiles = []
            for tile in range(count):
                value = parts[tile + 1][part * slots : (part + 1) * slots]
                if offset:
                    before = parts[tile][part * slots : (part + 1) * slots]
                    value = jnp.where(
                        lane[:slots] < offset,
                        pltpu.roll(before, offset, axis=1),
                        pltpu.roll(value, offset, axis=1),
                    )
                tiles.append(value[picked % slots : picked % slots + 1])
            if place:
                tiles[0] = tiles[0] + carry[part]
            carry[part] = tiles[-1]
            if not last:
                tiles = tiles[:-1]
            line = jnp.concatenate(tiles, axis=1)
            end = min(first * LANES + len(tiles) * LANES, CH_DEV * KEEP)
            out_ref[part, :, first * LANES : end] = line[:, : end - first * LANES]


def fine_tables(fine_rows):
    fine_len = fine_rows * ROWS
    offset = KEEP // 2 + EDGE
    bins = np.arange(fine_rows) - offset
    spin = 2.0 * np.pi * (np.outer(bins, np.arange(fine_rows)) % fine_rows) / fine_rows
    margin = ((0, -fine_rows % LANES), (0, 0))
    dft = np.concatenate([np.pad(np.cos(spin), margin), np.pad(np.sin(spin), margin)], axis=0)
    twist = 2.0 * np.pi * (np.outer(bins, np.arange(LANES) % ROWS) % fine_len) / fine_len
    join = np.zeros((ROWS, 2, LANES // SLOT_LANES, 4, LANES // SLOT_LANES, 2, ROWS))
    turn = 2.0 * np.pi * (np.outer(np.arange(ROWS), np.arange(ROWS)) % ROWS) / ROWS
    (cosine, sine) = (np.cos(turn), np.sin(turn))
    for slot in range(LANES // SLOT_LANES):
        real, imag = (join[:, 0, slot, :, slot], join[:, 1, slot, :, slot])
        real[:, 0, 0], real[:, 0, 1] = (cosine, sine)
        real[:, 1, 0], real[:, 1, 1] = (-sine, cosine)
        real[:, 2, 0], real[:, 2, 1] = (-sine, cosine)
        real[:, 3, 0], real[:, 3, 1] = (-cosine, -sine)
        imag[:, 0, 0], imag[:, 0, 1] = (-sine, cosine)
        imag[:, 1, 0], imag[:, 1, 1] = (-cosine, -sine)
        imag[:, 2, 0], imag[:, 2, 1] = (-cosine, -sine)
        imag[:, 3, 0], imag[:, 3, 1] = (sine, -cosine)
    return (
        jnp.asarray(dft, jnp.bfloat16),
        jnp.asarray(np.pad(np.cos(twist), margin), jnp.float32),
        jnp.asarray(np.pad(np.sin(twist), margin), jnp.float32),
        jnp.asarray(join.reshape(LANES, 4 * LANES), jnp.bfloat16),
    )


class Plan:
    def __init__(self, mesh, samples, bands, section1_shape, section2_shape):
        (self.tms, self.zooms) = (mesh.shape["tm"], mesh.shape["zoom"])
        self.devices = self.tms * self.zooms
        self.bands = bands
        (self.taps, self.chan_len) = section1_shape
        self.fine_taps = section2_shape[0]
        self.live = LIVE_DEV * self.devices
        self.samples = samples
        self.row_len = ROWS * HOP
        self.blocks = self.row_len // LANES
        self.local_rows = samples // self.row_len
        reach = (ROWS - 1) * HOP + self.taps * self.chan_len
        unit = max(self.chan_len, 2 * LANES)
        self.depth = -(-reach // unit) * unit
        self.lead = -(-self.depth // self.row_len) - 1
        self.out_rows = self.local_rows + self.lead
        self.fine_rows = section2_shape[1] // ROWS
        self.bins = -(-self.fine_rows // LANES) * LANES

    def fits(self, section2_shape):
        return (
            self.row_len % LANES == 0
            and self.samples % self.row_len == 0
            and self.chan_len & (self.chan_len - 1) == 0
            and self.chan_len % LANES == 0
            and self.devices & (self.devices - 1) == 0
            and self.live % 8 == 0
            and (2 * ROWS * self.live) % LANES == 0
            and 2 * ROWS * self.live <= 4 * LANES
            and (CH_DEV + 2) * SLOT_LANES <= LANES
            and self.devices >= 4
            and self.lead <= PAD
            and self.out_rows <= self.fine_rows
            and self.out_rows % 16 == 0
            and self.fine_rows % 16 == 0
            and EDGE == LANES
            and KEEP + 2 * EDGE <= section2_shape[1]
            and section2_shape[1] % ROWS == 0
            and self.devices * self.samples == HOP * self.fine_taps * section2_shape[1]
        )


def direct_plan(plan, voltages, section1_taps, section2_taps, band_starts, band_widths):
    signal = voltages[0].reshape(2, plan.local_rows, plan.blocks, LANES).transpose(1, 2, 0, 3)
    far = [
        pltpu.with_memory_space_constraint(array, pltpu.HBM)
        for array in (band_starts, band_widths, section1_taps, signal)
    ]
    vmem = pl.BlockSpec(memory_space=pltpu.VMEM)
    columns = 2 * ROWS * plan.live
    block = jax.ShapeDtypeStruct((plan.out_rows, LANES), jnp.bfloat16)
    (*sent, width) = pl.pallas_call(
        functools.partial(section_one_kernel, plan),
        out_shape=[block] * plan.devices + [jax.ShapeDtypeStruct((8, LANES), jnp.int32)],
        in_specs=[pl.BlockSpec(memory_space=pltpu.HBM)] * 4,
        out_specs=[vmem] * (plan.devices + 1),
        scratch_shapes=[
            pltpu.VMEM((ROWS, 8, plan.depth), jnp.float32),
            pltpu.VMEM((plan.blocks, plan.local_rows + 2 * plan.lead, 2, LANES), jnp.bfloat16),
            pltpu.VMEM((columns // LANES, 2 * plan.out_rows, LANES), jnp.float32),
            pltpu.SMEM((plan.bands,), jnp.int32),
            pltpu.SMEM((plan.bands,), jnp.int32),
            pltpu.VMEM((plan.taps, plan.chan_len), jnp.float32),
            pltpu.SemaphoreType.DMA((3,)),
            pltpu.SemaphoreType.DMA((plan.blocks,)),
        ],
        compiler_params=pltpu.CompilerParams(vmem_limit_bytes=40 * 2**20),
        name="section_one",
    )(*far)
    order = list(range(plan.devices - 1, 0, -1))
    received = {0: sent[0]}
    for step in order:
        pairs = [(index, index ^ step) for index in range(plan.devices)]
        received[step] = lax.ppermute(sent[step], ("tm", "zoom"), pairs)
    split = len(order) // 2 + 1
    (early, late) = ([0] + order[:split], order[split:])
    fine_rows = plan.fine_rows
    spread = pl.pallas_call(
        functools.partial(fine_taps_kernel, plan),
        out_shape=jax.ShapeDtypeStruct((PAD + plan.fine_taps * fine_rows, LANES), jnp.float32),
        in_specs=[vmem, pl.BlockSpec(memory_space=pl.ANY)],
        out_specs=vmem,
        compiler_params=pltpu.CompilerParams(vmem_limit_bytes=16 * 2**20),
        name="fine_taps",
    )(section2_taps, received[order[1]])
    sums = pltpu.VMEM((fine_rows + plan.out_rows, LANES), jnp.float32)
    kept = pl.pallas_call(
        functools.partial(merge_kernel, plan, early),
        out_shape=jax.ShapeDtypeStruct((fine_rows, LANES), jnp.float32),
        in_specs=[vmem] * (1 + len(early)),
        out_specs=vmem,
        scratch_shapes=[sums],
        compiler_params=pltpu.CompilerParams(vmem_limit_bytes=16 * 2**20),
        name="merge",
    )(spread, *[received[step] for step in early])
    (dft, cosine_tab, sine_tab, join) = fine_tables(fine_rows)
    lines = pl.pallas_call(
        functools.partial(section_two_kernel, plan, late),
        out_shape=jax.ShapeDtypeStruct((2, 1, CH_DEV * KEEP), jnp.float32),
        in_specs=[vmem] * (7 + len(late)),
        out_specs=vmem,
        scratch_shapes=[sums],
        compiler_params=pltpu.CompilerParams(vmem_limit_bytes=24 * 2**20),
        name="section_two",
    )(
        width,
        kept,
        spread,
        dft,
        cosine_tab,
        sine_tab,
        join,
        *[received[step] for step in late],
    )
    return lines.reshape(1, 1, 2, 1, CH_DEV * KEEP)


def solution(mesh):
    placed = (P("pol", "groups", ("tm", "zoom")), P(), P(), P("groups"), P("groups"))

    def on_device(voltages, section1_taps, section2_taps, band_starts, band_widths):
        plan = Plan(
            mesh,
            voltages.shape[2],
            band_widths.shape[0],
            section1_taps.shape,
            section2_taps.shape,
        )
        arrays = (voltages, section1_taps, section2_taps, band_starts, band_widths)
        if plan.fits(section2_taps.shape):
            return direct_plan(plan, *arrays)
        return general_plan(*arrays)

    return jax.shard_map(
        on_device,
        mesh=mesh,
        in_specs=placed,
        out_specs=P("pol", "zoom", "groups", None, "tm"),
        check_vma=False,
    )
```

```python
import functools
import math

import jax
import jax.numpy as jnp
import numpy as np
from jax import lax
from jax.experimental import pallas as pl
from jax.experimental.pallas import tpu as pltpu
from jax.sharding import PartitionSpec as P

HOP = 432
FA = 27
FB = 128
KEEP = 2916
EDGE = 128
CH_DEV = 5
LIVE_DEV = 3


def shifted(value, axis, steps):
    count = lax.axis_size(axis)
    initial, last = (max(0, -steps), min(count, count - steps))
    return lax.ppermute(value, axis, [(source, source + steps) for source in range(initial, last)])


def with_halo(value, sides, width):
    for axis, dim in sides:
        count, length = (lax.axis_size(axis), value.shape[dim])
        up = [(i, (i + 1) % count) for i in range(count - 1)]
        down = [(j, i) for i, j in up]
        last = lax.slice_in_dim(value, length - width, length, axis=dim)
        initial = lax.slice_in_dim(value, 0, width, axis=dim)
        before = lax.ppermute(last, axis, up)
        after = lax.ppermute(initial, axis, down)
        value = jnp.concatenate([before, value, after], axis=dim)
    return value


def angle_table(rows, cols, length):
    product = (
        jnp.arange(rows, dtype=jnp.int32)[:, None]
        * jnp.arange(cols, dtype=jnp.int32)[None, :]
        % length
    )
    return product.astype(jnp.float32) * (2.0 * math.pi / length)


def rotation_block(length):
    angles = angle_table(length, length, length)
    cosine_tab = jnp.cos(angles).astype(jnp.bfloat16)
    sine_tab = jnp.sin(angles).astype(jnp.bfloat16)
    return jnp.stack([jnp.stack([cosine_tab, sine_tab]), jnp.stack([-sine_tab, cosine_tab])])


def joined_table(length):
    angles = angle_table(length, length, length)
    cosine_tab = jnp.cos(angles).astype(jnp.bfloat16)
    sine_tab = jnp.sin(angles).astype(jnp.bfloat16)
    top_rows = jnp.concatenate([cosine_tab, -sine_tab], axis=1)
    bottom_rows = jnp.concatenate([sine_tab, cosine_tab], axis=1)
    return jnp.concatenate([top_rows, bottom_rows], axis=0)


def bin_index(radix_a, radix_b, keep_len, edge_len):
    fine_len = radix_a * radix_b
    offsets = (np.arange(keep_len + 2 * edge_len) - keep_len // 2 - edge_len) % fine_len
    base = offsets % radix_a * (2 * radix_b) + offsets // radix_a
    return (base, base + radix_b)


def frame_view(segment, spectra, chan_len, hop_len):
    pieces = -(-chan_len // hop_len)
    framed = segment[:, : (spectra + pieces - 1) * hop_len].reshape(
        segment.shape[0], spectra + pieces - 1, hop_len
    )
    joined = jnp.concatenate(
        [framed[:, offset : offset + spectra] for offset in range(pieces)], axis=2
    )
    return joined[:, :, :chan_len]


def weighted_frames(signal, taps, spectra, hop_len):
    chan_len = taps.shape[1]
    running = jnp.zeros((2, spectra, chan_len), jnp.float32)
    for tap_index in range(taps.shape[0]):
        frames = frame_view(signal[:, tap_index * chan_len :], spectra, chan_len, hop_len)
        running = running + taps[tap_index][None, None, :] * frames.astype(jnp.float32)
    return running.astype(jnp.bfloat16)


def fine_spectra(series, section2_taps, radix_a, radix_b, keep_len, edge_len):
    tap_count, fine_len = section2_taps.shape
    items = series.shape[1]
    row_count = series.shape[2] // fine_len
    spectra = row_count - tap_count + 1
    row_blocks = series.reshape(2, items, row_count, fine_len)
    running = jnp.zeros((2, items, spectra, fine_len), jnp.float32)
    for tap_index in range(tap_count):
        running = running + section2_taps[tap_index] * row_blocks[
            :, :, tap_index : tap_index + spectra
        ].astype(jnp.float32)
    weighted = running.astype(jnp.bfloat16).reshape(2, items, spectra, radix_a, radix_b)
    partial_value = jnp.einsum(
        "pqkm,qcfmb->pcfkb", rotation_block(radix_a), weighted, preferred_element_type=jnp.float32
    )
    angles = angle_table(radix_a, radix_b, fine_len)
    cosine_tab = jnp.cos(angles)
    sine_tab = jnp.sin(angles)
    real_part = partial_value[0] * cosine_tab + partial_value[1] * sine_tab
    imag_part = partial_value[1] * cosine_tab - partial_value[0] * sine_tab
    twiddled = jnp.concatenate([real_part, imag_part], axis=-1).astype(jnp.bfloat16)
    spectrum = jnp.einsum(
        "cfkm,mj->cfkj", twiddled, joined_table(radix_b), preferred_element_type=jnp.float32
    )
    flattened = spectrum.reshape(items, spectra, radix_a * 2 * radix_b)
    real_index, imag_index = bin_index(radix_a, radix_b, keep_len, edge_len)
    return jnp.stack(
        [jnp.take(flattened, real_index, axis=2), jnp.take(flattened, imag_index, axis=2)]
    )


def stitch_bands(extended, upper_rim, lower_rim, slot_ids, band_width, keep_len, edge_len):
    centre = extended[..., edge_len : edge_len + keep_len]
    live = (slot_ids < band_width).astype(jnp.float32)[None, :, None, None]
    upper_ok = (slot_ids + 1 < band_width).astype(jnp.float32)[None, :, None, None]
    lower_ok = ((slot_ids >= 1) & (slot_ids < band_width)).astype(jnp.float32)[None, :, None, None]
    ramp = (jnp.arange(edge_len, dtype=jnp.float32) + 0.5) / (2.0 * edge_len)
    upper_weight = ramp * upper_ok
    lower_weight = ramp[::-1] * lower_ok
    low_part = centre[..., :edge_len] * (1.0 - lower_weight) + lower_rim * lower_weight
    high_part = centre[..., keep_len - edge_len :] * (1.0 - upper_weight) + upper_rim * upper_weight
    joined = jnp.concatenate(
        [low_part, centre[..., edge_len : keep_len - edge_len], high_part], axis=-1
    )
    return joined * live


def general_plan(voltages, section1_taps, section2_taps, band_starts, band_widths):
    signal = voltages[0]
    tap_count, chan_len = section1_taps.shape
    spectra = signal.shape[1] // HOP
    rim_len = tap_count * chan_len - HOP
    pieces = -(-chan_len // HOP)
    following = shifted(signal[:, :rim_len], ("tm", "zoom"), -1)
    padded = jnp.concatenate(
        [signal, following, jnp.zeros((2, pieces * HOP), jnp.bfloat16)], axis=1
    )
    weighted = weighted_frames(padded, section1_taps, spectra, HOP)
    coarse = jnp.einsum(
        "pqkn,qsn->pks", rotation_block(chan_len), weighted, preferred_element_type=jnp.float32
    ).astype(jnp.bfloat16)
    tm_count = lax.axis_size("tm")
    zoom_count = lax.axis_size("zoom")
    slot_local = jnp.arange(CH_DEV, dtype=jnp.int32)
    slot_ids = lax.axis_index("tm") * CH_DEV + slot_local
    band_count = band_widths.shape[0]
    band_ids = jnp.arange(band_count, dtype=jnp.int32)
    my_band = band_ids == lax.axis_index("zoom")
    band_width = jnp.sum(jnp.where(my_band, band_widths, 0))
    device_count = tm_count * zoom_count
    live_count = LIVE_DEV * device_count
    band_ends = jnp.cumsum(band_widths)
    band_firsts = band_ends - band_widths
    live_ids = jnp.arange(live_count, dtype=jnp.int32)
    band_of = jnp.sum((band_ends[None, :] <= live_ids[:, None]).astype(jnp.int32), axis=1)
    member = band_of[:, None] == band_ids[None, :]
    first_of = jnp.sum(jnp.where(member, band_firsts[None, :], 0), axis=1)
    start_of = jnp.sum(jnp.where(member, band_starts[None, :], 0), axis=1)
    live_channels = (start_of + live_ids - first_of) % chan_len
    packed_order = live_channels.reshape(device_count, LIVE_DEV).T.reshape(-1)
    packed = jnp.take(coarse, packed_order, axis=1).reshape(2, LIVE_DEV, device_count, spectra)
    received = lax.all_to_all(packed, ("tm", "zoom"), split_axis=2, concat_axis=2, tiled=True)
    series = received.reshape(2, received.shape[1], -1)
    computed = fine_spectra(series, section2_taps, FA, FB, KEEP, EDGE)
    wanted = jnp.sum(jnp.where(my_band, band_firsts, 0)) + slot_ids
    valid = slot_ids < band_width
    piece = lax.all_gather(computed, ("tm", "zoom"), axis=1, tiled=True)
    piece_ids = jnp.arange(piece.shape[1], dtype=jnp.int32)
    chosen = ((wanted[:, None] == piece_ids[None, :]) & valid[:, None]).astype(jnp.float32)
    extended = jnp.einsum("kn,pnfx->pkfx", chosen, piece, precision=lax.Precision.HIGHEST)
    seam_rows = jnp.concatenate([extended[..., :EDGE], extended[..., KEEP + EDGE :]], axis=-1)
    widened = with_halo(seam_rows, (("tm", 1),), 1)
    upper_rim = widened[:, 2:, :, :EDGE]
    lower_rim = widened[:, :CH_DEV, :, EDGE:]
    stitched = stitch_bands(extended, upper_rim, lower_rim, slot_ids, band_width, KEEP, EDGE)
    fine_count = stitched.shape[2]
    result = jnp.transpose(stitched, (0, 2, 1, 3)).reshape(2, fine_count, CH_DEV * KEEP)
    return result[None, None]


ROWS = 8
LANES = 128
SLOT_LANES = 2 * ROWS
PAD = 8
NT = (((1,), (1,)), ((), ()))


def sine_quarter(value):
    square = value * value
    total = -3.5988432e-06
    for factor in (1.604411848e-04, -4.6817541353e-03, 7.96926262462e-02, -6.459640975062e-01):
        total = total * square + factor
    return (total * square + 1.5707963267949) * value


def section_one_kernel(plan, starts_hbm, widths_hbm, taps_hbm, signal_ref, *rest):
    (outs, (width_ref, taps_rows, frames, total, *rest)) = (
        rest[: plan.devices],
        rest[plan.devices :],
    )
    (starts_ref, widths_ref, taps_ref, small_sems, sems) = rest
    small = [
        pltpu.make_async_copy(source, target, small_sems.at[index])
        for index, (source, target) in enumerate(
            [(starts_hbm, starts_ref), (widths_hbm, widths_ref), (taps_hbm, taps_ref)]
        )
    ]
    for copy in small:
        copy.start()
    blocks, chan_len, live = (plan.blocks, plan.chan_len, plan.live)
    half = ROWS * live
    columns = 2 * half
    lead = plan.lead
    copies = [
        pltpu.make_async_copy(
            signal_ref.at[:, block], frames.at[block, pl.ds(lead, plan.local_rows)], sems.at[block]
        )
        for block in range(blocks)
    ]
    for copy in copies:
        copy.start(priority=1)
    edge = jnp.zeros((blocks, lead, 2, LANES), jnp.bfloat16)
    frames[:, :lead] = edge
    frames[:, lead + plan.local_rows :] = edge

    for copy in small:
        copy.wait()
    row = lax.broadcasted_iota(jnp.int32, (columns, 1), 0)
    imag = (row >= half).astype(jnp.int32)
    shift = (row - imag * half) // live
    ident = row - imag * half - shift * live
    channel = jnp.zeros((columns, 1), jnp.int32)
    first = jnp.int32(0)
    firsts = []
    for band in range(plan.bands):
        inside = (ident >= first) & (ident < first + widths_ref[band])
        channel = jnp.where(inside, starts_ref[band] + ident - first, channel)
        firsts.append(first)
        first = first + widths_ref[band]
    phase = lax.broadcasted_iota(jnp.int32, (columns, chan_len), 1) - HOP * shift
    turn = (channel * phase + imag * (chan_len // 4)) & (chan_len - 1)
    quarter = chan_len // 4
    folded = jnp.abs(turn - 2 * quarter)
    angle = (folded - quarter).astype(jnp.float32) * (1.0 / quarter)
    rotation = sine_quarter(angle).astype(jnp.bfloat16)

    flat = jnp.concatenate(
        [jnp.broadcast_to(taps_ref[tap : tap + 1, :], (8, chan_len)) for tap in range(plan.taps)]
        + [jnp.zeros((8, plan.depth - plan.taps * chan_len), jnp.float32)],
        axis=1,
    )
    for shift_index in range(ROWS):
        taps_rows[shift_index] = (
            pltpu.roll(flat, HOP * shift_index, axis=1) if shift_index else flat
        )
    count = 2 * plan.out_rows
    pairs = frames.reshape(blocks, 2 * (plan.local_rows + 2 * lead), LANES)
    acc = jnp.zeros((count, columns), jnp.float32)
    order = sorted(range(plan.depth // LANES), key=lambda index: (index % blocks, index // blocks))
    turns = chan_len // LANES
    bounds = (9, blocks)

    def column_tile(index):
        scale = jnp.concatenate(
            [
                jnp.broadcast_to(
                    taps_rows[shift_index, :, pl.ds(index * LANES, LANES)][None],
                    (live // 8, 8, LANES),
                ).reshape(live, LANES)
                for shift_index in range(ROWS)
            ],
            axis=0,
        ).astype(jnp.bfloat16)
        turned = rotation[:, index % turns * LANES : (index % turns + 1) * LANES]
        return jnp.concatenate([scale * turned[:half], scale * turned[half:]], axis=0)

    groups = [order[piece : piece + turns] for piece in range(0, len(order), turns)]
    (begin, seen) = (0, 0)
    for bound in bounds:
        end = begin
        while end < len(groups) and max(index % blocks for index in groups[end]) < bound:
            end += 1
        staged = groups[begin:end]
        rights = [
            jnp.concatenate([column_tile(index) for index in group], axis=1) for group in staged
        ]
        for copy in copies[seen:bound]:
            copy.wait()
        for group, right in zip(staged, rights):
            left = jnp.concatenate(
                [pairs[index % blocks, pl.ds(2 * (index // blocks), count), :] for index in group],
                axis=1,
            )
            acc = acc + lax.dot_general(left, right, NT, preferred_element_type=jnp.float32)
        (begin, seen) = (end, bound)
    for tile in range(columns // LANES):
        total[tile] = acc[:, tile * LANES : (tile + 1) * LANES]
    (real_rows, imag_rows) = (
        jnp.concatenate(
            [total[tile, pl.ds(part, plan.out_rows, 2), :] for tile in range(columns // LANES)],
            axis=1,
        )
        for part in range(2)
    )
    lane = lax.broadcasted_iota(jnp.int32, (1, columns), 1)
    sign = jnp.where(lane < half, -1.0, 1.0)
    coarse = (real_rows + sign * pltpu.roll(imag_rows, half, axis=1)).astype(jnp.bfloat16)

    (tm, zoom) = (lax.axis_index("tm"), lax.axis_index("zoom"))
    mine = jnp.int32(0)
    for band in range(plan.bands):
        mine = jnp.where(zoom == band, widths_ref[band], mine)
    width_ref[...] = jnp.broadcast_to(mine, width_ref.shape)
    code = ident * SLOT_LANES + imag * ROWS + shift
    out_lane = lax.broadcasted_iota(jnp.int32, (1, LANES), 1)
    slot = out_lane // SLOT_LANES
    picks = []
    for step in range(plan.devices):
        target = jnp.bitwise_xor(tm * plan.zooms + zoom, step)
        (target_tm, target_zoom) = (target // plan.zooms, target % plan.zooms)
        (band_first, width) = (jnp.int32(0), jnp.int32(0))
        for band in range(plan.bands):
            band_first = jnp.where(target_zoom == band, firsts[band], band_first)
            width = jnp.where(target_zoom == band, widths_ref[band], width)
        base = target_tm * CH_DEV - 1
        position = base + slot
        valid = (position >= 0) & (position < width) & (slot < CH_DEV + 2)
        wanted = jnp.where(valid, (band_first + base) * SLOT_LANES + out_lane, -1)
        pick = (code == wanted).astype(jnp.float32).astype(jnp.bfloat16)
        picks.append(pick)

    chosen = lax.dot_general(
        coarse,
        jnp.concatenate(picks, axis=1),
        (((1,), (0,)), ((), ())),
        preferred_element_type=jnp.float32,
    ).astype(jnp.bfloat16)
    for step in range(plan.devices):
        outs[step][...] = chosen[:, step * LANES : (step + 1) * LANES]


def fine_taps_kernel(plan, taps_ref, after_ref, out_ref):
    lane = lax.broadcasted_iota(jnp.int32, (SLOT_LANES, LANES), 1)
    row = lax.broadcasted_iota(jnp.int32, (SLOT_LANES, LANES), 0)
    keep = lane // ROWS == row
    source = lax.broadcasted_iota(jnp.int32, (2 * LANES, LANES), 0)
    target = lax.broadcasted_iota(jnp.int32, (2 * LANES, LANES), 1)
    spread = (source % ROWS == target % ROWS).astype(jnp.float32).astype(jnp.bfloat16)
    for tap in range(plan.fine_taps):
        (high, low) = ([], [])
        for tile in range(plan.fine_rows // SLOT_LANES):
            line = taps_ref[tap : tap + 1, tile * LANES : (tile + 1) * LANES]
            part = jnp.where(keep, jnp.broadcast_to(line, (SLOT_LANES, LANES)), 0.0)
            rounded = part.astype(jnp.bfloat16)
            high.append(rounded)
            low.append((part - rounded.astype(jnp.float32)).astype(jnp.bfloat16))
        both = jnp.concatenate([jnp.concatenate(high, axis=0), jnp.concatenate(low, axis=0)], axis=1)
        out_ref[pl.ds(PAD + tap * plan.fine_rows, plan.fine_rows), :] = lax.dot_general(
            both, spread, (((1,), (0,)), ((), ())), preferred_element_type=jnp.float32
        )
    out_ref[:PAD] = jnp.zeros((PAD, LANES), jnp.float32)


def add_blocks(plan, steps, taps_ref, blocks, sums):
    here = lax.axis_index("tm") * plan.zooms + lax.axis_index("zoom")
    (fine_rows, out_rows) = (plan.fine_rows, plan.out_rows)
    sums[...] = jnp.zeros_like(sums)
    for step, block in zip(steps, blocks):
        start = jnp.bitwise_xor(here, step) * plan.local_rows + (PAD - plan.lead)
        goal = pl.ds(lax.rem(start + (fine_rows - PAD), fine_rows), out_rows)
        scale = taps_ref[pl.ds(start, out_rows), :]
        sums[goal, :] += scale * block[...].astype(jnp.float32)
    return jnp.concatenate(
        [
            sums[:out_rows] + sums[fine_rows : fine_rows + out_rows],
            sums[out_rows:fine_rows],
        ],
        axis=0,
    )


def merge_kernel(plan, steps, taps_ref, *rest):
    (blocks, (kept_ref, sums)) = (rest[: len(steps)], rest[len(steps) :])
    kept_ref[...] = add_blocks(plan, steps, taps_ref, blocks, sums)


def section_two_kernel(
    plan, steps, width_ref, kept_ref, taps_ref, dft_ref, cos_ref, sin_ref, join_ref, *rest
):
    (blocks, (out_ref, sums)) = (rest[: len(steps)], rest[len(steps) :])
    tm = lax.axis_index("tm")
    (fine_rows, bins) = (plan.fine_rows, plan.bins)
    fine_in = kept_ref[...] + add_blocks(plan, steps, taps_ref, blocks, sums)
    spun = lax.dot_general(
        dft_ref[...],
        fine_in.astype(jnp.bfloat16),
        (((1,), (0,)), ((), ())),
        preferred_element_type=jnp.float32,
    )
    (cosine_tab, sine_tab) = (cos_ref[...], sin_ref[...])
    mixed = jnp.concatenate(
        [
            (part * factor).astype(jnp.bfloat16)
            for part in (spun[:bins], spun[bins:])
            for factor in (cosine_tab, sine_tab)
        ],
        axis=1,
    )
    joined = lax.dot_general(join_ref[...], mixed, NT, preferred_element_type=jnp.float32)

    slots = LANES // SLOT_LANES
    high = 2 * slots
    flat = [jnp.zeros((high, LANES), jnp.float32)] * (-(-(ROWS * fine_rows) // LANES) + 2)
    for turn in range(ROWS):
        (first, offset) = divmod(turn * fine_rows, LANES)
        piece = jnp.concatenate(
            [joined[turn * high : (turn + 1) * high], jnp.zeros((high, LANES), jnp.float32)], axis=1
        )
        if offset:
            piece = pltpu.roll(piece, offset, axis=1)
        for tile in range(min(bins // LANES + 1, len(flat) - first)):
            flat[first + tile] = flat[first + tile] + piece[:, tile * LANES : (tile + 1) * LANES]

    row = lax.broadcasted_iota(jnp.int32, (high, LANES), 0)
    lane = lax.broadcasted_iota(jnp.int32, (high, LANES), 1)
    width = width_ref[0:1, :]
    slot = tm * CH_DEV + row % slots - 1
    live = (slot < width).astype(jnp.float32)
    upper_ok = (slot + 1 < width).astype(jnp.float32)
    lower_ok = ((slot >= 1) & (slot < width)).astype(jnp.float32)
    (lead, skew) = divmod(KEEP + EDGE, LANES)
    below = jnp.where(
        lane < LANES - skew,
        pltpu.roll(flat[lead], LANES - skew, axis=1),
        pltpu.roll(flat[lead + 1], LANES - skew, axis=1),
    )
    below = pltpu.roll(below, 1, axis=0)
    (lead, skew) = divmod(KEEP - EDGE, LANES)
    above = pltpu.roll(pltpu.roll(flat[0], skew, axis=1), high - 1, axis=0)
    position = lane.astype(jnp.float32)
    own = flat[1:]
    span = -(-KEEP // LANES)
    parts = []
    for tile in range(span):
        value = own[tile]
        if tile == 0:
            weight = (EDGE - 0.5 - position) * (0.5 / EDGE) * lower_ok
            value = value * (1.0 - weight) + below * weight
        if tile in (lead, lead + 1):
            ramp = (position + (tile * LANES - (KEEP - EDGE) + 0.5)) * (0.5 / EDGE)
            inside = lane >= skew if tile == lead else lane < skew
            weight = jnp.where(inside, ramp * upper_ok, 0.0)
            value = value * (1.0 - weight) + above * weight
        value = value * live
        if tile == span - 1:
            value = jnp.where(lane < KEEP - tile * LANES, value, 0.0)
        parts.append(value)
    parts = [jnp.zeros_like(parts[0])] + parts + [jnp.zeros_like(parts[0])]

    carry = [None, None]
    for place in range(CH_DEV):
        (first, offset) = divmod(place * KEEP, LANES)
        (after, _) = divmod((place + 1) * KEEP, LANES)
        last = place == CH_DEV - 1
        count = after - first + 1
        for part in range(2):
            picked = part * slots + place + 1
            tiles = []
            for tile in range(count):
                value = parts[tile + 1][part * slots : (part + 1) * slots]
                if offset:
                    before = parts[tile][part * slots : (part + 1) * slots]
                    value = jnp.where(
                        lane[:slots] < offset,
                        pltpu.roll(before, offset, axis=1),
                        pltpu.roll(value, offset, axis=1),
                    )
                tiles.append(value[picked % slots : picked % slots + 1])
            if place:
                tiles[0] = tiles[0] + carry[part]
            carry[part] = tiles[-1]
            if not last:
                tiles = tiles[:-1]
            line = jnp.concatenate(tiles, axis=1)
            end = min(first * LANES + len(tiles) * LANES, CH_DEV * KEEP)
            out_ref[part, :, first * LANES : end] = line[:, : end - first * LANES]


def fine_tables(fine_rows):
    fine_len = fine_rows * ROWS
    offset = KEEP // 2 + EDGE
    bins = np.arange(fine_rows) - offset
    spin = 2.0 * np.pi * (np.outer(bins, np.arange(fine_rows)) % fine_rows) / fine_rows
    margin = ((0, -fine_rows % LANES), (0, 0))
    dft = np.concatenate([np.pad(np.cos(spin), margin), np.pad(np.sin(spin), margin)], axis=0)
    twist = 2.0 * np.pi * (np.outer(bins, np.arange(LANES) % ROWS) % fine_len) / fine_len
    join = np.zeros((ROWS, 2, LANES // SLOT_LANES, 4, LANES // SLOT_LANES, 2, ROWS))
    turn = 2.0 * np.pi * (np.outer(np.arange(ROWS), np.arange(ROWS)) % ROWS) / ROWS
    (cosine, sine) = (np.cos(turn), np.sin(turn))
    for slot in range(LANES // SLOT_LANES):
        real, imag = (join[:, 0, slot, :, slot], join[:, 1, slot, :, slot])
        real[:, 0, 0], real[:, 0, 1] = (cosine, sine)
        real[:, 1, 0], real[:, 1, 1] = (-sine, cosine)
        real[:, 2, 0], real[:, 2, 1] = (-sine, cosine)
        real[:, 3, 0], real[:, 3, 1] = (-cosine, -sine)
        imag[:, 0, 0], imag[:, 0, 1] = (-sine, cosine)
        imag[:, 1, 0], imag[:, 1, 1] = (-cosine, -sine)
        imag[:, 2, 0], imag[:, 2, 1] = (-cosine, -sine)
        imag[:, 3, 0], imag[:, 3, 1] = (sine, -cosine)
    return (
        jnp.asarray(dft, jnp.bfloat16),
        jnp.asarray(np.pad(np.cos(twist), margin), jnp.float32),
        jnp.asarray(np.pad(np.sin(twist), margin), jnp.float32),
        jnp.asarray(join.reshape(LANES, 4 * LANES), jnp.bfloat16),
    )


class Plan:
    def __init__(self, mesh, samples, bands, section1_shape, section2_shape):
        (self.tms, self.zooms) = (mesh.shape["tm"], mesh.shape["zoom"])
        self.devices = self.tms * self.zooms
        self.bands = bands
        (self.taps, self.chan_len) = section1_shape
        self.fine_taps = section2_shape[0]
        self.live = LIVE_DEV * self.devices
        self.samples = samples
        self.row_len = ROWS * HOP
        self.blocks = self.row_len // LANES
        self.local_rows = samples // self.row_len
        reach = (ROWS - 1) * HOP + self.taps * self.chan_len
        unit = max(self.chan_len, 2 * LANES)
        self.depth = -(-reach // unit) * unit
        self.lead = -(-self.depth // self.row_len) - 1
        self.out_rows = self.local_rows + self.lead
        self.fine_rows = section2_shape[1] // ROWS
        self.bins = -(-self.fine_rows // LANES) * LANES

    def fits(self, section2_shape):
        return (
            self.row_len % LANES == 0
            and self.samples % self.row_len == 0
            and self.chan_len & (self.chan_len - 1) == 0
            and self.chan_len % LANES == 0
            and self.devices & (self.devices - 1) == 0
            and self.live % 8 == 0
            and (2 * ROWS * self.live) % LANES == 0
            and 2 * ROWS * self.live <= 4 * LANES
            and (CH_DEV + 2) * SLOT_LANES <= LANES
            and self.devices >= 4
            and self.lead <= PAD
            and self.out_rows <= self.fine_rows
            and self.out_rows % 16 == 0
            and self.fine_rows % 16 == 0
            and EDGE == LANES
            and KEEP + 2 * EDGE <= section2_shape[1]
            and section2_shape[1] % ROWS == 0
            and self.devices * self.samples == HOP * self.fine_taps * section2_shape[1]
        )


def direct_plan(plan, voltages, section1_taps, section2_taps, band_starts, band_widths):
    signal = voltages[0].reshape(2, plan.local_rows, plan.blocks, LANES).transpose(1, 2, 0, 3)
    far = [
        pltpu.with_memory_space_constraint(array, pltpu.HBM)
        for array in (band_starts, band_widths, section1_taps, signal)
    ]
    vmem = pl.BlockSpec(memory_space=pltpu.VMEM)
    columns = 2 * ROWS * plan.live
    block = jax.ShapeDtypeStruct((plan.out_rows, LANES), jnp.bfloat16)
    (*sent, width) = pl.pallas_call(
        functools.partial(section_one_kernel, plan),
        out_shape=[block] * plan.devices + [jax.ShapeDtypeStruct((8, LANES), jnp.int32)],
        in_specs=[pl.BlockSpec(memory_space=pltpu.HBM)] * 4,
        out_specs=[vmem] * (plan.devices + 1),
        scratch_shapes=[
            pltpu.VMEM((ROWS, 8, plan.depth), jnp.float32),
            pltpu.VMEM((plan.blocks, plan.local_rows + 2 * plan.lead, 2, LANES), jnp.bfloat16),
            pltpu.VMEM((columns // LANES, 2 * plan.out_rows, LANES), jnp.float32),
            pltpu.SMEM((plan.bands,), jnp.int32),
            pltpu.SMEM((plan.bands,), jnp.int32),
            pltpu.VMEM((plan.taps, plan.chan_len), jnp.float32),
            pltpu.SemaphoreType.DMA((3,)),
            pltpu.SemaphoreType.DMA((plan.blocks,)),
        ],
        compiler_params=pltpu.CompilerParams(vmem_limit_bytes=40 * 2**20),
        name="section_one",
    )(*far)
    order = list(range(plan.devices - 1, 0, -1))
    received = {0: sent[0]}
    for step in order:
        pairs = [(index, index ^ step) for index in range(plan.devices)]
        received[step] = lax.ppermute(sent[step], ("tm", "zoom"), pairs)
    split = len(order) // 2 + 1
    (early, late) = ([0] + order[:split], order[split:])
    fine_rows = plan.fine_rows
    spread = pl.pallas_call(
        functools.partial(fine_taps_kernel, plan),
        out_shape=jax.ShapeDtypeStruct((PAD + plan.fine_taps * fine_rows, LANES), jnp.float32),
        in_specs=[vmem, pl.BlockSpec(memory_space=pl.ANY)],
        out_specs=vmem,
        compiler_params=pltpu.CompilerParams(vmem_limit_bytes=16 * 2**20),
        name="fine_taps",
    )(section2_taps, received[order[1]])
    sums = pltpu.VMEM((fine_rows + plan.out_rows, LANES), jnp.float32)
    kept = pl.pallas_call(
        functools.partial(merge_kernel, plan, early),
        out_shape=jax.ShapeDtypeStruct((fine_rows, LANES), jnp.float32),
        in_specs=[vmem] * (1 + len(early)),
        out_specs=vmem,
        scratch_shapes=[sums],
        compiler_params=pltpu.CompilerParams(vmem_limit_bytes=16 * 2**20),
        name="merge",
    )(spread, *[received[step] for step in early])
    (dft, cosine_tab, sine_tab, join) = fine_tables(fine_rows)
    lines = pl.pallas_call(
        functools.partial(section_two_kernel, plan, late),
        out_shape=jax.ShapeDtypeStruct((2, 1, CH_DEV * KEEP), jnp.float32),
        in_specs=[vmem] * (7 + len(late)),
        out_specs=vmem,
        scratch_shapes=[sums],
        compiler_params=pltpu.CompilerParams(vmem_limit_bytes=24 * 2**20),
        name="section_two",
    )(
        width,
        kept,
        spread,
        dft,
        cosine_tab,
        sine_tab,
        join,
        *[received[step] for step in late],
    )
    return lines.reshape(1, 1, 2, 1, CH_DEV * KEEP)


def solution(mesh):
    placed = (P("pol", "groups", ("tm", "zoom")), P(), P(), P("groups"), P("groups"))

    def on_device(voltages, section1_taps, section2_taps, band_starts, band_widths):
        plan = Plan(
            mesh,
            voltages.shape[2],
            band_widths.shape[0],
            section1_taps.shape,
            section2_taps.shape,
        )
        arrays = (voltages, section1_taps, section2_taps, band_starts, band_widths)
        if plan.fits(section2_taps.shape):
            return direct_plan(plan, *arrays)
        return general_plan(*arrays)

    return jax.shard_map(
        on_device,
        mesh=mesh,
        in_specs=placed,
        out_specs=P("pol", "zoom", "groups", None, "tm"),
        check_vma=False,
    )
```

```python
import functools
import math

import jax
import jax.numpy as jnp
import numpy as np
from jax import lax
from jax.experimental import pallas as pl
from jax.experimental.pallas import tpu as pltpu
from jax.sharding import PartitionSpec as P

HOP = 432
FA = 27
FB = 128
KEEP = 2916
EDGE = 128
CH_DEV = 5
LIVE_DEV = 3


def shifted(value, axis, steps):
    count = lax.axis_size(axis)
    initial, last = (max(0, -steps), min(count, count - steps))
    return lax.ppermute(value, axis, [(source, source + steps) for source in range(initial, last)])


def with_halo(value, sides, width):
    for axis, dim in sides:
        count, length = (lax.axis_size(axis), value.shape[dim])
        up = [(i, (i + 1) % count) for i in range(count - 1)]
        down = [(j, i) for i, j in up]
        last = lax.slice_in_dim(value, length - width, length, axis=dim)
        initial = lax.slice_in_dim(value, 0, width, axis=dim)
        before = lax.ppermute(last, axis, up)
        after = lax.ppermute(initial, axis, down)
        value = jnp.concatenate([before, value, after], axis=dim)
    return value


def angle_table(rows, cols, length):
    product = (
        jnp.arange(rows, dtype=jnp.int32)[:, None]
        * jnp.arange(cols, dtype=jnp.int32)[None, :]
        % length
    )
    return product.astype(jnp.float32) * (2.0 * math.pi / length)


def rotation_block(length):
    angles = angle_table(length, length, length)
    cosine_tab = jnp.cos(angles).astype(jnp.bfloat16)
    sine_tab = jnp.sin(angles).astype(jnp.bfloat16)
    return jnp.stack([jnp.stack([cosine_tab, sine_tab]), jnp.stack([-sine_tab, cosine_tab])])


def joined_table(length):
    angles = angle_table(length, length, length)
    cosine_tab = jnp.cos(angles).astype(jnp.bfloat16)
    sine_tab = jnp.sin(angles).astype(jnp.bfloat16)
    top_rows = jnp.concatenate([cosine_tab, -sine_tab], axis=1)
    bottom_rows = jnp.concatenate([sine_tab, cosine_tab], axis=1)
    return jnp.concatenate([top_rows, bottom_rows], axis=0)


def bin_index(radix_a, radix_b, keep_len, edge_len):
    fine_len = radix_a * radix_b
    offsets = (np.arange(keep_len + 2 * edge_len) - keep_len // 2 - edge_len) % fine_len
    base = offsets % radix_a * (2 * radix_b) + offsets // radix_a
    return (base, base + radix_b)


def frame_view(segment, spectra, chan_len, hop_len):
    pieces = -(-chan_len // hop_len)
    framed = segment[:, : (spectra + pieces - 1) * hop_len].reshape(
        segment.shape[0], spectra + pieces - 1, hop_len
    )
    joined = jnp.concatenate(
        [framed[:, offset : offset + spectra] for offset in range(pieces)], axis=2
    )
    return joined[:, :, :chan_len]


def weighted_frames(signal, taps, spectra, hop_len):
    chan_len = taps.shape[1]
    running = jnp.zeros((2, spectra, chan_len), jnp.float32)
    for tap_index in range(taps.shape[0]):
        frames = frame_view(signal[:, tap_index * chan_len :], spectra, chan_len, hop_len)
        running = running + taps[tap_index][None, None, :] * frames.astype(jnp.float32)
    return running.astype(jnp.bfloat16)


def fine_spectra(series, section2_taps, radix_a, radix_b, keep_len, edge_len):
    tap_count, fine_len = section2_taps.shape
    items = series.shape[1]
    row_count = series.shape[2] // fine_len
    spectra = row_count - tap_count + 1
    row_blocks = series.reshape(2, items, row_count, fine_len)
    running = jnp.zeros((2, items, spectra, fine_len), jnp.float32)
    for tap_index in range(tap_count):
        running = running + section2_taps[tap_index] * row_blocks[
            :, :, tap_index : tap_index + spectra
        ].astype(jnp.float32)
    weighted = running.astype(jnp.bfloat16).reshape(2, items, spectra, radix_a, radix_b)
    partial_value = jnp.einsum(
        "pqkm,qcfmb->pcfkb", rotation_block(radix_a), weighted, preferred_element_type=jnp.float32
    )
    angles = angle_table(radix_a, radix_b, fine_len)
    cosine_tab = jnp.cos(angles)
    sine_tab = jnp.sin(angles)
    real_part = partial_value[0] * cosine_tab + partial_value[1] * sine_tab
    imag_part = partial_value[1] * cosine_tab - partial_value[0] * sine_tab
    twiddled = jnp.concatenate([real_part, imag_part], axis=-1).astype(jnp.bfloat16)
    spectrum = jnp.einsum(
        "cfkm,mj->cfkj", twiddled, joined_table(radix_b), preferred_element_type=jnp.float32
    )
    flattened = spectrum.reshape(items, spectra, radix_a * 2 * radix_b)
    real_index, imag_index = bin_index(radix_a, radix_b, keep_len, edge_len)
    return jnp.stack(
        [jnp.take(flattened, real_index, axis=2), jnp.take(flattened, imag_index, axis=2)]
    )


def stitch_bands(extended, upper_rim, lower_rim, slot_ids, band_width, keep_len, edge_len):
    centre = extended[..., edge_len : edge_len + keep_len]
    live = (slot_ids < band_width).astype(jnp.float32)[None, :, None, None]
    upper_ok = (slot_ids + 1 < band_width).astype(jnp.float32)[None, :, None, None]
    lower_ok = ((slot_ids >= 1) & (slot_ids < band_width)).astype(jnp.float32)[None, :, None, None]
    ramp = (jnp.arange(edge_len, dtype=jnp.float32) + 0.5) / (2.0 * edge_len)
    upper_weight = ramp * upper_ok
    lower_weight = ramp[::-1] * lower_ok
    low_part = centre[..., :edge_len] * (1.0 - lower_weight) + lower_rim * lower_weight
    high_part = centre[..., keep_len - edge_len :] * (1.0 - upper_weight) + upper_rim * upper_weight
    joined = jnp.concatenate(
        [low_part, centre[..., edge_len : keep_len - edge_len], high_part], axis=-1
    )
    return joined * live


def general_plan(voltages, section1_taps, section2_taps, band_starts, band_widths):
    signal = voltages[0]
    tap_count, chan_len = section1_taps.shape
    spectra = signal.shape[1] // HOP
    rim_len = tap_count * chan_len - HOP
    pieces = -(-chan_len // HOP)
    following = shifted(signal[:, :rim_len], ("tm", "zoom"), -1)
    padded = jnp.concatenate(
        [signal, following, jnp.zeros((2, pieces * HOP), jnp.bfloat16)], axis=1
    )
    weighted = weighted_frames(padded, section1_taps, spectra, HOP)
    coarse = jnp.einsum(
        "pqkn,qsn->pks", rotation_block(chan_len), weighted, preferred_element_type=jnp.float32
    ).astype(jnp.bfloat16)
    tm_count = lax.axis_size("tm")
    zoom_count = lax.axis_size("zoom")
    slot_local = jnp.arange(CH_DEV, dtype=jnp.int32)
    slot_ids = lax.axis_index("tm") * CH_DEV + slot_local
    band_count = band_widths.shape[0]
    band_ids = jnp.arange(band_count, dtype=jnp.int32)
    my_band = band_ids == lax.axis_index("zoom")
    band_width = jnp.sum(jnp.where(my_band, band_widths, 0))
    device_count = tm_count * zoom_count
    live_count = LIVE_DEV * device_count
    band_ends = jnp.cumsum(band_widths)
    band_firsts = band_ends - band_widths
    live_ids = jnp.arange(live_count, dtype=jnp.int32)
    band_of = jnp.sum((band_ends[None, :] <= live_ids[:, None]).astype(jnp.int32), axis=1)
    member = band_of[:, None] == band_ids[None, :]
    first_of = jnp.sum(jnp.where(member, band_firsts[None, :], 0), axis=1)
    start_of = jnp.sum(jnp.where(member, band_starts[None, :], 0), axis=1)
    live_channels = (start_of + live_ids - first_of) % chan_len
    packed_order = live_channels.reshape(device_count, LIVE_DEV).T.reshape(-1)
    packed = jnp.take(coarse, packed_order, axis=1).reshape(2, LIVE_DEV, device_count, spectra)
    received = lax.all_to_all(packed, ("tm", "zoom"), split_axis=2, concat_axis=2, tiled=True)
    series = received.reshape(2, received.shape[1], -1)
    computed = fine_spectra(series, section2_taps, FA, FB, KEEP, EDGE)
    wanted = jnp.sum(jnp.where(my_band, band_firsts, 0)) + slot_ids
    valid = slot_ids < band_width
    piece = lax.all_gather(computed, ("tm", "zoom"), axis=1, tiled=True)
    piece_ids = jnp.arange(piece.shape[1], dtype=jnp.int32)
    chosen = ((wanted[:, None] == piece_ids[None, :]) & valid[:, None]).astype(jnp.float32)
    extended = jnp.einsum("kn,pnfx->pkfx", chosen, piece, precision=lax.Precision.HIGHEST)
    seam_rows = jnp.concatenate([extended[..., :EDGE], extended[..., KEEP + EDGE :]], axis=-1)
    widened = with_halo(seam_rows, (("tm", 1),), 1)
    upper_rim = widened[:, 2:, :, :EDGE]
    lower_rim = widened[:, :CH_DEV, :, EDGE:]
    stitched = stitch_bands(extended, upper_rim, lower_rim, slot_ids, band_width, KEEP, EDGE)
    fine_count = stitched.shape[2]
    result = jnp.transpose(stitched, (0, 2, 1, 3)).reshape(2, fine_count, CH_DEV * KEEP)
    return result[None, None]


ROWS = 8
LANES = 128
SLOT_LANES = 2 * ROWS
PAD = 8
NT = (((1,), (1,)), ((), ()))


def sine_quarter(value):
    square = value * value
    total = -3.5988432e-06
    for factor in (1.604411848e-04, -4.6817541353e-03, 7.96926262462e-02, -6.459640975062e-01):
        total = total * square + factor
    return (total * square + 1.5707963267949) * value


def section_one_kernel(plan, starts_hbm, widths_hbm, taps_hbm, signal_ref, *rest):
    (outs, (width_ref, taps_rows, frames, total, *rest)) = (
        rest[: plan.devices],
        rest[plan.devices :],
    )
    (starts_ref, widths_ref, taps_ref, small_sems, sems) = rest
    small = [
        pltpu.make_async_copy(source, target, small_sems.at[index])
        for index, (source, target) in enumerate(
            [(starts_hbm, starts_ref), (widths_hbm, widths_ref), (taps_hbm, taps_ref)]
        )
    ]
    for copy in small:
        copy.start()
    blocks, chan_len, live = (plan.blocks, plan.chan_len, plan.live)
    half = ROWS * live
    columns = 2 * half
    lead = plan.lead
    copies = [
        pltpu.make_async_copy(
            signal_ref.at[:, block], frames.at[block, pl.ds(lead, plan.local_rows)], sems.at[block]
        )
        for block in range(blocks)
    ]
    for copy in copies:
        copy.start(priority=1)
    edge = jnp.zeros((blocks, lead, 2, LANES), jnp.bfloat16)
    frames[:, :lead] = edge
    frames[:, lead + plan.local_rows :] = edge

    for copy in small:
        copy.wait()
    row = lax.broadcasted_iota(jnp.int32, (columns, 1), 0)
    imag = (row >= half).astype(jnp.int32)
    shift = (row - imag * half) // live
    ident = row - imag * half - shift * live
    channel = jnp.zeros((columns, 1), jnp.int32)
    first = jnp.int32(0)
    firsts = []
    for band in range(plan.bands):
        inside = (ident >= first) & (ident < first + widths_ref[band])
        channel = jnp.where(inside, starts_ref[band] + ident - first, channel)
        firsts.append(first)
        first = first + widths_ref[band]
    phase = lax.broadcasted_iota(jnp.int32, (columns, chan_len), 1) - HOP * shift
    turn = (channel * phase + imag * (chan_len // 4)) & (chan_len - 1)
    quarter = chan_len // 4
    folded = jnp.abs(turn - 2 * quarter)
    angle = (folded - quarter).astype(jnp.float32) * (1.0 / quarter)
    rotation = sine_quarter(angle).astype(jnp.bfloat16)

    flat = jnp.concatenate(
        [jnp.broadcast_to(taps_ref[tap : tap + 1, :], (8, chan_len)) for tap in range(plan.taps)]
        + [jnp.zeros((8, plan.depth - plan.taps * chan_len), jnp.float32)],
        axis=1,
    )
    for shift_index in range(ROWS):
        taps_rows[shift_index] = (
            pltpu.roll(flat, HOP * shift_index, axis=1) if shift_index else flat
        )
    count = 2 * plan.out_rows
    pairs = frames.reshape(blocks, 2 * (plan.local_rows + 2 * lead), LANES)
    acc = jnp.zeros((count, columns), jnp.float32)
    order = sorted(range(plan.depth // LANES), key=lambda index: (index % blocks, index // blocks))
    turns = chan_len // LANES
    bounds = (9, blocks)

    def column_tile(index):
        scale = jnp.concatenate(
            [
                jnp.broadcast_to(
                    taps_rows[shift_index, :, pl.ds(index * LANES, LANES)][None],
                    (live // 8, 8, LANES),
                ).reshape(live, LANES)
                for shift_index in range(ROWS)
            ],
            axis=0,
        ).astype(jnp.bfloat16)
        turned = rotation[:, index % turns * LANES : (index % turns + 1) * LANES]
        return jnp.concatenate([scale * turned[:half], scale * turned[half:]], axis=0)

    groups = [order[piece : piece + turns] for piece in range(0, len(order), turns)]
    (begin, seen) = (0, 0)
    for bound in bounds:
        end = begin
        while end < len(groups) and max(index % blocks for index in groups[end]) < bound:
            end += 1
        staged = groups[begin:end]
        rights = [
            jnp.concatenate([column_tile(index) for index in group], axis=1) for group in staged
        ]
        for copy in copies[seen:bound]:
            copy.wait()
        for group, right in zip(staged, rights):
            left = jnp.concatenate(
                [pairs[index % blocks, pl.ds(2 * (index // blocks), count), :] for index in group],
                axis=1,
            )
            acc = acc + lax.dot_general(left, right, NT, preferred_element_type=jnp.float32)
        (begin, seen) = (end, bound)
    for tile in range(columns // LANES):
        total[tile] = acc[:, tile * LANES : (tile + 1) * LANES]
    (real_rows, imag_rows) = (
        jnp.concatenate(
            [total[tile, pl.ds(part, plan.out_rows, 2), :] for tile in range(columns // LANES)],
            axis=1,
        )
        for part in range(2)
    )
    lane = lax.broadcasted_iota(jnp.int32, (1, columns), 1)
    sign = jnp.where(lane < half, -1.0, 1.0)
    coarse = (real_rows + sign * pltpu.roll(imag_rows, half, axis=1)).astype(jnp.bfloat16)

    (tm, zoom) = (lax.axis_index("tm"), lax.axis_index("zoom"))
    mine = jnp.int32(0)
    for band in range(plan.bands):
        mine = jnp.where(zoom == band, widths_ref[band], mine)
    width_ref[...] = jnp.broadcast_to(mine, width_ref.shape)
    code = ident * SLOT_LANES + imag * ROWS + shift
    out_lane = lax.broadcasted_iota(jnp.int32, (1, LANES), 1)
    slot = out_lane // SLOT_LANES
    picks = []
    for step in range(plan.devices):
        target = jnp.bitwise_xor(tm * plan.zooms + zoom, step)
        (target_tm, target_zoom) = (target // plan.zooms, target % plan.zooms)
        (band_first, width) = (jnp.int32(0), jnp.int32(0))
        for band in range(plan.bands):
            band_first = jnp.where(target_zoom == band, firsts[band], band_first)
            width = jnp.where(target_zoom == band, widths_ref[band], width)
        base = target_tm * CH_DEV - 1
        position = base + slot
        valid = (position >= 0) & (position < width) & (slot < CH_DEV + 2)
        wanted = jnp.where(valid, (band_first + base) * SLOT_LANES + out_lane, -1)
        pick = (code == wanted).astype(jnp.float32).astype(jnp.bfloat16)
        picks.append(pick)

    chosen = lax.dot_general(
        coarse,
        jnp.concatenate(picks, axis=1),
        (((1,), (0,)), ((), ())),
        preferred_element_type=jnp.float32,
    ).astype(jnp.bfloat16)
    for step in range(plan.devices):
        outs[step][...] = chosen[:, step * LANES : (step + 1) * LANES]


def fine_taps_kernel(plan, taps_ref, after_ref, out_ref):
    lane = lax.broadcasted_iota(jnp.int32, (SLOT_LANES, LANES), 1)
    row = lax.broadcasted_iota(jnp.int32, (SLOT_LANES, LANES), 0)
    keep = lane // ROWS == row
    source = lax.broadcasted_iota(jnp.int32, (2 * LANES, LANES), 0)
    target = lax.broadcasted_iota(jnp.int32, (2 * LANES, LANES), 1)
    spread = (source % ROWS == target % ROWS).astype(jnp.float32).astype(jnp.bfloat16)
    for tap in range(plan.fine_taps):
        (high, low) = ([], [])
        for tile in range(plan.fine_rows // SLOT_LANES):
            line = taps_ref[tap : tap + 1, tile * LANES : (tile + 1) * LANES]
            part = jnp.where(keep, jnp.broadcast_to(line, (SLOT_LANES, LANES)), 0.0)
            rounded = part.astype(jnp.bfloat16)
            high.append(rounded)
            low.append((part - rounded.astype(jnp.float32)).astype(jnp.bfloat16))
        both = jnp.concatenate([jnp.concatenate(high, axis=0), jnp.concatenate(low, axis=0)], axis=1)
        out_ref[pl.ds(PAD + tap * plan.fine_rows, plan.fine_rows), :] = lax.dot_general(
            both, spread, (((1,), (0,)), ((), ())), preferred_element_type=jnp.float32
        )
    out_ref[:PAD] = jnp.zeros((PAD, LANES), jnp.float32)


def add_blocks(plan, steps, taps_ref, blocks, sums):
    here = lax.axis_index("tm") * plan.zooms + lax.axis_index("zoom")
    (fine_rows, out_rows) = (plan.fine_rows, plan.out_rows)
    sums[...] = jnp.zeros_like(sums)
    for step, block in zip(steps, blocks):
        start = jnp.bitwise_xor(here, step) * plan.local_rows + (PAD - plan.lead)
        goal = pl.ds(lax.rem(start + (fine_rows - PAD), fine_rows), out_rows)
        scale = taps_ref[pl.ds(start, out_rows), :]
        sums[goal, :] += scale * block[...].astype(jnp.float32)
    return jnp.concatenate(
        [
            sums[:out_rows] + sums[fine_rows : fine_rows + out_rows],
            sums[out_rows:fine_rows],
        ],
        axis=0,
    )


def merge_kernel(plan, steps, taps_ref, *rest):
    (blocks, (kept_ref, sums)) = (rest[: len(steps)], rest[len(steps) :])
    kept_ref[...] = add_blocks(plan, steps, taps_ref, blocks, sums)


def section_two_kernel(
    plan, steps, width_ref, kept_ref, taps_ref, dft_ref, cos_ref, sin_ref, join_ref, *rest
):
    (blocks, (out_ref, sums)) = (rest[: len(steps)], rest[len(steps) :])
    tm = lax.axis_index("tm")
    (fine_rows, bins) = (plan.fine_rows, plan.bins)
    fine_in = kept_ref[...] + add_blocks(plan, steps, taps_ref, blocks, sums)
    spun = lax.dot_general(
        fine_in.T.astype(jnp.bfloat16),
        dft_ref[...],
        (((1,), (0,)), ((), ())),
        preferred_element_type=jnp.float32,
    )
    (cosine_tab, sine_tab) = (cos_ref[...], sin_ref[...])
    mixed = jnp.concatenate(
        [
            (part * factor).astype(jnp.bfloat16)
            for part in (spun[:, :bins], spun[:, bins:])
            for factor in (cosine_tab, sine_tab)
        ],
        axis=0,
    )
    joined = lax.dot_general(
        join_ref[...], mixed, (((1,), (0,)), ((), ())), preferred_element_type=jnp.float32
    )

    slots = LANES // SLOT_LANES
    high = 2 * slots
    flat = [jnp.zeros((high, LANES), jnp.float32)] * (-(-(ROWS * fine_rows) // LANES) + 2)
    for turn in range(ROWS):
        (first, offset) = divmod(turn * fine_rows, LANES)
        piece = jnp.concatenate(
            [joined[turn * high : (turn + 1) * high], jnp.zeros((high, LANES), jnp.float32)], axis=1
        )
        if offset:
            piece = pltpu.roll(piece, offset, axis=1)
        for tile in range(min(bins // LANES + 1, len(flat) - first)):
            flat[first + tile] = flat[first + tile] + piece[:, tile * LANES : (tile + 1) * LANES]

    row = lax.broadcasted_iota(jnp.int32, (high, LANES), 0)
    lane = lax.broadcasted_iota(jnp.int32, (high, LANES), 1)
    width = width_ref[0:1, :]
    slot = tm * CH_DEV + row % slots - 1
    live = (slot < width).astype(jnp.float32)
    upper_ok = (slot + 1 < width).astype(jnp.float32)
    lower_ok = ((slot >= 1) & (slot < width)).astype(jnp.float32)
    (lead, skew) = divmod(KEEP + EDGE, LANES)
    below = jnp.where(
        lane < LANES - skew,
        pltpu.roll(flat[lead], LANES - skew, axis=1),
        pltpu.roll(flat[lead + 1], LANES - skew, axis=1),
    )
    below = pltpu.roll(below, 1, axis=0)
    (lead, skew) = divmod(KEEP - EDGE, LANES)
    above = pltpu.roll(pltpu.roll(flat[0], skew, axis=1), high - 1, axis=0)
    position = lane.astype(jnp.float32)
    own = flat[1:]
    span = -(-KEEP // LANES)
    parts = []
    for tile in range(span):
        value = own[tile]
        if tile == 0:
            weight = (EDGE - 0.5 - position) * (0.5 / EDGE) * lower_ok
            value = value * (1.0 - weight) + below * weight
        if tile in (lead, lead + 1):
            ramp = (position + (tile * LANES - (KEEP - EDGE) + 0.5)) * (0.5 / EDGE)
            inside = lane >= skew if tile == lead else lane < skew
            weight = jnp.where(inside, ramp * upper_ok, 0.0)
            value = value * (1.0 - weight) + above * weight
        value = value * live
        if tile == span - 1:
            value = jnp.where(lane < KEEP - tile * LANES, value, 0.0)
        parts.append(value)
    parts = [jnp.zeros_like(parts[0])] + parts + [jnp.zeros_like(parts[0])]

    carry = [None, None]
    for place in range(CH_DEV):
        (first, offset) = divmod(place * KEEP, LANES)
        (after, _) = divmod((place + 1) * KEEP, LANES)
        last = place == CH_DEV - 1
        count = after - first + 1
        for part in range(2):
            picked = part * slots + place + 1
            tiles = []
            for tile in range(count):
                value = parts[tile + 1][part * slots : (part + 1) * slots]
                if offset:
                    before = parts[tile][part * slots : (part + 1) * slots]
                    value = jnp.where(
                        lane[:slots] < offset,
                        pltpu.roll(before, offset, axis=1),
                        pltpu.roll(value, offset, axis=1),
                    )
                tiles.append(value[picked % slots : picked % slots + 1])
            if place:
                tiles[0] = tiles[0] + carry[part]
            carry[part] = tiles[-1]
            if not last:
                tiles = tiles[:-1]
            line = jnp.concatenate(tiles, axis=1)
            end = min(first * LANES + len(tiles) * LANES, CH_DEV * KEEP)
            out_ref[part, :, first * LANES : end] = line[:, : end - first * LANES]


def fine_tables(fine_rows):
    fine_len = fine_rows * ROWS
    offset = KEEP // 2 + EDGE
    bins = np.arange(fine_rows) - offset
    spin = 2.0 * np.pi * (np.outer(bins, np.arange(fine_rows)) % fine_rows) / fine_rows
    margin = ((0, -fine_rows % LANES), (0, 0))
    dft = np.concatenate([np.pad(np.cos(spin), margin), np.pad(np.sin(spin), margin)], axis=0)
    twist = 2.0 * np.pi * (np.outer(bins, np.arange(LANES) % ROWS) % fine_len) / fine_len
    join = np.zeros((ROWS, 2, LANES // SLOT_LANES, 4, LANES // SLOT_LANES, 2, ROWS))
    turn = 2.0 * np.pi * (np.outer(np.arange(ROWS), np.arange(ROWS)) % ROWS) / ROWS
    (cosine, sine) = (np.cos(turn), np.sin(turn))
    for slot in range(LANES // SLOT_LANES):
        real, imag = (join[:, 0, slot, :, slot], join[:, 1, slot, :, slot])
        real[:, 0, 0], real[:, 0, 1] = (cosine, sine)
        real[:, 1, 0], real[:, 1, 1] = (-sine, cosine)
        real[:, 2, 0], real[:, 2, 1] = (-sine, cosine)
        real[:, 3, 0], real[:, 3, 1] = (-cosine, -sine)
        imag[:, 0, 0], imag[:, 0, 1] = (-sine, cosine)
        imag[:, 1, 0], imag[:, 1, 1] = (-cosine, -sine)
        imag[:, 2, 0], imag[:, 2, 1] = (-cosine, -sine)
        imag[:, 3, 0], imag[:, 3, 1] = (sine, -cosine)
    return (
        jnp.asarray(dft.T, jnp.bfloat16),
        jnp.asarray(np.pad(np.cos(twist), margin).T, jnp.float32),
        jnp.asarray(np.pad(np.sin(twist), margin).T, jnp.float32),
        jnp.asarray(join.reshape(LANES, 4 * LANES), jnp.bfloat16),
    )


class Plan:
    def __init__(self, mesh, samples, bands, section1_shape, section2_shape):
        (self.tms, self.zooms) = (mesh.shape["tm"], mesh.shape["zoom"])
        self.devices = self.tms * self.zooms
        self.bands = bands
        (self.taps, self.chan_len) = section1_shape
        self.fine_taps = section2_shape[0]
        self.live = LIVE_DEV * self.devices
        self.samples = samples
        self.row_len = ROWS * HOP
        self.blocks = self.row_len // LANES
        self.local_rows = samples // self.row_len
        reach = (ROWS - 1) * HOP + self.taps * self.chan_len
        unit = max(self.chan_len, 2 * LANES)
        self.depth = -(-reach // unit) * unit
        self.lead = -(-self.depth // self.row_len) - 1
        self.out_rows = self.local_rows + self.lead
        self.fine_rows = section2_shape[1] // ROWS
        self.bins = -(-self.fine_rows // LANES) * LANES

    def fits(self, section2_shape):
        return (
            self.row_len % LANES == 0
            and self.samples % self.row_len == 0
            and self.chan_len & (self.chan_len - 1) == 0
            and self.chan_len % LANES == 0
            and self.devices & (self.devices - 1) == 0
            and self.live % 8 == 0
            and (2 * ROWS * self.live) % LANES == 0
            and 2 * ROWS * self.live <= 4 * LANES
            and (CH_DEV + 2) * SLOT_LANES <= LANES
            and self.devices >= 4
            and self.lead <= PAD
            and self.out_rows <= self.fine_rows
            and self.out_rows % 16 == 0
            and self.fine_rows % 16 == 0
            and EDGE == LANES
            and KEEP + 2 * EDGE <= section2_shape[1]
            and section2_shape[1] % ROWS == 0
            and self.devices * self.samples == HOP * self.fine_taps * section2_shape[1]
        )


def direct_plan(plan, voltages, section1_taps, section2_taps, band_starts, band_widths):
    signal = voltages[0].reshape(2, plan.local_rows, plan.blocks, LANES).transpose(1, 2, 0, 3)
    far = [
        pltpu.with_memory_space_constraint(array, pltpu.HBM)
        for array in (band_starts, band_widths, section1_taps, signal)
    ]
    vmem = pl.BlockSpec(memory_space=pltpu.VMEM)
    columns = 2 * ROWS * plan.live
    block = jax.ShapeDtypeStruct((plan.out_rows, LANES), jnp.bfloat16)
    (*sent, width) = pl.pallas_call(
        functools.partial(section_one_kernel, plan),
        out_shape=[block] * plan.devices + [jax.ShapeDtypeStruct((8, LANES), jnp.int32)],
        in_specs=[pl.BlockSpec(memory_space=pltpu.HBM)] * 4,
        out_specs=[vmem] * (plan.devices + 1),
        scratch_shapes=[
            pltpu.VMEM((ROWS, 8, plan.depth), jnp.float32),
            pltpu.VMEM((plan.blocks, plan.local_rows + 2 * plan.lead, 2, LANES), jnp.bfloat16),
            pltpu.VMEM((columns // LANES, 2 * plan.out_rows, LANES), jnp.float32),
            pltpu.SMEM((plan.bands,), jnp.int32),
            pltpu.SMEM((plan.bands,), jnp.int32),
            pltpu.VMEM((plan.taps, plan.chan_len), jnp.float32),
            pltpu.SemaphoreType.DMA((3,)),
            pltpu.SemaphoreType.DMA((plan.blocks,)),
        ],
        compiler_params=pltpu.CompilerParams(vmem_limit_bytes=40 * 2**20),
        name="section_one",
    )(*far)
    order = list(range(plan.devices - 1, 0, -1))
    received = {0: sent[0]}
    for step in order:
        pairs = [(index, index ^ step) for index in range(plan.devices)]
        received[step] = lax.ppermute(sent[step], ("tm", "zoom"), pairs)
    split = len(order) // 2 + 1
    (early, late) = ([0] + order[:split], order[split:])
    fine_rows = plan.fine_rows
    spread = pl.pallas_call(
        functools.partial(fine_taps_kernel, plan),
        out_shape=jax.ShapeDtypeStruct((PAD + plan.fine_taps * fine_rows, LANES), jnp.float32),
        in_specs=[vmem, pl.BlockSpec(memory_space=pl.ANY)],
        out_specs=vmem,
        compiler_params=pltpu.CompilerParams(vmem_limit_bytes=16 * 2**20),
        name="fine_taps",
    )(section2_taps, received[order[1]])
    sums = pltpu.VMEM((fine_rows + plan.out_rows, LANES), jnp.float32)
    kept = pl.pallas_call(
        functools.partial(merge_kernel, plan, early),
        out_shape=jax.ShapeDtypeStruct((fine_rows, LANES), jnp.float32),
        in_specs=[vmem] * (1 + len(early)),
        out_specs=vmem,
        scratch_shapes=[sums],
        compiler_params=pltpu.CompilerParams(vmem_limit_bytes=16 * 2**20),
        name="merge",
    )(spread, *[received[step] for step in early])
    (dft, cosine_tab, sine_tab, join) = fine_tables(fine_rows)
    lines = pl.pallas_call(
        functools.partial(section_two_kernel, plan, late),
        out_shape=jax.ShapeDtypeStruct((2, 1, CH_DEV * KEEP), jnp.float32),
        in_specs=[vmem] * (7 + len(late)),
        out_specs=vmem,
        scratch_shapes=[sums],
        compiler_params=pltpu.CompilerParams(vmem_limit_bytes=24 * 2**20),
        name="section_two",
    )(
        width,
        kept,
        spread,
        dft,
        cosine_tab,
        sine_tab,
        join,
        *[received[step] for step in late],
    )
    return lines.reshape(1, 1, 2, 1, CH_DEV * KEEP)


def solution(mesh):
    placed = (P("pol", "groups", ("tm", "zoom")), P(), P(), P("groups"), P("groups"))

    def on_device(voltages, section1_taps, section2_taps, band_starts, band_widths):
        plan = Plan(
            mesh,
            voltages.shape[2],
            band_widths.shape[0],
            section1_taps.shape,
            section2_taps.shape,
        )
        arrays = (voltages, section1_taps, section2_taps, band_starts, band_widths)
        if plan.fits(section2_taps.shape):
            return direct_plan(plan, *arrays)
        return general_plan(*arrays)

    return jax.shard_map(
        on_device,
        mesh=mesh,
        in_specs=placed,
        out_specs=P("pol", "zoom", "groups", None, "tm"),
        check_vma=False,
    )
```

```python
import functools
import math

import jax
import jax.numpy as jnp
import numpy as np
from jax import lax
from jax.experimental import pallas as pl
from jax.experimental.pallas import tpu as pltpu
from jax.sharding import PartitionSpec as P

HOP = 432
FA = 27
FB = 128
KEEP = 2916
EDGE = 128
CH_DEV = 5
LIVE_DEV = 3


def shifted(value, axis, steps):
    count = lax.axis_size(axis)
    initial, last = (max(0, -steps), min(count, count - steps))
    return lax.ppermute(value, axis, [(source, source + steps) for source in range(initial, last)])


def with_halo(value, sides, width):
    for axis, dim in sides:
        count, length = (lax.axis_size(axis), value.shape[dim])
        up = [(i, (i + 1) % count) for i in range(count - 1)]
        down = [(j, i) for i, j in up]
        last = lax.slice_in_dim(value, length - width, length, axis=dim)
        initial = lax.slice_in_dim(value, 0, width, axis=dim)
        before = lax.ppermute(last, axis, up)
        after = lax.ppermute(initial, axis, down)
        value = jnp.concatenate([before, value, after], axis=dim)
    return value


def angle_table(rows, cols, length):
    product = (
        jnp.arange(rows, dtype=jnp.int32)[:, None]
        * jnp.arange(cols, dtype=jnp.int32)[None, :]
        % length
    )
    return product.astype(jnp.float32) * (2.0 * math.pi / length)


def rotation_block(length):
    angles = angle_table(length, length, length)
    cosine_tab = jnp.cos(angles).astype(jnp.bfloat16)
    sine_tab = jnp.sin(angles).astype(jnp.bfloat16)
    return jnp.stack([jnp.stack([cosine_tab, sine_tab]), jnp.stack([-sine_tab, cosine_tab])])


def joined_table(length):
    angles = angle_table(length, length, length)
    cosine_tab = jnp.cos(angles).astype(jnp.bfloat16)
    sine_tab = jnp.sin(angles).astype(jnp.bfloat16)
    top_rows = jnp.concatenate([cosine_tab, -sine_tab], axis=1)
    bottom_rows = jnp.concatenate([sine_tab, cosine_tab], axis=1)
    return jnp.concatenate([top_rows, bottom_rows], axis=0)


def bin_index(radix_a, radix_b, keep_len, edge_len):
    fine_len = radix_a * radix_b
    offsets = (np.arange(keep_len + 2 * edge_len) - keep_len // 2 - edge_len) % fine_len
    base = offsets % radix_a * (2 * radix_b) + offsets // radix_a
    return (base, base + radix_b)


def frame_view(segment, spectra, chan_len, hop_len):
    pieces = -(-chan_len // hop_len)
    framed = segment[:, : (spectra + pieces - 1) * hop_len].reshape(
        segment.shape[0], spectra + pieces - 1, hop_len
    )
    joined = jnp.concatenate(
        [framed[:, offset : offset + spectra] for offset in range(pieces)], axis=2
    )
    return joined[:, :, :chan_len]


def weighted_frames(signal, taps, spectra, hop_len):
    chan_len = taps.shape[1]
    running = jnp.zeros((2, spectra, chan_len), jnp.float32)
    for tap_index in range(taps.shape[0]):
        frames = frame_view(signal[:, tap_index * chan_len :], spectra, chan_len, hop_len)
        running = running + taps[tap_index][None, None, :] * frames.astype(jnp.float32)
    return running.astype(jnp.bfloat16)


def fine_spectra(series, section2_taps, radix_a, radix_b, keep_len, edge_len):
    tap_count, fine_len = section2_taps.shape
    items = series.shape[1]
    row_count = series.shape[2] // fine_len
    spectra = row_count - tap_count + 1
    row_blocks = series.reshape(2, items, row_count, fine_len)
    running = jnp.zeros((2, items, spectra, fine_len), jnp.float32)
    for tap_index in range(tap_count):
        running = running + section2_taps[tap_index] * row_blocks[
            :, :, tap_index : tap_index + spectra
        ].astype(jnp.float32)
    weighted = running.astype(jnp.bfloat16).reshape(2, items, spectra, radix_a, radix_b)
    partial_value = jnp.einsum(
        "pqkm,qcfmb->pcfkb", rotation_block(radix_a), weighted, preferred_element_type=jnp.float32
    )
    angles = angle_table(radix_a, radix_b, fine_len)
    cosine_tab = jnp.cos(angles)
    sine_tab = jnp.sin(angles)
    real_part = partial_value[0] * cosine_tab + partial_value[1] * sine_tab
    imag_part = partial_value[1] * cosine_tab - partial_value[0] * sine_tab
    twiddled = jnp.concatenate([real_part, imag_part], axis=-1).astype(jnp.bfloat16)
    spectrum = jnp.einsum(
        "cfkm,mj->cfkj", twiddled, joined_table(radix_b), preferred_element_type=jnp.float32
    )
    flattened = spectrum.reshape(items, spectra, radix_a * 2 * radix_b)
    real_index, imag_index = bin_index(radix_a, radix_b, keep_len, edge_len)
    return jnp.stack(
        [jnp.take(flattened, real_index, axis=2), jnp.take(flattened, imag_index, axis=2)]
    )


def stitch_bands(extended, upper_rim, lower_rim, slot_ids, band_width, keep_len, edge_len):
    centre = extended[..., edge_len : edge_len + keep_len]
    live = (slot_ids < band_width).astype(jnp.float32)[None, :, None, None]
    upper_ok = (slot_ids + 1 < band_width).astype(jnp.float32)[None, :, None, None]
    lower_ok = ((slot_ids >= 1) & (slot_ids < band_width)).astype(jnp.float32)[None, :, None, None]
    ramp = (jnp.arange(edge_len, dtype=jnp.float32) + 0.5) / (2.0 * edge_len)
    upper_weight = ramp * upper_ok
    lower_weight = ramp[::-1] * lower_ok
    low_part = centre[..., :edge_len] * (1.0 - lower_weight) + lower_rim * lower_weight
    high_part = centre[..., keep_len - edge_len :] * (1.0 - upper_weight) + upper_rim * upper_weight
    joined = jnp.concatenate(
        [low_part, centre[..., edge_len : keep_len - edge_len], high_part], axis=-1
    )
    return joined * live


def general_plan(voltages, section1_taps, section2_taps, band_starts, band_widths):
    signal = voltages[0]
    tap_count, chan_len = section1_taps.shape
    spectra = signal.shape[1] // HOP
    rim_len = tap_count * chan_len - HOP
    pieces = -(-chan_len // HOP)
    following = shifted(signal[:, :rim_len], ("tm", "zoom"), -1)
    padded = jnp.concatenate(
        [signal, following, jnp.zeros((2, pieces * HOP), jnp.bfloat16)], axis=1
    )
    weighted = weighted_frames(padded, section1_taps, spectra, HOP)
    coarse = jnp.einsum(
        "pqkn,qsn->pks", rotation_block(chan_len), weighted, preferred_element_type=jnp.float32
    ).astype(jnp.bfloat16)
    tm_count = lax.axis_size("tm")
    zoom_count = lax.axis_size("zoom")
    slot_local = jnp.arange(CH_DEV, dtype=jnp.int32)
    slot_ids = lax.axis_index("tm") * CH_DEV + slot_local
    band_count = band_widths.shape[0]
    band_ids = jnp.arange(band_count, dtype=jnp.int32)
    my_band = band_ids == lax.axis_index("zoom")
    band_width = jnp.sum(jnp.where(my_band, band_widths, 0))
    device_count = tm_count * zoom_count
    live_count = LIVE_DEV * device_count
    band_ends = jnp.cumsum(band_widths)
    band_firsts = band_ends - band_widths
    live_ids = jnp.arange(live_count, dtype=jnp.int32)
    band_of = jnp.sum((band_ends[None, :] <= live_ids[:, None]).astype(jnp.int32), axis=1)
    member = band_of[:, None] == band_ids[None, :]
    first_of = jnp.sum(jnp.where(member, band_firsts[None, :], 0), axis=1)
    start_of = jnp.sum(jnp.where(member, band_starts[None, :], 0), axis=1)
    live_channels = (start_of + live_ids - first_of) % chan_len
    packed_order = live_channels.reshape(device_count, LIVE_DEV).T.reshape(-1)
    packed = jnp.take(coarse, packed_order, axis=1).reshape(2, LIVE_DEV, device_count, spectra)
    received = lax.all_to_all(packed, ("tm", "zoom"), split_axis=2, concat_axis=2, tiled=True)
    series = received.reshape(2, received.shape[1], -1)
    computed = fine_spectra(series, section2_taps, FA, FB, KEEP, EDGE)
    wanted = jnp.sum(jnp.where(my_band, band_firsts, 0)) + slot_ids
    valid = slot_ids < band_width
    piece = lax.all_gather(computed, ("tm", "zoom"), axis=1, tiled=True)
    piece_ids = jnp.arange(piece.shape[1], dtype=jnp.int32)
    chosen = ((wanted[:, None] == piece_ids[None, :]) & valid[:, None]).astype(jnp.float32)
    extended = jnp.einsum("kn,pnfx->pkfx", chosen, piece, precision=lax.Precision.HIGHEST)
    seam_rows = jnp.concatenate([extended[..., :EDGE], extended[..., KEEP + EDGE :]], axis=-1)
    widened = with_halo(seam_rows, (("tm", 1),), 1)
    upper_rim = widened[:, 2:, :, :EDGE]
    lower_rim = widened[:, :CH_DEV, :, EDGE:]
    stitched = stitch_bands(extended, upper_rim, lower_rim, slot_ids, band_width, KEEP, EDGE)
    fine_count = stitched.shape[2]
    result = jnp.transpose(stitched, (0, 2, 1, 3)).reshape(2, fine_count, CH_DEV * KEEP)
    return result[None, None]


ROWS = 8
LANES = 128
SLOT_LANES = 2 * ROWS
PAD = 8
NT = (((1,), (1,)), ((), ()))


def sine_quarter(value):
    square = value * value
    total = -3.5988432e-06
    for factor in (1.604411848e-04, -4.6817541353e-03, 7.96926262462e-02, -6.459640975062e-01):
        total = total * square + factor
    return (total * square + 1.5707963267949) * value


def section_one_kernel(plan, starts_hbm, widths_hbm, taps_hbm, signal_ref, *rest):
    (outs, (width_ref, taps_rows, frames, total, *rest)) = (
        rest[: plan.devices],
        rest[plan.devices :],
    )
    (starts_ref, widths_ref, taps_ref, small_sems, sems) = rest
    small = [
        pltpu.make_async_copy(source, target, small_sems.at[index])
        for index, (source, target) in enumerate(
            [(starts_hbm, starts_ref), (widths_hbm, widths_ref), (taps_hbm, taps_ref)]
        )
    ]
    for copy in small:
        copy.start()
    blocks, chan_len, live = (plan.blocks, plan.chan_len, plan.live)
    half = ROWS * live
    columns = 2 * half
    lead = plan.lead
    copies = [
        pltpu.make_async_copy(
            signal_ref.at[:, block], frames.at[block, pl.ds(lead, plan.local_rows)], sems.at[block]
        )
        for block in range(blocks)
    ]
    for copy in copies:
        copy.start(priority=1)
    edge = jnp.zeros((blocks, lead, 2, LANES), jnp.bfloat16)
    frames[:, :lead] = edge
    frames[:, lead + plan.local_rows :] = edge

    for copy in small:
        copy.wait()
    row = lax.broadcasted_iota(jnp.int32, (columns, 1), 0)
    imag = (row >= half).astype(jnp.int32)
    shift = (row - imag * half) // live
    ident = row - imag * half - shift * live
    channel = jnp.zeros((columns, 1), jnp.int32)
    first = jnp.int32(0)
    firsts = []
    for band in range(plan.bands):
        inside = (ident >= first) & (ident < first + widths_ref[band])
        channel = jnp.where(inside, starts_ref[band] + ident - first, channel)
        firsts.append(first)
        first = first + widths_ref[band]
    phase = lax.broadcasted_iota(jnp.int32, (columns, LANES), 1) - HOP * shift
    quarter = chan_len // 4
    turn = (channel * phase + imag * quarter) & (chan_len - 1)
    folded = jnp.abs(turn - 2 * quarter)
    angle = (folded - quarter).astype(jnp.float32) * (1.0 / quarter)
    first_lanes = sine_quarter(angle)
    ahead = jnp.concatenate([first_lanes[half:], -first_lanes[:half]], axis=0)
    tiles = [first_lanes]
    for tile in range(1, 4):
        quarters = (channel * tile) & 3
        same = (quarters == 0).astype(jnp.float32) - (quarters == 2).astype(jnp.float32)
        next_one = (quarters == 1).astype(jnp.float32) - (quarters == 3).astype(jnp.float32)
        tiles.append(same * first_lanes + next_one * ahead)
    rotation = jnp.concatenate(tiles, axis=1).astype(jnp.bfloat16)

    filled = plan.taps * chan_len + LANES
    flat = jnp.concatenate(
        [jnp.broadcast_to(taps_ref[tap : tap + 1, :], (8, chan_len)) for tap in range(plan.taps)]
        + [jnp.zeros((8, LANES), jnp.float32)],
        axis=1,
    )
    for shift_index in range(ROWS):
        (skipped, offset) = divmod(HOP * shift_index, LANES)
        moved = pltpu.roll(flat, offset, axis=1) if offset else flat
        first = skipped * LANES
        end = min(first + filled, plan.depth)
        if first:
            taps_rows[shift_index, :, :first] = jnp.zeros((8, first), jnp.float32)
        taps_rows[shift_index, :, first:end] = moved[:, : end - first]
        if end < plan.depth:
            taps_rows[shift_index, :, end:] = jnp.zeros((8, plan.depth - end), jnp.float32)
    count = 2 * plan.out_rows
    pairs = frames.reshape(blocks, 2 * (plan.local_rows + 2 * lead), LANES)
    acc = jnp.zeros((count, columns), jnp.float32)
    order = sorted(range(plan.depth // LANES), key=lambda index: (index % blocks, index // blocks))
    turns = chan_len // LANES
    bounds = (9, blocks)

    def column_tile(index):
        scale = jnp.concatenate(
            [
                jnp.broadcast_to(
                    taps_rows[shift_index, :, pl.ds(index * LANES, LANES)][None],
                    (live // 8, 8, LANES),
                ).reshape(live, LANES)
                for shift_index in range(ROWS)
            ],
            axis=0,
        ).astype(jnp.bfloat16)
        turned = rotation[:, index % turns * LANES : (index % turns + 1) * LANES]
        return jnp.concatenate([scale * turned[:half], scale * turned[half:]], axis=0)

    groups = [order[piece : piece + turns] for piece in range(0, len(order), turns)]
    (begin, seen) = (0, 0)
    for bound in bounds:
        end = begin
        while end < len(groups) and max(index % blocks for index in groups[end]) < bound:
            end += 1
        staged = groups[begin:end]
        rights = [
            jnp.concatenate([column_tile(index) for index in group], axis=1) for group in staged
        ]
        for copy in copies[seen:bound]:
            copy.wait()
        for group, right in zip(staged, rights):
            left = jnp.concatenate(
                [pairs[index % blocks, pl.ds(2 * (index // blocks), count), :] for index in group],
                axis=1,
            )
            acc = acc + lax.dot_general(left, right, NT, preferred_element_type=jnp.float32)
        (begin, seen) = (end, bound)
    for tile in range(columns // LANES):
        total[tile] = acc[:, tile * LANES : (tile + 1) * LANES]
    (real_rows, imag_rows) = (
        jnp.concatenate(
            [total[tile, pl.ds(part, plan.out_rows, 2), :] for tile in range(columns // LANES)],
            axis=1,
        )
        for part in range(2)
    )
    lane = lax.broadcasted_iota(jnp.int32, (1, columns), 1)
    sign = jnp.where(lane < half, -1.0, 1.0)
    coarse = (real_rows + sign * pltpu.roll(imag_rows, half, axis=1)).astype(jnp.bfloat16)

    (tm, zoom) = (lax.axis_index("tm"), lax.axis_index("zoom"))
    mine = jnp.int32(0)
    for band in range(plan.bands):
        mine = jnp.where(zoom == band, widths_ref[band], mine)
    width_ref[...] = jnp.broadcast_to(mine, width_ref.shape)
    code = ident * SLOT_LANES + imag * ROWS + shift
    out_lane = lax.broadcasted_iota(jnp.int32, (1, LANES), 1)
    slot = out_lane // SLOT_LANES
    picks = []
    for step in range(plan.devices):
        target = jnp.bitwise_xor(tm * plan.zooms + zoom, step)
        (target_tm, target_zoom) = (target // plan.zooms, target % plan.zooms)
        (band_first, width) = (jnp.int32(0), jnp.int32(0))
        for band in range(plan.bands):
            band_first = jnp.where(target_zoom == band, firsts[band], band_first)
            width = jnp.where(target_zoom == band, widths_ref[band], width)
        base = target_tm * CH_DEV - 1
        position = base + slot
        valid = (position >= 0) & (position < width) & (slot < CH_DEV + 2)
        wanted = jnp.where(valid, (band_first + base) * SLOT_LANES + out_lane, -1)
        pick = (code == wanted).astype(jnp.float32).astype(jnp.bfloat16)
        picks.append(pick)

    chosen = lax.dot_general(
        coarse,
        jnp.concatenate(picks, axis=1),
        (((1,), (0,)), ((), ())),
        preferred_element_type=jnp.float32,
    ).astype(jnp.bfloat16)
    for step in range(plan.devices):
        outs[step][...] = chosen[:, step * LANES : (step + 1) * LANES]


def fine_taps_kernel(plan, taps_ref, after_ref, out_ref):
    lane = lax.broadcasted_iota(jnp.int32, (SLOT_LANES, LANES), 1)
    row = lax.broadcasted_iota(jnp.int32, (SLOT_LANES, LANES), 0)
    keep = lane // ROWS == row
    source = lax.broadcasted_iota(jnp.int32, (2 * LANES, LANES), 0)
    target = lax.broadcasted_iota(jnp.int32, (2 * LANES, LANES), 1)
    spread = (source % ROWS == target % ROWS).astype(jnp.float32).astype(jnp.bfloat16)
    for tap in range(plan.fine_taps):
        (high, low) = ([], [])
        for tile in range(plan.fine_rows // SLOT_LANES):
            line = taps_ref[tap : tap + 1, tile * LANES : (tile + 1) * LANES]
            part = jnp.where(keep, jnp.broadcast_to(line, (SLOT_LANES, LANES)), 0.0)
            rounded = part.astype(jnp.bfloat16)
            high.append(rounded)
            low.append((part - rounded.astype(jnp.float32)).astype(jnp.bfloat16))
        both = jnp.concatenate([jnp.concatenate(high, axis=0), jnp.concatenate(low, axis=0)], axis=1)
        out_ref[pl.ds(PAD + tap * plan.fine_rows, plan.fine_rows), :] = lax.dot_general(
            both, spread, (((1,), (0,)), ((), ())), preferred_element_type=jnp.float32
        )
    out_ref[:PAD] = jnp.zeros((PAD, LANES), jnp.float32)


def add_blocks(plan, steps, taps_ref, blocks, sums):
    here = lax.axis_index("tm") * plan.zooms + lax.axis_index("zoom")
    (fine_rows, out_rows) = (plan.fine_rows, plan.out_rows)
    sums[...] = jnp.zeros_like(sums)
    for step, block in zip(steps, blocks):
        start = jnp.bitwise_xor(here, step) * plan.local_rows + (PAD - plan.lead)
        goal = pl.ds(lax.rem(start + (fine_rows - PAD), fine_rows), out_rows)
        scale = taps_ref[pl.ds(start, out_rows), :]
        sums[goal, :] += scale * block[...].astype(jnp.float32)
    return jnp.concatenate(
        [
            sums[:out_rows] + sums[fine_rows : fine_rows + out_rows],
            sums[out_rows:fine_rows],
        ],
        axis=0,
    )


def merge_kernel(plan, steps, taps_ref, *rest):
    (blocks, (kept_ref, sums)) = (rest[: len(steps)], rest[len(steps) :])
    kept_ref[...] = add_blocks(plan, steps, taps_ref, blocks, sums)


def section_two_kernel(
    plan, steps, width_ref, kept_ref, taps_ref, dft_ref, cos_ref, sin_ref, join_ref, *rest
):
    (blocks, (out_ref, sums)) = (rest[: len(steps)], rest[len(steps) :])
    tm = lax.axis_index("tm")
    (fine_rows, bins) = (plan.fine_rows, plan.bins)
    fine_in = kept_ref[...] + add_blocks(plan, steps, taps_ref, blocks, sums)
    spun = lax.dot_general(
        fine_in.T.astype(jnp.bfloat16),
        dft_ref[...],
        (((1,), (0,)), ((), ())),
        preferred_element_type=jnp.float32,
    )
    (cosine_tab, sine_tab) = (cos_ref[...], sin_ref[...])
    mixed = jnp.concatenate(
        [
            (part * factor).astype(jnp.bfloat16)
            for part in (spun[:, :bins], spun[:, bins:])
            for factor in (cosine_tab, sine_tab)
        ],
        axis=0,
    )
    joined = lax.dot_general(
        join_ref[...], mixed, (((1,), (0,)), ((), ())), preferred_element_type=jnp.float32
    )

    slots = LANES // SLOT_LANES
    high = 2 * slots
    flat = [jnp.zeros((high, LANES), jnp.float32)] * (-(-(ROWS * fine_rows) // LANES) + 2)
    for turn in range(ROWS):
        (first, offset) = divmod(turn * fine_rows, LANES)
        piece = jnp.concatenate(
            [joined[turn * high : (turn + 1) * high], jnp.zeros((high, LANES), jnp.float32)], axis=1
        )
        if offset:
            piece = pltpu.roll(piece, offset, axis=1)
        for tile in range(min(bins // LANES + 1, len(flat) - first)):
            flat[first + tile] = flat[first + tile] + piece[:, tile * LANES : (tile + 1) * LANES]

    row = lax.broadcasted_iota(jnp.int32, (high, LANES), 0)
    lane = lax.broadcasted_iota(jnp.int32, (high, LANES), 1)
    width = width_ref[0:1, :]
    slot = tm * CH_DEV + row % slots - 1
    live = (slot < width).astype(jnp.float32)
    upper_ok = (slot + 1 < width).astype(jnp.float32)
    lower_ok = ((slot >= 1) & (slot < width)).astype(jnp.float32)
    (lead, skew) = divmod(KEEP + EDGE, LANES)
    below = jnp.where(
        lane < LANES - skew,
        pltpu.roll(flat[lead], LANES - skew, axis=1),
        pltpu.roll(flat[lead + 1], LANES - skew, axis=1),
    )
    below = pltpu.roll(below, 1, axis=0)
    (lead, skew) = divmod(KEEP - EDGE, LANES)
    above = pltpu.roll(pltpu.roll(flat[0], skew, axis=1), high - 1, axis=0)
    position = lane.astype(jnp.float32)
    own = flat[1:]
    span = -(-KEEP // LANES)
    parts = []
    for tile in range(span):
        value = own[tile]
        if tile == 0:
            weight = (EDGE - 0.5 - position) * (0.5 / EDGE) * lower_ok
            value = value * (1.0 - weight) + below * weight
        if tile in (lead, lead + 1):
            ramp = (position + (tile * LANES - (KEEP - EDGE) + 0.5)) * (0.5 / EDGE)
            inside = lane >= skew if tile == lead else lane < skew
            weight = jnp.where(inside, ramp * upper_ok, 0.0)
            value = value * (1.0 - weight) + above * weight
        value = value * live
        if tile == span - 1:
            value = jnp.where(lane < KEEP - tile * LANES, value, 0.0)
        parts.append(value)
    parts = [jnp.zeros_like(parts[0])] + parts + [jnp.zeros_like(parts[0])]

    carry = [None, None]
    for place in range(CH_DEV):
        (first, offset) = divmod(place * KEEP, LANES)
        (after, _) = divmod((place + 1) * KEEP, LANES)
        last = place == CH_DEV - 1
        count = after - first + 1
        for part in range(2):
            picked = part * slots + place + 1
            tiles = []
            for tile in range(count):
                value = parts[tile + 1][part * slots : (part + 1) * slots]
                if offset:
                    before = parts[tile][part * slots : (part + 1) * slots]
                    value = jnp.where(
                        lane[:slots] < offset,
                        pltpu.roll(before, offset, axis=1),
                        pltpu.roll(value, offset, axis=1),
                    )
                tiles.append(value[picked % slots : picked % slots + 1])
            if place:
                tiles[0] = tiles[0] + carry[part]
            carry[part] = tiles[-1]
            if not last:
                tiles = tiles[:-1]
            line = jnp.concatenate(tiles, axis=1)
            end = min(first * LANES + len(tiles) * LANES, CH_DEV * KEEP)
            out_ref[part, :, first * LANES : end] = line[:, : end - first * LANES]


def fine_tables(fine_rows):
    fine_len = fine_rows * ROWS
    offset = KEEP // 2 + EDGE
    bins = np.arange(fine_rows) - offset
    spin = 2.0 * np.pi * (np.outer(bins, np.arange(fine_rows)) % fine_rows) / fine_rows
    margin = ((0, -fine_rows % LANES), (0, 0))
    dft = np.concatenate([np.pad(np.cos(spin), margin), np.pad(np.sin(spin), margin)], axis=0)
    twist = 2.0 * np.pi * (np.outer(bins, np.arange(LANES) % ROWS) % fine_len) / fine_len
    join = np.zeros((ROWS, 2, LANES // SLOT_LANES, 4, LANES // SLOT_LANES, 2, ROWS))
    turn = 2.0 * np.pi * (np.outer(np.arange(ROWS), np.arange(ROWS)) % ROWS) / ROWS
    (cosine, sine) = (np.cos(turn), np.sin(turn))
    for slot in range(LANES // SLOT_LANES):
        real, imag = (join[:, 0, slot, :, slot], join[:, 1, slot, :, slot])
        real[:, 0, 0], real[:, 0, 1] = (cosine, sine)
        real[:, 1, 0], real[:, 1, 1] = (-sine, cosine)
        real[:, 2, 0], real[:, 2, 1] = (-sine, cosine)
        real[:, 3, 0], real[:, 3, 1] = (-cosine, -sine)
        imag[:, 0, 0], imag[:, 0, 1] = (-sine, cosine)
        imag[:, 1, 0], imag[:, 1, 1] = (-cosine, -sine)
        imag[:, 2, 0], imag[:, 2, 1] = (-cosine, -sine)
        imag[:, 3, 0], imag[:, 3, 1] = (sine, -cosine)
    return (
        jnp.asarray(dft.T, jnp.bfloat16),
        jnp.asarray(np.pad(np.cos(twist), margin).T, jnp.float32),
        jnp.asarray(np.pad(np.sin(twist), margin).T, jnp.float32),
        jnp.asarray(join.reshape(LANES, 4 * LANES), jnp.bfloat16),
    )


class Plan:
    def __init__(self, mesh, samples, bands, section1_shape, section2_shape):
        (self.tms, self.zooms) = (mesh.shape["tm"], mesh.shape["zoom"])
        self.devices = self.tms * self.zooms
        self.bands = bands
        (self.taps, self.chan_len) = section1_shape
        self.fine_taps = section2_shape[0]
        self.live = LIVE_DEV * self.devices
        self.samples = samples
        self.row_len = ROWS * HOP
        self.blocks = self.row_len // LANES
        self.local_rows = samples // self.row_len
        reach = (ROWS - 1) * HOP + self.taps * self.chan_len
        unit = max(self.chan_len, 2 * LANES)
        self.depth = -(-reach // unit) * unit
        self.lead = -(-self.depth // self.row_len) - 1
        self.out_rows = self.local_rows + self.lead
        self.fine_rows = section2_shape[1] // ROWS
        self.bins = -(-self.fine_rows // LANES) * LANES

    def fits(self, section2_shape):
        return (
            self.row_len % LANES == 0
            and self.samples % self.row_len == 0
            and self.chan_len & (self.chan_len - 1) == 0
            and self.chan_len == 4 * LANES
            and self.devices & (self.devices - 1) == 0
            and self.live % 8 == 0
            and (2 * ROWS * self.live) % LANES == 0
            and 2 * ROWS * self.live <= 4 * LANES
            and (CH_DEV + 2) * SLOT_LANES <= LANES
            and self.devices >= 4
            and self.lead <= PAD
            and self.out_rows <= self.fine_rows
            and self.out_rows % 16 == 0
            and self.fine_rows % 16 == 0
            and EDGE == LANES
            and KEEP + 2 * EDGE <= section2_shape[1]
            and section2_shape[1] % ROWS == 0
            and self.devices * self.samples == HOP * self.fine_taps * section2_shape[1]
        )


def direct_plan(plan, voltages, section1_taps, section2_taps, band_starts, band_widths):
    signal = voltages[0].reshape(2, plan.local_rows, plan.blocks, LANES).transpose(1, 2, 0, 3)
    far = [
        pltpu.with_memory_space_constraint(array, pltpu.HBM)
        for array in (band_starts, band_widths, section1_taps, signal)
    ]
    vmem = pl.BlockSpec(memory_space=pltpu.VMEM)
    columns = 2 * ROWS * plan.live
    block = jax.ShapeDtypeStruct((plan.out_rows, LANES), jnp.bfloat16)
    (*sent, width) = pl.pallas_call(
        functools.partial(section_one_kernel, plan),
        out_shape=[block] * plan.devices + [jax.ShapeDtypeStruct((8, LANES), jnp.int32)],
        in_specs=[pl.BlockSpec(memory_space=pltpu.HBM)] * 4,
        out_specs=[vmem] * (plan.devices + 1),
        scratch_shapes=[
            pltpu.VMEM((ROWS, 8, plan.depth), jnp.float32),
            pltpu.VMEM((plan.blocks, plan.local_rows + 2 * plan.lead, 2, LANES), jnp.bfloat16),
            pltpu.VMEM((columns // LANES, 2 * plan.out_rows, LANES), jnp.float32),
            pltpu.SMEM((plan.bands,), jnp.int32),
            pltpu.SMEM((plan.bands,), jnp.int32),
            pltpu.VMEM((plan.taps, plan.chan_len), jnp.float32),
            pltpu.SemaphoreType.DMA((3,)),
            pltpu.SemaphoreType.DMA((plan.blocks,)),
        ],
        compiler_params=pltpu.CompilerParams(vmem_limit_bytes=40 * 2**20),
        name="section_one",
    )(*far)
    order = list(range(plan.devices - 1, 0, -1))
    received = {0: sent[0]}
    for step in order:
        pairs = [(index, index ^ step) for index in range(plan.devices)]
        received[step] = lax.ppermute(sent[step], ("tm", "zoom"), pairs)
    split = len(order) // 2 + 1
    (early, late) = ([0] + order[:split], order[split:])
    fine_rows = plan.fine_rows
    spread = pl.pallas_call(
        functools.partial(fine_taps_kernel, plan),
        out_shape=jax.ShapeDtypeStruct((PAD + plan.fine_taps * fine_rows, LANES), jnp.float32),
        in_specs=[vmem, pl.BlockSpec(memory_space=pl.ANY)],
        out_specs=vmem,
        compiler_params=pltpu.CompilerParams(vmem_limit_bytes=16 * 2**20),
        name="fine_taps",
    )(section2_taps, received[order[1]])
    sums = pltpu.VMEM((fine_rows + plan.out_rows, LANES), jnp.float32)
    kept = pl.pallas_call(
        functools.partial(merge_kernel, plan, early),
        out_shape=jax.ShapeDtypeStruct((fine_rows, LANES), jnp.float32),
        in_specs=[vmem] * (1 + len(early)),
        out_specs=vmem,
        scratch_shapes=[sums],
        compiler_params=pltpu.CompilerParams(vmem_limit_bytes=16 * 2**20),
        name="merge",
    )(spread, *[received[step] for step in early])
    (dft, cosine_tab, sine_tab, join) = fine_tables(fine_rows)
    lines = pl.pallas_call(
        functools.partial(section_two_kernel, plan, late),
        out_shape=jax.ShapeDtypeStruct((2, 1, CH_DEV * KEEP), jnp.float32),
        in_specs=[vmem] * (7 + len(late)),
        out_specs=vmem,
        scratch_shapes=[sums],
        compiler_params=pltpu.CompilerParams(vmem_limit_bytes=24 * 2**20),
        name="section_two",
    )(
        width,
        kept,
        spread,
        dft,
        cosine_tab,
        sine_tab,
        join,
        *[received[step] for step in late],
    )
    return lines.reshape(1, 1, 2, 1, CH_DEV * KEEP)


def solution(mesh):
    placed = (P("pol", "groups", ("tm", "zoom")), P(), P(), P("groups"), P("groups"))

    def on_device(voltages, section1_taps, section2_taps, band_starts, band_widths):
        plan = Plan(
            mesh,
            voltages.shape[2],
            band_widths.shape[0],
            section1_taps.shape,
            section2_taps.shape,
        )
        arrays = (voltages, section1_taps, section2_taps, band_starts, band_widths)
        if plan.fits(section2_taps.shape):
            return direct_plan(plan, *arrays)
        return general_plan(*arrays)

    return jax.shard_map(
        on_device,
        mesh=mesh,
        in_specs=placed,
        out_specs=P("pol", "zoom", "groups", None, "tm"),
        check_vma=False,
    )
```

```python
import functools
import math

import jax
import jax.numpy as jnp
import numpy as np
from jax import lax
from jax.experimental import pallas as pl
from jax.experimental.pallas import tpu as pltpu
from jax.sharding import PartitionSpec as P

HOP = 432
FA = 27
FB = 128
KEEP = 2916
EDGE = 128
CH_DEV = 5
LIVE_DEV = 3


def shifted(value, axis, steps):
    count = lax.axis_size(axis)
    initial, last = (max(0, -steps), min(count, count - steps))
    return lax.ppermute(value, axis, [(source, source + steps) for source in range(initial, last)])


def with_halo(value, sides, width):
    for axis, dim in sides:
        count, length = (lax.axis_size(axis), value.shape[dim])
        up = [(i, (i + 1) % count) for i in range(count - 1)]
        down = [(j, i) for i, j in up]
        last = lax.slice_in_dim(value, length - width, length, axis=dim)
        initial = lax.slice_in_dim(value, 0, width, axis=dim)
        before = lax.ppermute(last, axis, up)
        after = lax.ppermute(initial, axis, down)
        value = jnp.concatenate([before, value, after], axis=dim)
    return value


def angle_table(rows, cols, length):
    product = (
        jnp.arange(rows, dtype=jnp.int32)[:, None]
        * jnp.arange(cols, dtype=jnp.int32)[None, :]
        % length
    )
    return product.astype(jnp.float32) * (2.0 * math.pi / length)


def rotation_block(length):
    angles = angle_table(length, length, length)
    cosine_tab = jnp.cos(angles).astype(jnp.bfloat16)
    sine_tab = jnp.sin(angles).astype(jnp.bfloat16)
    return jnp.stack([jnp.stack([cosine_tab, sine_tab]), jnp.stack([-sine_tab, cosine_tab])])


def joined_table(length):
    angles = angle_table(length, length, length)
    cosine_tab = jnp.cos(angles).astype(jnp.bfloat16)
    sine_tab = jnp.sin(angles).astype(jnp.bfloat16)
    top_rows = jnp.concatenate([cosine_tab, -sine_tab], axis=1)
    bottom_rows = jnp.concatenate([sine_tab, cosine_tab], axis=1)
    return jnp.concatenate([top_rows, bottom_rows], axis=0)


def bin_index(radix_a, radix_b, keep_len, edge_len):
    fine_len = radix_a * radix_b
    offsets = (np.arange(keep_len + 2 * edge_len) - keep_len // 2 - edge_len) % fine_len
    base = offsets % radix_a * (2 * radix_b) + offsets // radix_a
    return (base, base + radix_b)


def frame_view(segment, spectra, chan_len, hop_len):
    pieces = -(-chan_len // hop_len)
    framed = segment[:, : (spectra + pieces - 1) * hop_len].reshape(
        segment.shape[0], spectra + pieces - 1, hop_len
    )
    joined = jnp.concatenate(
        [framed[:, offset : offset + spectra] for offset in range(pieces)], axis=2
    )
    return joined[:, :, :chan_len]


def weighted_frames(signal, taps, spectra, hop_len):
    chan_len = taps.shape[1]
    running = jnp.zeros((2, spectra, chan_len), jnp.float32)
    for tap_index in range(taps.shape[0]):
        frames = frame_view(signal[:, tap_index * chan_len :], spectra, chan_len, hop_len)
        running = running + taps[tap_index][None, None, :] * frames.astype(jnp.float32)
    return running.astype(jnp.bfloat16)


def fine_spectra(series, section2_taps, radix_a, radix_b, keep_len, edge_len):
    tap_count, fine_len = section2_taps.shape
    items = series.shape[1]
    row_count = series.shape[2] // fine_len
    spectra = row_count - tap_count + 1
    row_blocks = series.reshape(2, items, row_count, fine_len)
    running = jnp.zeros((2, items, spectra, fine_len), jnp.float32)
    for tap_index in range(tap_count):
        running = running + section2_taps[tap_index] * row_blocks[
            :, :, tap_index : tap_index + spectra
        ].astype(jnp.float32)
    weighted = running.astype(jnp.bfloat16).reshape(2, items, spectra, radix_a, radix_b)
    partial_value = jnp.einsum(
        "pqkm,qcfmb->pcfkb", rotation_block(radix_a), weighted, preferred_element_type=jnp.float32
    )
    angles = angle_table(radix_a, radix_b, fine_len)
    cosine_tab = jnp.cos(angles)
    sine_tab = jnp.sin(angles)
    real_part = partial_value[0] * cosine_tab + partial_value[1] * sine_tab
    imag_part = partial_value[1] * cosine_tab - partial_value[0] * sine_tab
    twiddled = jnp.concatenate([real_part, imag_part], axis=-1).astype(jnp.bfloat16)
    spectrum = jnp.einsum(
        "cfkm,mj->cfkj", twiddled, joined_table(radix_b), preferred_element_type=jnp.float32
    )
    flattened = spectrum.reshape(items, spectra, radix_a * 2 * radix_b)
    real_index, imag_index = bin_index(radix_a, radix_b, keep_len, edge_len)
    return jnp.stack(
        [jnp.take(flattened, real_index, axis=2), jnp.take(flattened, imag_index, axis=2)]
    )


def stitch_bands(extended, upper_rim, lower_rim, slot_ids, band_width, keep_len, edge_len):
    centre = extended[..., edge_len : edge_len + keep_len]
    live = (slot_ids < band_width).astype(jnp.float32)[None, :, None, None]
    upper_ok = (slot_ids + 1 < band_width).astype(jnp.float32)[None, :, None, None]
    lower_ok = ((slot_ids >= 1) & (slot_ids < band_width)).astype(jnp.float32)[None, :, None, None]
    ramp = (jnp.arange(edge_len, dtype=jnp.float32) + 0.5) / (2.0 * edge_len)
    upper_weight = ramp * upper_ok
    lower_weight = ramp[::-1] * lower_ok
    low_part = centre[..., :edge_len] * (1.0 - lower_weight) + lower_rim * lower_weight
    high_part = centre[..., keep_len - edge_len :] * (1.0 - upper_weight) + upper_rim * upper_weight
    joined = jnp.concatenate(
        [low_part, centre[..., edge_len : keep_len - edge_len], high_part], axis=-1
    )
    return joined * live


def general_plan(voltages, section1_taps, section2_taps, band_starts, band_widths):
    signal = voltages[0]
    tap_count, chan_len = section1_taps.shape
    spectra = signal.shape[1] // HOP
    rim_len = tap_count * chan_len - HOP
    pieces = -(-chan_len // HOP)
    following = shifted(signal[:, :rim_len], ("tm", "zoom"), -1)
    padded = jnp.concatenate(
        [signal, following, jnp.zeros((2, pieces * HOP), jnp.bfloat16)], axis=1
    )
    weighted = weighted_frames(padded, section1_taps, spectra, HOP)
    coarse = jnp.einsum(
        "pqkn,qsn->pks", rotation_block(chan_len), weighted, preferred_element_type=jnp.float32
    ).astype(jnp.bfloat16)
    tm_count = lax.axis_size("tm")
    zoom_count = lax.axis_size("zoom")
    slot_local = jnp.arange(CH_DEV, dtype=jnp.int32)
    slot_ids = lax.axis_index("tm") * CH_DEV + slot_local
    band_count = band_widths.shape[0]
    band_ids = jnp.arange(band_count, dtype=jnp.int32)
    my_band = band_ids == lax.axis_index("zoom")
    band_width = jnp.sum(jnp.where(my_band, band_widths, 0))
    device_count = tm_count * zoom_count
    live_count = LIVE_DEV * device_count
    band_ends = jnp.cumsum(band_widths)
    band_firsts = band_ends - band_widths
    live_ids = jnp.arange(live_count, dtype=jnp.int32)
    band_of = jnp.sum((band_ends[None, :] <= live_ids[:, None]).astype(jnp.int32), axis=1)
    member = band_of[:, None] == band_ids[None, :]
    first_of = jnp.sum(jnp.where(member, band_firsts[None, :], 0), axis=1)
    start_of = jnp.sum(jnp.where(member, band_starts[None, :], 0), axis=1)
    live_channels = (start_of + live_ids - first_of) % chan_len
    packed_order = live_channels.reshape(device_count, LIVE_DEV).T.reshape(-1)
    packed = jnp.take(coarse, packed_order, axis=1).reshape(2, LIVE_DEV, device_count, spectra)
    received = lax.all_to_all(packed, ("tm", "zoom"), split_axis=2, concat_axis=2, tiled=True)
    series = received.reshape(2, received.shape[1], -1)
    computed = fine_spectra(series, section2_taps, FA, FB, KEEP, EDGE)
    wanted = jnp.sum(jnp.where(my_band, band_firsts, 0)) + slot_ids
    valid = slot_ids < band_width
    piece = lax.all_gather(computed, ("tm", "zoom"), axis=1, tiled=True)
    piece_ids = jnp.arange(piece.shape[1], dtype=jnp.int32)
    chosen = ((wanted[:, None] == piece_ids[None, :]) & valid[:, None]).astype(jnp.float32)
    extended = jnp.einsum("kn,pnfx->pkfx", chosen, piece, precision=lax.Precision.HIGHEST)
    seam_rows = jnp.concatenate([extended[..., :EDGE], extended[..., KEEP + EDGE :]], axis=-1)
    widened = with_halo(seam_rows, (("tm", 1),), 1)
    upper_rim = widened[:, 2:, :, :EDGE]
    lower_rim = widened[:, :CH_DEV, :, EDGE:]
    stitched = stitch_bands(extended, upper_rim, lower_rim, slot_ids, band_width, KEEP, EDGE)
    fine_count = stitched.shape[2]
    result = jnp.transpose(stitched, (0, 2, 1, 3)).reshape(2, fine_count, CH_DEV * KEEP)
    return result[None, None]


ROWS = 8
LANES = 128
SLOT_LANES = 2 * ROWS
PAD = 8
NT = (((1,), (1,)), ((), ()))


def sine_quarter(value):
    square = value * value
    total = -3.5988432e-06
    for factor in (1.604411848e-04, -4.6817541353e-03, 7.96926262462e-02, -6.459640975062e-01):
        total = total * square + factor
    return (total * square + 1.5707963267949) * value


def section_one_kernel(plan, starts_hbm, widths_hbm, taps_hbm, signal_ref, *rest):
    (outs, (width_ref, taps_rows, frames, total, *rest)) = (
        rest[: plan.devices],
        rest[plan.devices :],
    )
    (starts_ref, widths_ref, taps_ref, small_sems, sems) = rest
    small = [
        pltpu.make_async_copy(source, target, small_sems.at[index])
        for index, (source, target) in enumerate(
            [(starts_hbm, starts_ref), (widths_hbm, widths_ref), (taps_hbm, taps_ref)]
        )
    ]
    for copy in small:
        copy.start()
    blocks, chan_len, live = (plan.blocks, plan.chan_len, plan.live)
    half = ROWS * live
    columns = 2 * half
    lead = plan.lead
    copies = [
        pltpu.make_async_copy(
            signal_ref.at[:, block], frames.at[block, pl.ds(lead, plan.local_rows)], sems.at[block]
        )
        for block in range(blocks)
    ]
    for copy in copies:
        copy.start(priority=1)
    edge = jnp.zeros((blocks, lead, 2, LANES), jnp.bfloat16)
    frames[:, :lead] = edge
    frames[:, lead + plan.local_rows :] = edge

    for copy in small:
        copy.wait()
    row = lax.broadcasted_iota(jnp.int32, (columns, 1), 0)
    imag = (row >= half).astype(jnp.int32)
    shift = (row - imag * half) // live
    ident = row - imag * half - shift * live
    channel = jnp.zeros((columns, 1), jnp.int32)
    first = jnp.int32(0)
    firsts = []
    for band in range(plan.bands):
        inside = (ident >= first) & (ident < first + widths_ref[band])
        channel = jnp.where(inside, starts_ref[band] + ident - first, channel)
        firsts.append(first)
        first = first + widths_ref[band]
    phase = lax.broadcasted_iota(jnp.int32, (columns, LANES), 1) - HOP * shift
    quarter = chan_len // 4
    turn = (channel * phase + imag * quarter) & (chan_len - 1)
    folded = jnp.abs(turn - 2 * quarter)
    angle = (folded - quarter).astype(jnp.float32) * (1.0 / quarter)
    first_lanes = sine_quarter(angle)
    ahead = jnp.concatenate([first_lanes[half:], -first_lanes[:half]], axis=0)
    tiles = [first_lanes]
    for tile in range(1, 4):
        quarters = (channel * tile) & 3
        same = (quarters == 0).astype(jnp.float32) - (quarters == 2).astype(jnp.float32)
        next_one = (quarters == 1).astype(jnp.float32) - (quarters == 3).astype(jnp.float32)
        tiles.append(same * first_lanes + next_one * ahead)
    rotation = jnp.concatenate(tiles, axis=1).astype(jnp.bfloat16)

    filled = plan.taps * chan_len + LANES
    flat = jnp.concatenate(
        [jnp.broadcast_to(taps_ref[tap : tap + 1, :], (8, chan_len)) for tap in range(plan.taps)]
        + [jnp.zeros((8, LANES), jnp.float32)],
        axis=1,
    )
    for shift_index in range(ROWS):
        (skipped, offset) = divmod(HOP * shift_index, LANES)
        moved = pltpu.roll(flat, offset, axis=1) if offset else flat
        first = skipped * LANES
        end = min(first + filled, plan.depth)
        if first:
            taps_rows[shift_index, :, :first] = jnp.zeros((8, first), jnp.float32)
        taps_rows[shift_index, :, first:end] = moved[:, : end - first]
        if end < plan.depth:
            taps_rows[shift_index, :, end:] = jnp.zeros((8, plan.depth - end), jnp.float32)
    count = 2 * plan.out_rows
    pairs = frames.reshape(blocks, 2 * (plan.local_rows + 2 * lead), LANES)
    acc = jnp.zeros((count, columns), jnp.float32)
    order = sorted(range(plan.depth // LANES), key=lambda index: (index % blocks, index // blocks))
    turns = chan_len // LANES
    bounds = (5, 12, blocks)

    def column_tile(index):
        scale = jnp.concatenate(
            [
                jnp.broadcast_to(
                    taps_rows[shift_index, :, pl.ds(index * LANES, LANES)][None],
                    (live // 8, 8, LANES),
                ).reshape(live, LANES)
                for shift_index in range(ROWS)
            ],
            axis=0,
        ).astype(jnp.bfloat16)
        turned = rotation[:, index % turns * LANES : (index % turns + 1) * LANES]
        return jnp.concatenate([scale * turned[:half], scale * turned[half:]], axis=0)

    groups = [order[piece : piece + turns] for piece in range(0, len(order), turns)]
    (begin, seen) = (0, 0)
    for bound in bounds:
        end = begin
        while end < len(groups) and max(index % blocks for index in groups[end]) < bound:
            end += 1
        staged = groups[begin:end]
        rights = [
            jnp.concatenate([column_tile(index) for index in group], axis=1) for group in staged
        ]
        for copy in copies[seen:bound]:
            copy.wait()
        for group, right in zip(staged, rights):
            left = jnp.concatenate(
                [pairs[index % blocks, pl.ds(2 * (index // blocks), count), :] for index in group],
                axis=1,
            )
            acc = acc + lax.dot_general(left, right, NT, preferred_element_type=jnp.float32)
        (begin, seen) = (end, bound)
    for tile in range(columns // LANES):
        total[tile] = acc[:, tile * LANES : (tile + 1) * LANES]
    (real_rows, imag_rows) = (
        jnp.concatenate(
            [total[tile, pl.ds(part, plan.out_rows, 2), :] for tile in range(columns // LANES)],
            axis=1,
        )
        for part in range(2)
    )
    lane = lax.broadcasted_iota(jnp.int32, (1, columns), 1)
    sign = jnp.where(lane < half, -1.0, 1.0)
    coarse = (real_rows + sign * pltpu.roll(imag_rows, half, axis=1)).astype(jnp.bfloat16)

    (tm, zoom) = (lax.axis_index("tm"), lax.axis_index("zoom"))
    mine = jnp.int32(0)
    for band in range(plan.bands):
        mine = jnp.where(zoom == band, widths_ref[band], mine)
    width_ref[...] = jnp.broadcast_to(mine, width_ref.shape)
    code = ident * SLOT_LANES + imag * ROWS + shift
    out_lane = lax.broadcasted_iota(jnp.int32, (1, LANES), 1)
    slot = out_lane // SLOT_LANES
    picks = []
    for step in range(plan.devices):
        target = jnp.bitwise_xor(tm * plan.zooms + zoom, step)
        (target_tm, target_zoom) = (target // plan.zooms, target % plan.zooms)
        (band_first, width) = (jnp.int32(0), jnp.int32(0))
        for band in range(plan.bands):
            band_first = jnp.where(target_zoom == band, firsts[band], band_first)
            width = jnp.where(target_zoom == band, widths_ref[band], width)
        base = target_tm * CH_DEV - 1
        position = base + slot
        valid = (position >= 0) & (position < width) & (slot < CH_DEV + 2)
        wanted = jnp.where(valid, (band_first + base) * SLOT_LANES + out_lane, -1)
        pick = (code == wanted).astype(jnp.float32).astype(jnp.bfloat16)
        picks.append(pick)

    chosen = lax.dot_general(
        coarse,
        jnp.concatenate(picks, axis=1),
        (((1,), (0,)), ((), ())),
        preferred_element_type=jnp.float32,
    ).astype(jnp.bfloat16)
    for step in range(plan.devices):
        outs[step][...] = chosen[:, step * LANES : (step + 1) * LANES]


def fine_taps_kernel(plan, taps_ref, after_ref, out_ref):
    lane = lax.broadcasted_iota(jnp.int32, (SLOT_LANES, LANES), 1)
    row = lax.broadcasted_iota(jnp.int32, (SLOT_LANES, LANES), 0)
    keep = lane // ROWS == row
    source = lax.broadcasted_iota(jnp.int32, (2 * LANES, LANES), 0)
    target = lax.broadcasted_iota(jnp.int32, (2 * LANES, LANES), 1)
    spread = (source % ROWS == target % ROWS).astype(jnp.float32).astype(jnp.bfloat16)
    for tap in range(plan.fine_taps):
        (high, low) = ([], [])
        for tile in range(plan.fine_rows // SLOT_LANES):
            line = taps_ref[tap : tap + 1, tile * LANES : (tile + 1) * LANES]
            part = jnp.where(keep, jnp.broadcast_to(line, (SLOT_LANES, LANES)), 0.0)
            rounded = part.astype(jnp.bfloat16)
            high.append(rounded)
            low.append((part - rounded.astype(jnp.float32)).astype(jnp.bfloat16))
        both = jnp.concatenate([jnp.concatenate(high, axis=0), jnp.concatenate(low, axis=0)], axis=1)
        out_ref[pl.ds(PAD + tap * plan.fine_rows, plan.fine_rows), :] = lax.dot_general(
            both, spread, (((1,), (0,)), ((), ())), preferred_element_type=jnp.float32
        )
    out_ref[:PAD] = jnp.zeros((PAD, LANES), jnp.float32)


def add_blocks(plan, steps, taps_ref, blocks, sums):
    here = lax.axis_index("tm") * plan.zooms + lax.axis_index("zoom")
    (fine_rows, out_rows) = (plan.fine_rows, plan.out_rows)
    sums[...] = jnp.zeros_like(sums)
    for step, block in zip(steps, blocks):
        start = jnp.bitwise_xor(here, step) * plan.local_rows + (PAD - plan.lead)
        goal = pl.ds(lax.rem(start + (fine_rows - PAD), fine_rows), out_rows)
        scale = taps_ref[pl.ds(start, out_rows), :]
        sums[goal, :] += scale * block[...].astype(jnp.float32)
    return jnp.concatenate(
        [
            sums[:out_rows] + sums[fine_rows : fine_rows + out_rows],
            sums[out_rows:fine_rows],
        ],
        axis=0,
    )


def merge_kernel(plan, steps, taps_ref, *rest):
    (blocks, (kept_ref, sums)) = (rest[: len(steps)], rest[len(steps) :])
    kept_ref[...] = add_blocks(plan, steps, taps_ref, blocks, sums)


def section_two_kernel(
    plan, steps, width_ref, kept_ref, taps_ref, dft_ref, cos_ref, sin_ref, join_ref, *rest
):
    (blocks, (out_ref, sums)) = (rest[: len(steps)], rest[len(steps) :])
    tm = lax.axis_index("tm")
    (fine_rows, bins) = (plan.fine_rows, plan.bins)
    fine_in = kept_ref[...] + add_blocks(plan, steps, taps_ref, blocks, sums)
    spun = lax.dot_general(
        fine_in.T.astype(jnp.bfloat16),
        dft_ref[...],
        (((1,), (0,)), ((), ())),
        preferred_element_type=jnp.float32,
    )
    (cosine_tab, sine_tab) = (cos_ref[...], sin_ref[...])
    mixed = jnp.concatenate(
        [
            (part * factor).astype(jnp.bfloat16)
            for part in (spun[:, :bins], spun[:, bins:])
            for factor in (cosine_tab, sine_tab)
        ],
        axis=0,
    )
    joined = lax.dot_general(
        join_ref[...], mixed, (((1,), (0,)), ((), ())), preferred_element_type=jnp.float32
    )

    slots = LANES // SLOT_LANES
    high = 2 * slots
    flat = [jnp.zeros((high, LANES), jnp.float32)] * (-(-(ROWS * fine_rows) // LANES) + 2)
    for turn in range(ROWS):
        (first, offset) = divmod(turn * fine_rows, LANES)
        piece = jnp.concatenate(
            [joined[turn * high : (turn + 1) * high], jnp.zeros((high, LANES), jnp.float32)], axis=1
        )
        if offset:
            piece = pltpu.roll(piece, offset, axis=1)
        for tile in range(min(bins // LANES + 1, len(flat) - first)):
            flat[first + tile] = flat[first + tile] + piece[:, tile * LANES : (tile + 1) * LANES]

    row = lax.broadcasted_iota(jnp.int32, (high, LANES), 0)
    lane = lax.broadcasted_iota(jnp.int32, (high, LANES), 1)
    width = width_ref[0:1, :]
    slot = tm * CH_DEV + row % slots - 1
    live = (slot < width).astype(jnp.float32)
    upper_ok = (slot + 1 < width).astype(jnp.float32)
    lower_ok = ((slot >= 1) & (slot < width)).astype(jnp.float32)
    (lead, skew) = divmod(KEEP + EDGE, LANES)
    below = jnp.where(
        lane < LANES - skew,
        pltpu.roll(flat[lead], LANES - skew, axis=1),
        pltpu.roll(flat[lead + 1], LANES - skew, axis=1),
    )
    below = pltpu.roll(below, 1, axis=0)
    (lead, skew) = divmod(KEEP - EDGE, LANES)
    above = pltpu.roll(pltpu.roll(flat[0], skew, axis=1), high - 1, axis=0)
    position = lane.astype(jnp.float32)
    own = flat[1:]
    span = -(-KEEP // LANES)
    parts = []
    for tile in range(span):
        value = own[tile]
        if tile == 0:
            weight = (EDGE - 0.5 - position) * (0.5 / EDGE) * lower_ok
            value = value * (1.0 - weight) + below * weight
        if tile in (lead, lead + 1):
            ramp = (position + (tile * LANES - (KEEP - EDGE) + 0.5)) * (0.5 / EDGE)
            inside = lane >= skew if tile == lead else lane < skew
            weight = jnp.where(inside, ramp * upper_ok, 0.0)
            value = value * (1.0 - weight) + above * weight
        value = value * live
        if tile == span - 1:
            value = jnp.where(lane < KEEP - tile * LANES, value, 0.0)
        parts.append(value)
    parts = [jnp.zeros_like(parts[0])] + parts + [jnp.zeros_like(parts[0])]

    carry = [None, None]
    for place in range(CH_DEV):
        (first, offset) = divmod(place * KEEP, LANES)
        (after, _) = divmod((place + 1) * KEEP, LANES)
        last = place == CH_DEV - 1
        count = after - first + 1
        for part in range(2):
            picked = part * slots + place + 1
            pieces = [value[part * slots : (part + 1) * slots] for value in parts[: count + 1]]
            if offset:
                turned = [pltpu.roll(value, offset, axis=1) for value in pieces]
                pieces = [None] + [
                    jnp.where(lane[:slots] < offset, before, value)
                    for before, value in zip(turned, turned[1:])
                ]
            row_of = picked % slots
            tiles = [value[row_of : row_of + 1] for value in pieces[1:]]
            if place:
                tiles[0] = tiles[0] + carry[part]
            carry[part] = tiles[-1]
            if not last:
                tiles = tiles[:-1]
            line = jnp.concatenate(tiles, axis=1)
            end = min(first * LANES + len(tiles) * LANES, CH_DEV * KEEP)
            out_ref[part, :, first * LANES : end] = line[:, : end - first * LANES]


def fine_tables(fine_rows):
    fine_len = fine_rows * ROWS
    offset = KEEP // 2 + EDGE
    bins = np.arange(fine_rows) - offset
    spin = 2.0 * np.pi * (np.outer(bins, np.arange(fine_rows)) % fine_rows) / fine_rows
    margin = ((0, -fine_rows % LANES), (0, 0))
    dft = np.concatenate([np.pad(np.cos(spin), margin), np.pad(np.sin(spin), margin)], axis=0)
    twist = 2.0 * np.pi * (np.outer(bins, np.arange(LANES) % ROWS) % fine_len) / fine_len
    join = np.zeros((ROWS, 2, LANES // SLOT_LANES, 4, LANES // SLOT_LANES, 2, ROWS))
    turn = 2.0 * np.pi * (np.outer(np.arange(ROWS), np.arange(ROWS)) % ROWS) / ROWS
    (cosine, sine) = (np.cos(turn), np.sin(turn))
    for slot in range(LANES // SLOT_LANES):
        real, imag = (join[:, 0, slot, :, slot], join[:, 1, slot, :, slot])
        real[:, 0, 0], real[:, 0, 1] = (cosine, sine)
        real[:, 1, 0], real[:, 1, 1] = (-sine, cosine)
        real[:, 2, 0], real[:, 2, 1] = (-sine, cosine)
        real[:, 3, 0], real[:, 3, 1] = (-cosine, -sine)
        imag[:, 0, 0], imag[:, 0, 1] = (-sine, cosine)
        imag[:, 1, 0], imag[:, 1, 1] = (-cosine, -sine)
        imag[:, 2, 0], imag[:, 2, 1] = (-cosine, -sine)
        imag[:, 3, 0], imag[:, 3, 1] = (sine, -cosine)
    return (
        jnp.asarray(dft.T, jnp.bfloat16),
        jnp.asarray(np.pad(np.cos(twist), margin).T, jnp.float32),
        jnp.asarray(np.pad(np.sin(twist), margin).T, jnp.float32),
        jnp.asarray(join.reshape(LANES, 4 * LANES), jnp.bfloat16),
    )


class Plan:
    def __init__(self, mesh, samples, bands, section1_shape, section2_shape):
        (self.tms, self.zooms) = (mesh.shape["tm"], mesh.shape["zoom"])
        self.devices = self.tms * self.zooms
        self.bands = bands
        (self.taps, self.chan_len) = section1_shape
        self.fine_taps = section2_shape[0]
        self.live = LIVE_DEV * self.devices
        self.samples = samples
        self.row_len = ROWS * HOP
        self.blocks = self.row_len // LANES
        self.local_rows = samples // self.row_len
        reach = (ROWS - 1) * HOP + self.taps * self.chan_len
        unit = max(self.chan_len, 2 * LANES)
        self.depth = -(-reach // unit) * unit
        self.lead = -(-self.depth // self.row_len) - 1
        self.out_rows = self.local_rows + self.lead
        self.fine_rows = section2_shape[1] // ROWS
        self.bins = -(-self.fine_rows // LANES) * LANES

    def fits(self, section2_shape):
        return (
            self.row_len % LANES == 0
            and self.samples % self.row_len == 0
            and self.chan_len & (self.chan_len - 1) == 0
            and self.chan_len == 4 * LANES
            and self.devices & (self.devices - 1) == 0
            and self.live % 8 == 0
            and (2 * ROWS * self.live) % LANES == 0
            and 2 * ROWS * self.live <= 4 * LANES
            and (CH_DEV + 2) * SLOT_LANES <= LANES
            and self.devices >= 4
            and self.lead <= PAD
            and self.out_rows <= self.fine_rows
            and self.out_rows % 16 == 0
            and self.fine_rows % 16 == 0
            and EDGE == LANES
            and KEEP + 2 * EDGE <= section2_shape[1]
            and section2_shape[1] % ROWS == 0
            and self.devices * self.samples == HOP * self.fine_taps * section2_shape[1]
        )


def direct_plan(plan, voltages, section1_taps, section2_taps, band_starts, band_widths):
    signal = voltages[0].reshape(2, plan.local_rows, plan.blocks, LANES).transpose(1, 2, 0, 3)
    far = [
        pltpu.with_memory_space_constraint(array, pltpu.HBM)
        for array in (band_starts, band_widths, section1_taps, signal)
    ]
    vmem = pl.BlockSpec(memory_space=pltpu.VMEM)
    columns = 2 * ROWS * plan.live
    block = jax.ShapeDtypeStruct((plan.out_rows, LANES), jnp.bfloat16)
    (*sent, width) = pl.pallas_call(
        functools.partial(section_one_kernel, plan),
        out_shape=[block] * plan.devices + [jax.ShapeDtypeStruct((8, LANES), jnp.int32)],
        in_specs=[pl.BlockSpec(memory_space=pltpu.HBM)] * 4,
        out_specs=[vmem] * (plan.devices + 1),
        scratch_shapes=[
            pltpu.VMEM((ROWS, 8, plan.depth), jnp.float32),
            pltpu.VMEM((plan.blocks, plan.local_rows + 2 * plan.lead, 2, LANES), jnp.bfloat16),
            pltpu.VMEM((columns // LANES, 2 * plan.out_rows, LANES), jnp.float32),
            pltpu.SMEM((plan.bands,), jnp.int32),
            pltpu.SMEM((plan.bands,), jnp.int32),
            pltpu.VMEM((plan.taps, plan.chan_len), jnp.float32),
            pltpu.SemaphoreType.DMA((3,)),
            pltpu.SemaphoreType.DMA((plan.blocks,)),
        ],
        compiler_params=pltpu.CompilerParams(vmem_limit_bytes=40 * 2**20),
        name="section_one",
    )(*far)
    order = list(range(plan.devices - 1, 0, -1))
    received = {0: sent[0]}
    for step in order:
        pairs = [(index, index ^ step) for index in range(plan.devices)]
        received[step] = lax.ppermute(sent[step], ("tm", "zoom"), pairs)
    split = len(order) // 2 + 1
    (early, late) = ([0] + order[:split], order[split:])
    fine_rows = plan.fine_rows
    spread = pl.pallas_call(
        functools.partial(fine_taps_kernel, plan),
        out_shape=jax.ShapeDtypeStruct((PAD + plan.fine_taps * fine_rows, LANES), jnp.float32),
        in_specs=[vmem, pl.BlockSpec(memory_space=pl.ANY)],
        out_specs=vmem,
        compiler_params=pltpu.CompilerParams(vmem_limit_bytes=16 * 2**20),
        name="fine_taps",
    )(section2_taps, received[order[1]])
    sums = pltpu.VMEM((fine_rows + plan.out_rows, LANES), jnp.float32)
    kept = pl.pallas_call(
        functools.partial(merge_kernel, plan, early),
        out_shape=jax.ShapeDtypeStruct((fine_rows, LANES), jnp.float32),
        in_specs=[vmem] * (1 + len(early)),
        out_specs=vmem,
        scratch_shapes=[sums],
        compiler_params=pltpu.CompilerParams(vmem_limit_bytes=16 * 2**20),
        name="merge",
    )(spread, *[received[step] for step in early])
    (dft, cosine_tab, sine_tab, join) = fine_tables(fine_rows)
    lines = pl.pallas_call(
        functools.partial(section_two_kernel, plan, late),
        out_shape=jax.ShapeDtypeStruct((2, 1, CH_DEV * KEEP), jnp.float32),
        in_specs=[vmem] * (7 + len(late)),
        out_specs=vmem,
        scratch_shapes=[sums],
        compiler_params=pltpu.CompilerParams(vmem_limit_bytes=24 * 2**20),
        name="section_two",
    )(
        width,
        kept,
        spread,
        dft,
        cosine_tab,
        sine_tab,
        join,
        *[received[step] for step in late],
    )
    return lines.reshape(1, 1, 2, 1, CH_DEV * KEEP)


def solution(mesh):
    placed = (P("pol", "groups", ("tm", "zoom")), P(), P(), P("groups"), P("groups"))

    def on_device(voltages, section1_taps, section2_taps, band_starts, band_widths):
        plan = Plan(
            mesh,
            voltages.shape[2],
            band_widths.shape[0],
            section1_taps.shape,
            section2_taps.shape,
        )
        arrays = (voltages, section1_taps, section2_taps, band_starts, band_widths)
        if plan.fits(section2_taps.shape):
            return direct_plan(plan, *arrays)
        return general_plan(*arrays)

    return jax.shard_map(
        on_device,
        mesh=mesh,
        in_specs=placed,
        out_specs=P("pol", "zoom", "groups", None, "tm"),
        check_vma=False,
    )
```
